32 devices in a mesh: seq: 8 (over z, x), kvh: 4 (over y, core).
Axes of the slice: x: 2, y: 2, z: 4, core: 2. Of those that a mesh axis runs over, the one named last changes fastest.
Arguments:
- queries: bfloat16 [1024, 64, 128], P('seq', 'kvh'), may hold values from -160 to 160
- keys: bfloat16 [1024, 8, 128], P('seq', 'kvh'), may hold values from -4 to 4
- values: bfloat16 [1024, 8, 128], P('seq', 'kvh'), may hold values from -6 to 6
- output_gradient: bfloat16 [1024, 64, 128], P(('seq', 'kvh')), may hold values from -6 to 6
- doc_lengths: int32 [8], replicated, may hold values from 1 to 256, 1024 in all
- prefix_lengths: int32 [8], replicated, may hold values from 0 to 127
Outputs:
- grad_queries: bfloat16 [1024, 64, 128], P(('seq', 'kvh'))
- grad_keys: bfloat16 [1024, 8, 128], P('seq', 'kvh')
- grad_values: bfloat16 [1024, 8, 128], P('seq', 'kvh')
The draws below stay inside these ranges and needn't reach their ends.
Inputs may be any that keep to these rules, and one draw needn't show every extreme that they name: `doc_lengths`: lengths sum to 1024; the longest document has exactly 256 tokens.
All inputs are finite; a program needn't handle non-finite values.
Results may differ from the reference program's by a relative error of at most 0.015.
Values may be sent and summed in bfloat16 or wider, within the bound.
No kernel may reach another device: no remote copies, remote signals or barrier semaphores. Data moves between devices by JAX's collectives and lax.ppermute only.
A program may use at most 64 MiB of HBM per device.

```python
import math
import jax
import jax.numpy as jnp
import numpy as np
from jax import lax

QUERY_HEADS = 64
KEY_VALUE_HEADS = 8
HEAD_DIM = 128
QUERY_PER_KV = 8
SHARD_TOKENS = 128
BACK = 2
AHEAD = 1
STREAM_TOKENS = 1024
DOCS = 8
MOST = 256
N_SEQ = 8


def paired_draw(key):
    key_sample = jnp.clip(jax.random.normal(jax.random.fold_in(key, 31), (STREAM_TOKENS, KEY_VALUE_HEADS, HEAD_DIM), jnp.float32), -4.0, 4.0)
    query_draw = jnp.clip(jax.random.normal(jax.random.fold_in(key, 32), (STREAM_TOKENS, QUERY_HEADS, HEAD_DIM), jnp.float32), -4.0, 4.0)
    return (query_draw, key_sample)


def draw_queries(key, part):
    return paired_draw(key)[0].astype(jnp.bfloat16)


def draw_keys(key, part):
    return paired_draw(key)[1].astype(jnp.bfloat16)


def draw_prefix_lengths(key, part):
    highest = AHEAD * SHARD_TOKENS
    drawn = jax.random.randint(jax.random.fold_in(key, 21), (DOCS,), 0, highest, dtype=jnp.int32)
    chosen_doc = jax.random.randint(jax.random.fold_in(key, 22), (), 0, DOCS, dtype=jnp.int32)
    doc_slots = jnp.arange(DOCS, dtype=jnp.int32)
    drawn = jnp.where(doc_slots == chosen_doc, highest - 1, drawn)
    drawn = jnp.where(doc_slots == (chosen_doc + 1) % DOCS, 0, drawn)
    return drawn.astype(jnp.int32)


def steps_of(own_key, dims, shards, low, largest):
    gain, own = 1.0, jax.random.fold_in(own_key, 6)
    for dim, parts in shards:
        heights = jnp.exp(jax.random.uniform(jax.random.fold_in(own, dim), (parts,), jnp.float32, low / len(shards), largest / len(shards)))
        gain = gain * jnp.repeat(heights, dims[dim] // parts).reshape([-1 if axis == dim else 1 for axis in range(len(dims))])
    return gain


def split_up(number_of, total, reach, slope):
    loads = [(1 << 20) // math.isqrt(rank ** slope) + 1 for rank in range(2, number_of + 1)]
    rest, holding = total - reach - (number_of - 1), [1] * (number_of - 1)
    while rest > 0:
        candidates = [i for i in range(number_of - 1) if holding[i] < reach]
        mass, budget = sum([loads[i] for i in candidates]), rest
        for i in candidates:
            addition = min(reach - holding[i], max(1, budget * loads[i] // mass), rest)
            holding[i] = holding[i] + addition
            rest = rest - addition
    return np.array([reach] + holding)


def uneven(rng, amount, total, limit, skew):
    if amount == 2:
        one = jax.random.randint(rng, (), max(1, total - limit), min(limit, total - 1) + 1)
        return jnp.stack([one, total - one])
    lengths = jnp.asarray(split_up(amount, total, limit, skew), jnp.int32)
    couples = (amount - 1) // 2
    donor, taker = lengths[1:1 + 2 * couples:2], lengths[2:2 + 2 * couples:2]
    room = jnp.minimum(donor - 1, limit - taker)
    passed = jax.random.randint(jax.random.fold_in(rng, 1), (couples,), 0, 1 << 20) % (room + 1)
    lengths = lengths.at[1:1 + 2 * couples:2].set(donor - passed).at[2:2 + 2 * couples:2].set(taker + passed)
    return lengths[jax.random.permutation(jax.random.fold_in(rng, 2), amount)]


def scatter_about(stream_key, shape, width, bound, pieces=(), kind=jnp.bfloat16):
    entries = jax.random.normal(stream_key, shape, jnp.float32) * width
    if len(pieces) > 0:
        entries = steps_of(stream_key, shape, pieces, -0.22, 0.18) * entries
    return jnp.clip(entries, min=-bound, max=bound).astype(kind)


def setup_inputs(seed: int = 0) -> dict:
    key_of = jax.random.split(jax.random.key(seed), 7)
    return {
        "queries": draw_queries(jax.random.fold_in(key_of[6], 71), 0),
        "keys": draw_keys(jax.random.fold_in(key_of[6], 71), 0),
        "values": scatter_about(key_of[2], (STREAM_TOKENS, KEY_VALUE_HEADS, HEAD_DIM), 1.0, 6.0, ((0, 8), (1, 4))),
        "output_gradient": scatter_about(key_of[3], (STREAM_TOKENS, QUERY_HEADS, HEAD_DIM), 1.0, 6.0, ((0, 32),)),
        "doc_lengths": uneven(key_of[4], DOCS, STREAM_TOKENS, MOST, 2).astype(jnp.int32),
        "prefix_lengths": draw_prefix_lengths(jax.random.fold_in(key_of[6], 71), 0),
    }


def locate(positions, doc_end):
    return jnp.sum((positions[:, None] >= doc_end[None, :]).astype(jnp.int32), axis=1)


def reference(queries, keys, values, output_gradient, doc_lengths, prefix_lengths):
    score_scale = HEAD_DIM ** -0.5
    doc_end = jnp.cumsum(doc_lengths).astype(jnp.int32)
    prefix_end = (doc_end - doc_lengths + prefix_lengths).astype(jnp.int32)
    positions = jnp.arange(STREAM_TOKENS, dtype=jnp.int32)
    doc_index = locate(positions, doc_end)
    leading_part = BACK * SHARD_TOKENS
    trailing_part = AHEAD * SHARD_TOKENS
    window = leading_part + SHARD_TOKENS + trailing_part
    keys_padded = jnp.pad(keys, ((leading_part, trailing_part), (0, 0), (0, 0)))
    values_padded = jnp.pad(values, ((leading_part, trailing_part), (0, 0), (0, 0)))
    key_pos_all = jnp.arange(-leading_part, STREAM_TOKENS + trailing_part, dtype=jnp.int32)
    key_doc_all = jnp.pad(doc_index, (leading_part, trailing_part), constant_values=-1).astype(jnp.int32)
    key_prefix_all = jnp.where(key_doc_all >= 0, prefix_end[jnp.clip(key_doc_all, 0, DOCS - 1)], 0).astype(jnp.int32)

    def advance(accums, shard):
        keys_acc, values_acc = accums
        first_row = (shard * SHARD_TOKENS).astype(jnp.int32)
        query_tile_rows = lax.dynamic_slice_in_dim(queries, first_row, SHARD_TOKENS, 0).astype(jnp.float32).reshape(SHARD_TOKENS, KEY_VALUE_HEADS, QUERY_PER_KV, HEAD_DIM)
        cotangent_block = lax.dynamic_slice_in_dim(output_gradient, first_row, SHARD_TOKENS, 0).astype(jnp.float32).reshape(SHARD_TOKENS, KEY_VALUE_HEADS, QUERY_PER_KV, HEAD_DIM)
        key_window = lax.dynamic_slice_in_dim(keys_padded, first_row, window, 0).astype(jnp.float32)
        value_window = lax.dynamic_slice_in_dim(values_padded, first_row, window, 0).astype(jnp.float32)
        key_pos = lax.dynamic_slice_in_dim(key_pos_all, first_row, window, 0)
        key_doc = lax.dynamic_slice_in_dim(key_doc_all, first_row, window, 0)
        key_prefix = lax.dynamic_slice_in_dim(key_prefix_all, first_row, window, 0)
        query_pos = first_row + jnp.arange(SHARD_TOKENS, dtype=jnp.int32)
        query_doc = lax.dynamic_slice_in_dim(doc_index, first_row, SHARD_TOKENS, 0)
        visible = (query_doc[:, None] == key_doc[None, :]) & ((key_pos[None, :] <= query_pos[:, None]) | (key_pos[None, :] < key_prefix[None, :]))
        scores = jnp.einsum("tgqd,sgd->gqts", query_tile_rows, key_window) * score_scale
        scores = jnp.where(visible[None, None], scores, -1e30)
        row_max = jnp.max(scores, axis=-1)
        expo = jnp.where(visible[None, None], jnp.exp(scores - row_max[..., None]), 0.0)
        row_sum = jnp.sum(expo, axis=-1)
        probs = expo / row_sum[..., None]
        probs_half = probs.astype(jnp.bfloat16)
        dprobs = jnp.einsum("tgqd,sgd->gqts", cotangent_block, value_window)
        row_delta = jnp.sum(probs * dprobs, axis=-1)
        dscores = (probs * (dprobs - row_delta[..., None])).astype(jnp.bfloat16)
        dscores_wide = dscores.astype(jnp.float32)
        grad_q = (score_scale * jnp.einsum("gqts,sgd->tgqd", dscores_wide, key_window)).astype(jnp.bfloat16)
        grad_k = score_scale * jnp.einsum("gqts,tgqd->sgd", dscores_wide, query_tile_rows)
        grad_v = jnp.einsum("gqts,tgqd->sgd", probs_half.astype(jnp.float32), cotangent_block)
        keys_acc = lax.dynamic_update_slice_in_dim(keys_acc, lax.dynamic_slice_in_dim(keys_acc, first_row, window, 0) + grad_k, first_row, 0)
        values_acc = lax.dynamic_update_slice_in_dim(values_acc, lax.dynamic_slice_in_dim(values_acc, first_row, window, 0) + grad_v, first_row, 0)
        return (keys_acc, values_acc), grad_q.reshape(SHARD_TOKENS, QUERY_HEADS, HEAD_DIM)

    zero_accumulator = jnp.zeros((STREAM_TOKENS + leading_part + trailing_part, KEY_VALUE_HEADS, HEAD_DIM), jnp.float32)
    (keys_acc, values_acc), query_blocks = lax.scan(advance, (zero_accumulator, zero_accumulator), jnp.arange(N_SEQ, dtype=jnp.int32))
    grad_queries = query_blocks.reshape(STREAM_TOKENS, QUERY_HEADS, HEAD_DIM)
    grad_keys = keys_acc[leading_part:leading_part + STREAM_TOKENS].astype(jnp.bfloat16)
    grad_values = values_acc[leading_part:leading_part + STREAM_TOKENS].astype(jnp.bfloat16)
    return (grad_queries, grad_keys, grad_values)
```

```python
import functools

import jax
import jax.numpy as jnp
from jax import lax
from jax.experimental import pallas as pl
from jax.experimental.pallas import tpu as pltpu
from jax.sharding import PartitionSpec as P

BACK = 2
AHEAD = 1
LOG2E = 1.4426950408889634
VMEM_BYTES = 40 * 1024 * 1024
NEG = -1e30

_VMEM = pl.BlockSpec(memory_space=pltpu.VMEM)
_SMEM = pl.BlockSpec(memory_space=pltpu.SMEM)
_ANY = pl.BlockSpec(memory_space=pl.ANY)


def prep_kernel(parts, cot_ref, key_ref, value_ref, cot_out, kv_out, sems):
    rows = cot_ref.shape[0]
    heads = cot_ref.shape[1] // parts
    copies = []
    for part in range(parts):
        copy = pltpu.make_async_copy(
            cot_ref.at[:, pl.ds(part * heads, heads), :],
            cot_out.at[pl.ds(part * rows, rows)],
            sems.at[part],
        )
        copy.start()
        copies.append(copy)
    for number, ref in enumerate((key_ref, value_ref)):
        wide = ref[...].astype(jnp.float32)
        for group in range(ref.shape[1]):
            kv_out[number, group] = wide[:, group, :].astype(jnp.bfloat16)
    for copy in copies:
        copy.wait()


def prepare(cotangent, keys, values, parts):
    rows, heads, size = cotangent.shape
    kv_rows, kv_heads, _ = keys.shape
    return pl.pallas_call(
        functools.partial(prep_kernel, parts),
        out_shape=(
            jax.ShapeDtypeStruct((parts * rows, heads // parts, size), jnp.bfloat16),
            jax.ShapeDtypeStruct((2, kv_heads, kv_rows, size), jnp.bfloat16),
        ),
        in_specs=[_ANY, _VMEM, _VMEM],
        out_specs=(_ANY, _VMEM),
        scratch_shapes=[pltpu.SemaphoreType.DMA((parts,))],
        compiler_params=pltpu.CompilerParams(vmem_limit_bytes=VMEM_BYTES),
        name="prepare",
    )(cotangent, keys, values)


def bounds(position, lengths, prefixes):
    docs = lengths.shape[0]

    def step(doc, carry):
        start, low, high = carry
        end = start + lengths[doc]
        inside = (position >= start) & (position < end)
        reach = jnp.minimum(end, jnp.maximum(position + 1, start + prefixes[doc]))
        return end, jnp.where(inside, start, low), jnp.where(inside, reach, high)

    zero = jnp.zeros_like(position)
    carry = (jnp.int32(0), zero, zero)
    if docs <= 16:
        for doc in range(docs):
            carry = step(doc, carry)
    else:
        carry = lax.fori_loop(0, docs, step, carry)
    return carry[1], carry[2]


def grad_kernel(
    tokens, lengths, prefixes, q_ref, cot_ref, kv_own, kv_back1, kv_back2, kv_ahead,
    dq_ref, own_out, back1_out, back2_out, ahead_out, window, acc,
):
    rows, heads, size = q_ref.shape
    kv_heads = kv_own.shape[1]
    group_size = heads // kv_heads
    span = (BACK + 1 + AHEAD) * rows
    reach = span - rows + tokens
    lanes = tokens * group_size
    scale = size ** (-0.5)
    shard = lax.axis_index("seq")

    for slot, ref in enumerate((kv_back2, kv_back1, kv_own, kv_ahead)):
        for number in range(2):
            for group in range(kv_heads):
                window[number, group, pl.ds(slot * rows, rows)] = ref[number, group]
    acc[...] = jnp.zeros_like(acc)

    contract_last = (((1,), (1,)), ((), ()))
    contract_first = (((0,), (0,)), ((), ()))
    lane_token = lax.broadcasted_iota(jnp.int32, (1, lanes), 1) // group_size
    key_iota = lax.broadcasted_iota(jnp.int32, (reach, lanes), 0)
    for chunk in range(rows // tokens):
        first = chunk * tokens
        low, high = bounds(shard * rows + first + lane_token, lengths, prefixes)
        origin = (shard - BACK) * rows + first
        low = low - origin
        high = high - origin
        visible = (key_iota >= low) & (key_iota < high)
        for group in range(kv_heads):
            pick = (pl.ds(first, tokens), pl.ds(group * group_size, group_size))
            q = q_ref[pick].astype(jnp.float32).reshape(lanes, size).astype(jnp.bfloat16)
            cot = cot_ref[pick].astype(jnp.float32).reshape(lanes, size).astype(jnp.bfloat16)
            here = pl.ds(first, reach)
            k = window[0, group, here]
            v = window[1, group, here]
            scores = lax.dot_general(k, q, contract_last, preferred_element_type=jnp.float32)
            scores = jnp.where(visible, scores * (scale * LOG2E), NEG)
            top = jnp.max(scores, axis=0, keepdims=True)
            expo = jnp.exp2(scores - top)
            total = jnp.sum(expo, axis=0, keepdims=True)
            probs = expo * (1.0 / total)
            dprobs = lax.dot_general(v, cot, contract_last, preferred_element_type=jnp.float32)
            delta = jnp.sum(probs * dprobs, axis=0, keepdims=True)
            dscores = (probs * (dprobs - delta)).astype(jnp.bfloat16)
            acc[1, group, here] += jnp.dot(
                probs.astype(jnp.bfloat16), cot, preferred_element_type=jnp.float32
            )
            acc[0, group, here] += jnp.dot(dscores, q, preferred_element_type=jnp.float32)
            dq = lax.dot_general(k, dscores, contract_first, preferred_element_type=jnp.float32)
            dq = jnp.transpose(dq * scale)
            dq_ref[pick] = dq.reshape(tokens, group_size, size).astype(jnp.bfloat16)
    for slot, ref in enumerate((back2_out, back1_out, own_out, ahead_out)):
        for group in range(kv_heads):
            part = pl.ds(slot * rows, rows)
            ref[0, group] = (acc[0, group, part] * scale).astype(ref.dtype)
            ref[1, group] = acc[1, group, part].astype(ref.dtype)


def gradients(lengths, prefixes, queries, cotangent, blocks):
    rows, heads, size = queries.shape
    kv_shape = blocks[0].shape
    kv_heads = kv_shape[1]
    span = (BACK + 1 + AHEAD) * rows
    half = jax.ShapeDtypeStruct(kv_shape, jnp.bfloat16)
    work = heads * rows * span
    return pl.pallas_call(
        functools.partial(grad_kernel, 32),
        out_shape=(
            jax.ShapeDtypeStruct(queries.shape, jnp.bfloat16),
            jax.ShapeDtypeStruct(kv_shape, jnp.float32),
            half,
            half,
            half,
        ),
        in_specs=[_SMEM, _SMEM] + [_VMEM] * 6,
        out_specs=(_VMEM,) * 5,
        scratch_shapes=[
            pltpu.VMEM((2, kv_heads, span, size), jnp.bfloat16),
            pltpu.VMEM((2, kv_heads, span, size), jnp.float32),
        ],
        compiler_params=pltpu.CompilerParams(vmem_limit_bytes=VMEM_BYTES),
        cost_estimate=pl.CostEstimate(
            flops=10 * work * size, bytes_accessed=4 * queries.size * 2, transcendentals=work
        ),
        name="gradients",
    )(lengths, prefixes, queries, cotangent, *blocks)


def finish_kernel(dq_ref, own, from_ahead1, from_ahead2, from_back, dq_out, dk_out, dv_out):
    parts, rows, heads, _ = dq_ref.shape
    for part in range(parts):
        dq_out[:, pl.ds(part * heads, heads), :] = dq_ref[part]
    for number, ref in enumerate((dk_out, dv_out)):
        sums = []
        for group in range(ref.shape[1]):
            total = own[number, group]
            for other in (from_ahead1, from_ahead2, from_back):
                total = total + other[number, group].astype(jnp.float32)
            sums.append(total)
        ref[...] = jnp.stack(sums, axis=1).astype(jnp.bfloat16)


def finish(dq, own, received, parts):
    total_rows, heads, size = dq.shape
    rows = total_rows // parts
    _, kv_heads, kv_rows, _ = own.shape
    kv_out = jax.ShapeDtypeStruct((kv_rows, kv_heads, size), jnp.bfloat16)
    return pl.pallas_call(
        finish_kernel,
        out_shape=(
            jax.ShapeDtypeStruct((rows, heads * parts, size), jnp.bfloat16),
            kv_out,
            kv_out,
        ),
        in_specs=[_VMEM] * 5,
        out_specs=(_VMEM,) * 3,
        compiler_params=pltpu.CompilerParams(vmem_limit_bytes=VMEM_BYTES),
        name="finish",
    )(dq.reshape(parts, rows, heads, size), own, *received)


def shifted(block, distance):
    devices = range(lax.axis_size("seq"))
    route = [(i - distance, i) for i in devices if i - distance in devices]
    return lax.ppermute(block, "seq", route)


def local(queries, keys, values, output_gradient, doc_lengths, prefix_lengths):
    parts = lax.axis_size("kvh")
    cot, kv = prepare(output_gradient, keys, values, parts)
    cot = lax.all_to_all(cot, "kvh", split_axis=0, concat_axis=0, tiled=True)
    blocks = (kv, shifted(kv, 1), shifted(kv, 2), shifted(kv, -1))
    dq, own, back1, back2, ahead = gradients(
        doc_lengths, prefix_lengths, queries, cot, blocks
    )
    received = (shifted(back1, -1), shifted(back2, -2), shifted(ahead, 1))
    dq = lax.all_to_all(dq, "kvh", split_axis=0, concat_axis=0, tiled=True)
    return finish(dq, own, received, parts)


def solution(mesh):
    in_specs = (
        P("seq", "kvh", None),
        P("seq", "kvh", None),
        P("seq", "kvh", None),
        P(("seq", "kvh"), None, None),
        P(),
        P(),
    )
    out_specs = (P(("seq", "kvh"), None, None), P("seq", "kvh", None), P("seq", "kvh", None))
    return jax.shard_map(local, mesh=mesh, in_specs=in_specs, out_specs=out_specs, check_vma=False)
```

```python
import functools

import jax
import jax.numpy as jnp
from jax import lax
from jax.experimental import pallas as pl
from jax.experimental.pallas import tpu as pltpu
from jax.sharding import PartitionSpec as P

BACK = 2
AHEAD = 1
LOG2E = 1.4426950408889634
VMEM_BYTES = 40 * 1024 * 1024
PREPARE_VMEM_BYTES = 60 * 1024 * 1024
NEG = -1e30

_VMEM = pl.BlockSpec(memory_space=pltpu.VMEM)
_SMEM = pl.BlockSpec(memory_space=pltpu.SMEM)
_HBM = pl.BlockSpec(memory_space=pltpu.HBM)


def sequence(parts, shifts):
    masks, shifts = list(range(parts - 1, 0, -1)), list(shifts)
    order = [("mask", 0)]
    while masks or shifts:
        if shifts:
            order.append(("shift", shifts.pop(0)))
        if masks:
            order.append(("mask", masks.pop(0)))
    return order


def arrange(pieces, blocks, shifts):
    return [
        pieces[which] if kind == "mask" else blocks[which]
        for kind, which in sequence(len(pieces), shifts)
    ]


def arranged(parts, shifts, refs):
    order = sequence(parts, shifts)
    found = dict(zip(order, refs))
    return (
        [found["mask", mask] for mask in range(parts)],
        {shift: found["shift", shift] for shift in shifts},
        refs[len(order):],
    )


def prep_kernel(parts, cot_ref, key_ref, value_ref, *rest):
    kv_outs, cot_outs, (key_buf, value_buf, sems) = rest[:3], rest[3 : parts + 3], rest[parts + 3 :]
    heads = cot_ref.shape[1] // parts
    me = lax.axis_index("kvh")
    loads = []
    for number, (ref, buf) in enumerate(((key_ref, key_buf), (value_ref, value_buf))):
        loads.append(pltpu.make_async_copy(ref, buf, sems.at[parts + number]))
        loads[-1].start()
    copies = []
    for mask in range(parts):
        first = pl.multiple_of((me ^ mask) * heads, heads)
        copies.append(
            pltpu.make_async_copy(
                cot_ref.at[:, pl.ds(first, heads), :], cot_outs[mask], sems.at[mask]
            )
        )
        copies[-1].start()
    for number, buf in enumerate((key_buf, value_buf)):
        loads[number].wait()
        wide = buf[...].astype(jnp.float32)
        for group in range(buf.shape[1]):
            packed = wide[:, group, :].astype(jnp.bfloat16)
            for kv_out in kv_outs:
                kv_out[number, group] = packed
    for copy in copies:
        copy.wait()


def prepare(cotangent, keys, values, parts):
    rows, heads, size = cotangent.shape
    kv_rows, kv_heads, _ = keys.shape
    piece = jax.ShapeDtypeStruct((rows, heads // parts, size), jnp.bfloat16)
    outs = pl.pallas_call(
        functools.partial(prep_kernel, parts),
        out_shape=(jax.ShapeDtypeStruct((2, kv_heads, kv_rows, size), jnp.bfloat16),) * 3
        + (piece,) * parts,
        in_specs=[_HBM] * 3,
        out_specs=(_VMEM,) * (parts + 3),
        scratch_shapes=[
            pltpu.VMEM(keys.shape, jnp.bfloat16),
            pltpu.VMEM(values.shape, jnp.bfloat16),
            pltpu.SemaphoreType.DMA((parts + 2,)),
        ],
        compiler_params=pltpu.CompilerParams(vmem_limit_bytes=PREPARE_VMEM_BYTES),
        name="prepare",
    )(cotangent, keys, values)
    return outs[:3], outs[3:]


def bounds(position, lengths, prefixes):
    docs = lengths.shape[0]

    def step(doc, carry):
        start, low, high = carry
        end = start + lengths[doc]
        inside = (position >= start) & (position < end)
        reach = jnp.minimum(end, jnp.maximum(position + 1, start + prefixes[doc]))
        return end, jnp.where(inside, start, low), jnp.where(inside, reach, high)

    zero = jnp.zeros_like(position)
    carry = (jnp.int32(0), zero, zero)
    if docs <= 16:
        for doc in range(docs):
            carry = step(doc, carry)
    else:
        carry = lax.fori_loop(0, docs, step, carry)
    return carry[1], carry[2]


def grad_kernel(parts, lengths, prefixes, q_ref, *rest):
    cot_refs, got, rest = arranged(parts, (-1, 2, 1), rest)
    kv_own, rest = rest[0], rest[1:]
    kv_back1, kv_back2, kv_ahead = got[1], got[2], got[-1]
    dq_refs, rest = rest[:parts], rest[parts:]
    own_out, back1_out, back2_out, ahead_out, window, acc, cot_own, sems = rest
    rows, heads, size = q_ref.shape
    tokens = rows // parts
    kv_heads = kv_own.shape[1]
    group_size = heads // kv_heads
    span = (BACK + 1 + AHEAD) * rows
    reach = span - rows + tokens
    lanes = tokens * group_size
    scale = size ** (-0.5)
    shard = lax.axis_index("seq")
    me = lax.axis_index("kvh")

    loads = [
        pltpu.make_async_copy(
            kv_own, window.at[:, :, pl.ds(BACK * rows, rows)], sems.at[0]
        ),
        pltpu.make_async_copy(cot_refs[0], cot_own, sems.at[1]),
    ]
    cot_refs[0] = cot_own
    for load in loads:
        load.start()
    for slot, ref in ((0, kv_back2), (1, kv_back1), (BACK + 1, kv_ahead)):
        for number in range(2):
            for group in range(kv_heads):
                window[number, group, pl.ds(slot * rows, rows)] = ref[number, group]
    acc[...] = jnp.zeros_like(acc)

    contract_last = (((1,), (1,)), ((), ()))
    contract_first = (((0,), (0,)), ((), ()))
    for load in loads:
        load.wait()
    lane_token = lax.broadcasted_iota(jnp.int32, (1, lanes), 1) // group_size
    key_iota = lax.broadcasted_iota(jnp.int32, (reach, lanes), 0)
    for mask in range(parts):
        first = pl.multiple_of((me ^ mask) * tokens, tokens)
        low, high = bounds(shard * rows + first + lane_token, lengths, prefixes)
        origin = (shard - BACK) * rows + first
        low = low - origin
        high = high - origin
        visible = (key_iota >= low) & (key_iota < high)
        here = pl.ds(first, reach)
        for group in range(kv_heads):
            of_group = pl.ds(group * group_size, group_size)
            q = q_ref[pl.ds(first, tokens), of_group].astype(jnp.float32)
            q = q.reshape(lanes, size).astype(jnp.bfloat16)
            cot = cot_refs[mask][:, of_group].astype(jnp.float32)
            cot = cot.reshape(lanes, size).astype(jnp.bfloat16)
            k = window[0, group, here]
            v = window[1, group, here]
            scores = lax.dot_general(k, q, contract_last, preferred_element_type=jnp.float32)
            scores = jnp.where(visible, scores * (scale * LOG2E), NEG)
            top = jnp.max(scores, axis=0, keepdims=True)
            expo = jnp.exp2(scores - top)
            total = jnp.sum(expo, axis=0, keepdims=True)
            probs = expo * (1.0 / total)
            dprobs = lax.dot_general(v, cot, contract_last, preferred_element_type=jnp.float32)
            delta = jnp.sum(probs * dprobs, axis=0, keepdims=True)
            dscores = (probs * (dprobs - delta)).astype(jnp.bfloat16)
            acc[1, group, here] += jnp.dot(
                probs.astype(jnp.bfloat16), cot, preferred_element_type=jnp.float32
            )
            acc[0, group, here] += jnp.dot(dscores, q, preferred_element_type=jnp.float32)
            dq = lax.dot_general(k, dscores, contract_first, preferred_element_type=jnp.float32)
            dq = jnp.transpose(dq * scale)
            dq_refs[mask][:, of_group] = dq.reshape(tokens, group_size, size).astype(jnp.bfloat16)
    for slot, ref in enumerate((back2_out, back1_out, own_out, ahead_out)):
        for group in range(kv_heads):
            part = pl.ds(slot * rows, rows)
            ref[0, group] = (acc[0, group, part] * scale).astype(ref.dtype)
            ref[1, group] = acc[1, group, part].astype(ref.dtype)


def gradients(lengths, prefixes, queries, cots, got, kv):
    rows, heads, size = queries.shape
    parts = len(cots)
    kv_shape = kv.shape
    kv_heads = kv_shape[1]
    span = (BACK + 1 + AHEAD) * rows
    half = jax.ShapeDtypeStruct(kv_shape, jnp.bfloat16)
    work = heads * rows * span
    outs = pl.pallas_call(
        functools.partial(grad_kernel, parts),
        out_shape=(jax.ShapeDtypeStruct(cots[0].shape, jnp.bfloat16),) * parts
        + (jax.ShapeDtypeStruct(kv_shape, jnp.float32), half, half, half),
        in_specs=[_SMEM, _SMEM, _VMEM, _HBM] + [_VMEM] * (parts + 2) + [_HBM],
        out_specs=(_VMEM,) * (parts + 4),
        scratch_shapes=[
            pltpu.VMEM((2, kv_heads, span, size), jnp.bfloat16),
            pltpu.VMEM((2, kv_heads, span, size), jnp.float32),
            pltpu.VMEM(cots[0].shape, jnp.bfloat16),
            pltpu.SemaphoreType.DMA((2,)),
        ],
        compiler_params=pltpu.CompilerParams(vmem_limit_bytes=VMEM_BYTES),
        cost_estimate=pl.CostEstimate(
            flops=10 * work * size, bytes_accessed=4 * queries.size * 2, transcendentals=work
        ),
        name="gradients",
    )(lengths, prefixes, queries, *arrange(cots, got, (-1, 2, 1)), kv)
    return outs[:parts], outs[parts:]


def finish_kernel(parts, *refs):
    dq_refs, got, (own, dq_out, dk_out, dv_out) = arranged(parts, (1, -2, -1), refs)
    heads = dq_refs[0].shape[1]
    me = lax.axis_index("kvh")
    for mask in range(parts):
        first = pl.multiple_of((me ^ mask) * heads, heads)
        dq_out[:, pl.ds(first, heads), :] = dq_refs[mask][...]
    for number, ref in enumerate((dk_out, dv_out)):
        sums = []
        for group in range(ref.shape[1]):
            total = own[number, group]
            for other in (got[-1], got[-2], got[1]):
                total = total + other[number, group].astype(jnp.float32)
            sums.append(total)
        ref[...] = jnp.stack(sums, axis=1).astype(jnp.bfloat16)


def finish(dqs, own, got):
    parts = len(dqs)
    rows, heads, size = dqs[0].shape
    _, kv_heads, kv_rows, _ = own.shape
    kv_out = jax.ShapeDtypeStruct((kv_rows, kv_heads, size), jnp.bfloat16)
    return pl.pallas_call(
        functools.partial(finish_kernel, parts),
        out_shape=(
            jax.ShapeDtypeStruct((rows, heads * parts, size), jnp.bfloat16),
            kv_out,
            kv_out,
        ),
        in_specs=[_VMEM] * (parts + 4),
        out_specs=(_VMEM,) * 3,
        compiler_params=pltpu.CompilerParams(vmem_limit_bytes=VMEM_BYTES),
        name="finish",
    )(*arrange(dqs, got, (1, -2, -1)), own)


def shifted(block, distance):
    devices = range(lax.axis_size("seq"))
    route = [(i - distance, i) for i in devices if i - distance in devices]
    return lax.ppermute(block, "seq", route)


def swapped(block, mask):
    return lax.ppermute(block, "kvh", [(i, i ^ mask) for i in range(lax.axis_size("kvh"))])


def exchange(pieces, blocks):
    pieces = [pieces[0]] + [swapped(pieces[mask], mask) for mask in range(1, len(pieces))]
    return pieces, {shift: shifted(block, shift) for shift, block in blocks.items()}


def local(queries, keys, values, output_gradient, doc_lengths, prefix_lengths):
    parts = lax.axis_size("kvh")
    kv, cots = prepare(output_gradient, keys, values, parts)
    cots, got = exchange(cots, {1: kv[0], 2: kv[1], -1: kv[2]})
    dqs, (own, back1, back2, ahead) = gradients(
        doc_lengths, prefix_lengths, queries, cots, got, kv[0]
    )
    dqs, got = exchange(dqs, {-1: back1, -2: back2, 1: ahead})
    return finish(dqs, own, got)


def solution(mesh):
    in_specs = (
        P("seq", "kvh", None),
        P("seq", "kvh", None),
        P("seq", "kvh", None),
        P(("seq", "kvh"), None, None),
        P(),
        P(),
    )
    out_specs = (P(("seq", "kvh"), None, None), P("seq", "kvh", None), P("seq", "kvh", None))
    return jax.shard_map(local, mesh=mesh, in_specs=in_specs, out_specs=out_specs, check_vma=False)
```

```python
import functools

import jax
import jax.numpy as jnp
from jax import lax
from jax.experimental import pallas as pl
from jax.experimental.pallas import tpu as pltpu
from jax.sharding import PartitionSpec as P

BACK = 2
AHEAD = 1
LOG2E = 1.4426950408889634
VMEM_BYTES = 40 * 1024 * 1024
PREPARE_VMEM_BYTES = 60 * 1024 * 1024
NEG = -1e30

_VMEM = pl.BlockSpec(memory_space=pltpu.VMEM)
_SMEM = pl.BlockSpec(memory_space=pltpu.SMEM)
_HBM = pl.BlockSpec(memory_space=pltpu.HBM)


def sequence(parts, shifts):
    masks, shifts = list(range(parts - 1, 0, -1)), list(shifts)
    order = []
    while masks or shifts:
        if shifts:
            order.append(("shift", shifts.pop(0)))
        if masks:
            order.append(("mask", masks.pop(0)))
    return order


def arrange(pieces, blocks, shifts):
    return [
        pieces[which - 1] if kind == "mask" else blocks[which]
        for kind, which in sequence(len(pieces) + 1, shifts)
    ]


def arranged(parts, shifts, refs):
    order = sequence(parts, shifts)
    found = dict(zip(order, refs))
    return (
        [found["mask", mask] for mask in range(1, parts)],
        {shift: found["shift", shift] for shift in shifts},
        refs[len(order):],
    )


def regroup(buf):
    wide = buf[...].astype(jnp.float32)
    return [wide[:, group, :].astype(jnp.bfloat16) for group in range(buf.shape[1])]


def prep_kernel(parts, cot_ref, key_ref, value_ref, *rest):
    kv_outs, cot_outs, rest = rest[:3], rest[3 : parts + 2], rest[parts + 2 :]
    key_buf, value_buf, packed, sems, kv_sems = rest
    heads = cot_ref.shape[1] // parts
    me = lax.axis_index("kvh")
    loads = []
    for number, (ref, buf) in enumerate(((key_ref, key_buf), (value_ref, value_buf))):
        loads.append(pltpu.make_async_copy(ref, buf, sems.at[number]))
        loads[-1].start()
    copies = []
    for mask in range(1, parts):
        first = pl.multiple_of((me ^ mask) * heads, heads)
        copies.append(
            pltpu.make_async_copy(
                cot_ref.at[:, pl.ds(first, heads), :], cot_outs[mask - 1], sems.at[mask + 1]
            )
        )
        copies[-1].start()
    for number, buf in enumerate((key_buf, value_buf)):
        loads[number].wait()
        for group, block in enumerate(regroup(buf)):
            packed[number, group] = block
    for number, kv_out in enumerate(kv_outs):
        copies.append(pltpu.make_async_copy(packed, kv_out, kv_sems.at[number]))
        copies[-1].start()
    for copy in copies:
        copy.wait()


def prepare(cotangent, keys, values, parts):
    rows, heads, size = cotangent.shape
    kv_rows, kv_heads, _ = keys.shape
    piece = jax.ShapeDtypeStruct((rows, heads // parts, size), jnp.bfloat16)
    block = jax.ShapeDtypeStruct((2, kv_heads, kv_rows, size), jnp.bfloat16)
    outs = pl.pallas_call(
        functools.partial(prep_kernel, parts),
        out_shape=(block,) * 3 + (piece,) * (parts - 1),
        in_specs=[_HBM] * 3,
        out_specs=(_HBM,) * (parts + 2),
        scratch_shapes=[
            pltpu.VMEM(keys.shape, jnp.bfloat16),
            pltpu.VMEM(values.shape, jnp.bfloat16),
            pltpu.VMEM(block.shape, jnp.bfloat16),
            pltpu.SemaphoreType.DMA((parts + 1,)),
            pltpu.SemaphoreType.DMA((3,)),
        ],
        compiler_params=pltpu.CompilerParams(vmem_limit_bytes=PREPARE_VMEM_BYTES),
        name="prepare",
    )(cotangent, keys, values)
    return outs[:3], outs[3:]


def bounds(position, lengths, prefixes):
    docs = lengths.shape[0]

    def step(doc, carry):
        start, low, high = carry
        end = start + lengths[doc]
        inside = (position >= start) & (position < end)
        reach = jnp.minimum(end, jnp.maximum(position + 1, start + prefixes[doc]))
        return end, jnp.where(inside, start, low), jnp.where(inside, reach, high)

    zero = jnp.zeros_like(position)
    carry = (jnp.int32(0), zero, zero)
    if docs <= 16:
        for doc in range(docs):
            carry = step(doc, carry)
    else:
        carry = lax.fori_loop(0, docs, step, carry)
    return carry[1], carry[2]


def grad_kernel(parts, lengths, prefixes, q_ref, cot_ref, key_ref, value_ref, *rest):
    cot_refs, got, rest = arranged(parts, (-1, 2, 1), rest)
    kv_back1, kv_back2, kv_ahead = got[1], got[2], got[-1]
    dq_refs, rest = rest[:parts], rest[parts:]
    own_out, back1_out, back2_out, ahead_out, window, acc = rest
    rows, heads, size = q_ref.shape
    tokens = rows // parts
    kv_heads = key_ref.shape[1]
    group_size = heads // kv_heads
    span = (BACK + 1 + AHEAD) * rows
    reach = span - rows + tokens
    lanes = tokens * group_size
    scale = size ** (-0.5)
    shard = lax.axis_index("seq")
    me = lax.axis_index("kvh")

    for number, buf in enumerate((key_ref, value_ref)):
        for group, block in enumerate(regroup(buf)):
            window[number, group, pl.ds(BACK * rows, rows)] = block
    for slot, ref in ((0, kv_back2), (1, kv_back1), (BACK + 1, kv_ahead)):
        for number in range(2):
            for group in range(kv_heads):
                window[number, group, pl.ds(slot * rows, rows)] = ref[number, group]
    acc[...] = jnp.zeros_like(acc)

    contract_last = (((1,), (1,)), ((), ()))
    contract_first = (((0,), (0,)), ((), ()))
    lane_token = lax.broadcasted_iota(jnp.int32, (1, lanes), 1) // group_size
    key_iota = lax.broadcasted_iota(jnp.int32, (reach, lanes), 0)
    for mask in range(parts):
        first = pl.multiple_of((me ^ mask) * tokens, tokens)
        low, high = bounds(shard * rows + first + lane_token, lengths, prefixes)
        origin = (shard - BACK) * rows + first
        low = low - origin
        high = high - origin
        visible = (key_iota >= low) & (key_iota < high)
        here = pl.ds(first, reach)
        for group in range(kv_heads):
            of_group = pl.ds(group * group_size, group_size)
            q = q_ref[pl.ds(first, tokens), of_group].astype(jnp.float32)
            q = q.reshape(lanes, size).astype(jnp.bfloat16)
            if mask == 0:
                own_head = pl.multiple_of(me * heads + group * group_size, group_size)
                cot = cot_ref[:, pl.ds(own_head, group_size)].astype(jnp.float32)
            else:
                cot = cot_refs[mask - 1][:, of_group].astype(jnp.float32)
            cot = cot.reshape(lanes, size).astype(jnp.bfloat16)
            k = window[0, group, here]
            v = window[1, group, here]
            scores = lax.dot_general(k, q, contract_last, preferred_element_type=jnp.float32)
            scores = jnp.where(visible, scores * (scale * LOG2E), NEG)
            top = jnp.max(scores, axis=0, keepdims=True)
            expo = jnp.exp2(scores - top)
            total = jnp.sum(expo, axis=0, keepdims=True)
            probs = expo * (1.0 / total)
            dprobs = lax.dot_general(v, cot, contract_last, preferred_element_type=jnp.float32)
            delta = jnp.sum(probs * dprobs, axis=0, keepdims=True)
            dscores = (probs * (dprobs - delta)).astype(jnp.bfloat16)
            acc[1, group, here] += jnp.dot(
                probs.astype(jnp.bfloat16), cot, preferred_element_type=jnp.float32
            )
            acc[0, group, here] += jnp.dot(dscores, q, preferred_element_type=jnp.float32)
            dq = lax.dot_general(k, dscores, contract_first, preferred_element_type=jnp.float32)
            dq = jnp.transpose(dq * scale)
            dq_refs[mask][:, of_group] = dq.reshape(tokens, group_size, size).astype(jnp.bfloat16)
    for slot, ref in enumerate((back2_out, back1_out, own_out, ahead_out)):
        for group in range(kv_heads):
            part = pl.ds(slot * rows, rows)
            ref[0, group] = (acc[0, group, part] * scale).astype(ref.dtype)
            ref[1, group] = acc[1, group, part].astype(ref.dtype)


def gradients(lengths, prefixes, queries, cotangent, keys, values, cots, got):
    rows, heads, size = queries.shape
    parts = len(cots) + 1
    kv_shape = got[1].shape
    kv_heads = kv_shape[1]
    span = (BACK + 1 + AHEAD) * rows
    half = jax.ShapeDtypeStruct(kv_shape, jnp.bfloat16)
    work = heads * rows * span
    outs = pl.pallas_call(
        functools.partial(grad_kernel, parts),
        out_shape=(jax.ShapeDtypeStruct(cots[0].shape, jnp.bfloat16),) * parts
        + (jax.ShapeDtypeStruct(kv_shape, jnp.float32), half, half, half),
        in_specs=[_SMEM, _SMEM] + [_VMEM] * (parts + 6),
        out_specs=(_VMEM,) * (parts + 4),
        scratch_shapes=[
            pltpu.VMEM((2, kv_heads, span, size), jnp.bfloat16),
            pltpu.VMEM((2, kv_heads, span, size), jnp.float32),
        ],
        compiler_params=pltpu.CompilerParams(vmem_limit_bytes=VMEM_BYTES),
        cost_estimate=pl.CostEstimate(
            flops=10 * work * size, bytes_accessed=4 * queries.size * 2, transcendentals=work
        ),
        name="gradients",
    )(lengths, prefixes, queries, cotangent, keys, values, *arrange(cots, got, (-1, 2, 1)))
    return outs[:parts], outs[parts:]


def finish_kernel(parts, *refs):
    dq_refs, got, rest = arranged(parts, (1, -2, -1), refs)
    dq_own, own, dq_out, dk_out, dv_out = rest
    dq_refs = [dq_own] + dq_refs
    heads = dq_refs[0].shape[1]
    me = lax.axis_index("kvh")
    for mask in range(parts):
        first = pl.multiple_of((me ^ mask) * heads, heads)
        dq_out[:, pl.ds(first, heads), :] = dq_refs[mask][...]
    for number, ref in enumerate((dk_out, dv_out)):
        sums = []
        for group in range(ref.shape[1]):
            total = own[number, group]
            for other in (got[-1], got[-2], got[1]):
                total = total + other[number, group].astype(jnp.float32)
            sums.append(total)
        ref[...] = jnp.stack(sums, axis=1).astype(jnp.bfloat16)


def finish(dq_own, dqs, own, got):
    parts = len(dqs) + 1
    rows, heads, size = dqs[0].shape
    _, kv_heads, kv_rows, _ = own.shape
    kv_out = jax.ShapeDtypeStruct((kv_rows, kv_heads, size), jnp.bfloat16)
    return pl.pallas_call(
        functools.partial(finish_kernel, parts),
        out_shape=(
            jax.ShapeDtypeStruct((rows, heads * parts, size), jnp.bfloat16),
            kv_out,
            kv_out,
        ),
        in_specs=[_VMEM] * (parts + 4),
        out_specs=(_VMEM,) * 3,
        compiler_params=pltpu.CompilerParams(vmem_limit_bytes=VMEM_BYTES),
        name="finish",
    )(*arrange(dqs, got, (1, -2, -1)), dq_own, own)


def shifted(block, distance):
    count = lax.axis_size("seq")
    return lax.ppermute(block, "seq", [(i, (i + distance) % count) for i in range(count)])


def swapped(block, mask):
    return lax.ppermute(block, "kvh", [(i, i ^ mask) for i in range(lax.axis_size("kvh"))])


def exchange(pieces, blocks):
    pieces = [swapped(piece, mask) for mask, piece in enumerate(pieces, 1)]
    return pieces, {shift: shifted(block, shift) for shift, block in blocks.items()}


def local(queries, keys, values, output_gradient, doc_lengths, prefix_lengths):
    parts = lax.axis_size("kvh")
    kv, cots = prepare(output_gradient, keys, values, parts)
    cots, got = exchange(cots, {1: kv[0], 2: kv[1], -1: kv[2]})
    dqs, (own, back1, back2, ahead) = gradients(
        doc_lengths, prefix_lengths, queries, output_gradient, keys, values, cots, got
    )
    dqs_got, got = exchange(dqs[1:], {-1: back1, -2: back2, 1: ahead})
    return finish(dqs[0], dqs_got, own, got)


def solution(mesh):
    in_specs = (
        P("seq", "kvh", None),
        P("seq", "kvh", None),
        P("seq", "kvh", None),
        P(("seq", "kvh"), None, None),
        P(),
        P(),
    )
    out_specs = (P(("seq", "kvh"), None, None), P("seq", "kvh", None), P("seq", "kvh", None))
    return jax.shard_map(local, mesh=mesh, in_specs=in_specs, out_specs=out_specs, check_vma=False)
```

```python
import functools

import jax
import jax.numpy as jnp
from jax import lax
from jax.experimental import pallas as pl
from jax.experimental.pallas import tpu as pltpu
from jax.sharding import PartitionSpec as P

BACK = 2
AHEAD = 1
LOG2E = 1.4426950408889634
VMEM_BYTES = 40 * 1024 * 1024
NEG = -1e30

_VMEM = pl.BlockSpec(memory_space=pltpu.VMEM)
_SMEM = pl.BlockSpec(memory_space=pltpu.SMEM)
_HBM = pl.BlockSpec(memory_space=pltpu.HBM)


def order(parts):
    masks = ["mask", *range(parts - 1, 0, -1)][1:]
    return ["far", masks[0], "even", "odd"] + masks[1:]


def regroup(buf):
    wide = buf[...].astype(jnp.float32)
    return [wide[:, group, :].astype(jnp.bfloat16) for group in range(buf.shape[1])]


def prep_kernel(parts, cot_ref, key_ref, value_ref, *rest):
    kv_outs, cot_outs, (key_buf, value_buf, sems) = rest[:3], rest[3 : parts + 3], rest[parts + 3 :]
    heads = cot_ref.shape[1] // parts
    me = lax.axis_index("kvh")
    loads = []
    for number, (ref, buf) in enumerate(((key_ref, key_buf), (value_ref, value_buf))):
        loads.append(pltpu.make_async_copy(ref, buf, sems.at[number]))
        loads[-1].start()
    copies = []
    for mask in range(parts):
        first = pl.multiple_of((me ^ mask) * heads, heads)
        copies.append(
            pltpu.make_async_copy(
                cot_ref.at[:, pl.ds(first, heads), :], cot_outs[mask], sems.at[mask + 2]
            )
        )
        copies[-1].start()
    for number, buf in enumerate((key_buf, value_buf)):
        loads[number].wait()
        for group, block in enumerate(regroup(buf)):
            for kv_out in kv_outs:
                kv_out[number, group] = block
    for copy in copies:
        copy.wait()


def prepare(cotangent, keys, values, parts):
    rows, heads, size = cotangent.shape
    kv_rows, kv_heads, _ = keys.shape
    piece = pltpu.VMEM((rows, heads // parts, size), jnp.bfloat16)
    block = pltpu.VMEM((2, kv_heads, kv_rows, size), jnp.bfloat16)
    operands = [
        pltpu.with_memory_space_constraint(array, pltpu.HBM)
        for array in (cotangent, keys, values)
    ]
    outs = pl.pallas_call(
        functools.partial(prep_kernel, parts),
        out_shape=(block,) * 3 + (piece,) * parts,
        in_specs=[_HBM] * 3,
        out_specs=(_VMEM,) * (parts + 3),
        scratch_shapes=[
            pltpu.VMEM(keys.shape, jnp.bfloat16),
            pltpu.VMEM(values.shape, jnp.bfloat16),
            pltpu.SemaphoreType.DMA((parts + 2,)),
        ],
        compiler_params=pltpu.CompilerParams(vmem_limit_bytes=VMEM_BYTES),
        name="prepare",
    )(*operands)
    return outs[:3], outs[3:]


def bounds(position, lengths, prefixes):
    docs = lengths.shape[0]

    def step(doc, carry):
        start, low, high = carry
        end = start + lengths[doc]
        inside = (position >= start) & (position < end)
        reach = jnp.minimum(end, jnp.maximum(position + 1, start + prefixes[doc]))
        return end, jnp.where(inside, start, low), jnp.where(inside, reach, high)

    zero = jnp.zeros_like(position)
    carry = (jnp.int32(0), zero, zero)
    if docs <= 16:
        for doc in range(docs):
            carry = step(doc, carry)
    else:
        carry = lax.fori_loop(0, docs, step, carry)
    return carry[1], carry[2]


def neighbour_slots(shard):
    odd = shard % 2
    ahead, behind = BACK + 1, BACK - 1
    return jnp.where(odd == 1, behind, ahead), jnp.where(odd == 1, ahead, behind)


def grad_kernel(parts, lengths, prefixes, q_ref, cot_own, kv_own, *rest):
    names = order(parts)
    got, rest = dict(zip(names, rest)), rest[len(names) :]
    dq_refs, rest = rest[:parts], rest[parts:]
    own_out, far_out, even_out, odd_out, window, acc = rest
    rows, heads, size = q_ref.shape
    tokens = rows // parts
    kv_heads = kv_own.shape[1]
    group_size = heads // kv_heads
    span = (BACK + 1 + AHEAD) * rows
    reach = span - rows + tokens
    lanes = tokens * group_size
    scale = size ** (-0.5)
    shard = lax.axis_index("seq")
    me = lax.axis_index("kvh")

    even_slot, odd_slot = neighbour_slots(shard)
    slots = ((BACK, kv_own), (0, got["far"]), (even_slot, got["even"]), (odd_slot, got["odd"]))
    for slot, ref in slots:
        for number in range(2):
            for group in range(kv_heads):
                part = pl.ds(pl.multiple_of(slot * rows, rows), rows)
                window[number, group, part] = ref[number, group]
    acc[...] = jnp.zeros_like(acc)

    contract_last = (((1,), (1,)), ((), ()))
    contract_first = (((0,), (0,)), ((), ()))
    lane_token = lax.broadcasted_iota(jnp.int32, (1, lanes), 1) // group_size
    key_iota = lax.broadcasted_iota(jnp.int32, (reach, lanes), 0)
    for mask in range(parts):
        first = pl.multiple_of((me ^ mask) * tokens, tokens)
        low, high = bounds(shard * rows + first + lane_token, lengths, prefixes)
        origin = (shard - BACK) * rows + first
        low = low - origin
        high = high - origin
        visible = (key_iota >= low) & (key_iota < high)
        here = pl.ds(first, reach)
        for group in range(kv_heads):
            of_group = pl.ds(group * group_size, group_size)
            q = q_ref[pl.ds(first, tokens), of_group].astype(jnp.float32)
            q = q.reshape(lanes, size).astype(jnp.bfloat16)
            cot = (got[mask] if mask else cot_own)[:, of_group].astype(jnp.float32)
            cot = cot.reshape(lanes, size).astype(jnp.bfloat16)
            k = window[0, group, here]
            v = window[1, group, here]
            scores = lax.dot_general(k, q, contract_last, preferred_element_type=jnp.float32)
            scores = jnp.where(visible, scores * (scale * LOG2E), NEG)
            top = jnp.max(scores, axis=0, keepdims=True)
            expo = jnp.exp2(scores - top)
            total = jnp.sum(expo, axis=0, keepdims=True)
            probs = expo * (1.0 / total)
            dprobs = lax.dot_general(v, cot, contract_last, preferred_element_type=jnp.float32)
            delta = jnp.sum(probs * dprobs, axis=0, keepdims=True)
            dscores = (probs * (dprobs - delta)).astype(jnp.bfloat16)
            acc[1, group, here] += jnp.dot(
                probs.astype(jnp.bfloat16), cot, preferred_element_type=jnp.float32
            )
            acc[0, group, here] += jnp.dot(dscores, q, preferred_element_type=jnp.float32)
            dq = lax.dot_general(k, dscores, contract_first, preferred_element_type=jnp.float32)
            dq = jnp.transpose(dq * scale)
            dq_refs[mask][:, of_group] = dq.reshape(tokens, group_size, size).astype(jnp.bfloat16)
    for slot, ref in ((0, far_out), (even_slot, even_out), (odd_slot, odd_out), (BACK, own_out)):
        for group in range(kv_heads):
            part = pl.ds(pl.multiple_of(slot * rows, rows), rows)
            ref[0, group] = (acc[0, group, part] * scale).astype(ref.dtype)
            ref[1, group] = acc[1, group, part].astype(ref.dtype)


def gradients(lengths, prefixes, queries, cot_own, kv_own, got, parts):
    rows, heads, size = queries.shape
    kv_shape = got["far"].shape
    kv_heads = kv_shape[1]
    span = (BACK + 1 + AHEAD) * rows
    half = jax.ShapeDtypeStruct(kv_shape, jnp.bfloat16)
    work = heads * rows * span
    outs = pl.pallas_call(
        functools.partial(grad_kernel, parts),
        out_shape=(jax.ShapeDtypeStruct(got[1].shape, jnp.bfloat16),) * parts
        + (jax.ShapeDtypeStruct(kv_shape, jnp.float32), half, half, half),
        in_specs=[_SMEM, _SMEM] + [_VMEM] * (parts + 5),
        out_specs=(_VMEM,) * (parts + 4),
        scratch_shapes=[
            pltpu.VMEM((2, kv_heads, span, size), jnp.bfloat16),
            pltpu.VMEM((2, kv_heads, span, size), jnp.float32),
        ],
        compiler_params=pltpu.CompilerParams(vmem_limit_bytes=VMEM_BYTES),
        cost_estimate=pl.CostEstimate(
            flops=10 * work * size, bytes_accessed=4 * queries.size * 2, transcendentals=work
        ),
        name="gradients",
    )(lengths, prefixes, queries, cot_own, kv_own, *[got[name] for name in order(parts)])
    return outs[:parts], outs[parts:]


def finish_kernel(parts, *refs):
    names = order(parts)
    got, (dq_own, own, dq_out, dk_out, dv_out) = dict(zip(names, refs)), refs[len(names) :]
    heads = dq_own.shape[1]
    me = lax.axis_index("kvh")
    for mask in range(parts):
        first = pl.multiple_of((me ^ mask) * heads, heads)
        dq_out[:, pl.ds(first, heads), :] = (got[mask] if mask else dq_own)[...]
    for number, ref in enumerate((dk_out, dv_out)):
        sums = []
        for group in range(ref.shape[1]):
            total = own[number, group]
            for other in (got["far"], got["even"], got["odd"]):
                total = total + other[number, group].astype(jnp.float32)
            sums.append(total)
        ref[...] = jnp.stack(sums, axis=1).astype(jnp.bfloat16)


def finish(dq_own, own, got, parts):
    rows, heads, size = dq_own.shape
    _, kv_heads, kv_rows, _ = own.shape
    kv_out = jax.ShapeDtypeStruct((kv_rows, kv_heads, size), jnp.bfloat16)
    return pl.pallas_call(
        functools.partial(finish_kernel, parts),
        out_shape=(
            jax.ShapeDtypeStruct((rows, heads * parts, size), jnp.bfloat16),
            kv_out,
            kv_out,
        ),
        in_specs=[_VMEM] * (parts + 4),
        out_specs=(_VMEM,) * 3,
        compiler_params=pltpu.CompilerParams(vmem_limit_bytes=VMEM_BYTES),
        name="finish",
    )(*[got[name] for name in order(parts)], dq_own, own)


def shifted(block, distance):
    devices = range(lax.axis_size("seq"))
    route = [(i, i + distance) for i in devices if i + distance in devices]
    return lax.ppermute(block, "seq", route)


def paired(block, first):
    count = lax.axis_size("seq")
    route = []
    for i in range(count):
        partner = i + 1 if i % 2 == first else i - 1
        route.append((i, partner if 0 <= partner < count else i))
    return lax.ppermute(block, "seq", route)


def swapped(block, mask):
    return lax.ppermute(block, "kvh", [(i, i ^ mask) for i in range(lax.axis_size("kvh"))])


def exchange(pieces, far, even, odd, distance):
    got = {mask: swapped(piece, mask) for mask, piece in enumerate(pieces, 1)}
    got["far"] = shifted(far, distance)
    got["even"] = paired(even, 0)
    got["odd"] = paired(odd, 1)
    return got


def local(queries, keys, values, output_gradient, doc_lengths, prefix_lengths):
    parts = lax.axis_size("kvh")
    kv, cots = prepare(output_gradient, keys, values, parts)
    got = exchange(cots[1:], *kv, BACK)
    dqs, (own, far, even, odd) = gradients(
        doc_lengths, prefix_lengths, queries, cots[0], kv[0], got, parts
    )
    got = exchange(dqs[1:], far, even, odd, -BACK)
    return finish(dqs[0], own, got, parts)


def solution(mesh):
    in_specs = (
        P("seq", "kvh", None),
        P("seq", "kvh", None),
        P("seq", "kvh", None),
        P(("seq", "kvh"), None, None),
        P(),
        P(),
    )
    out_specs = (P(("seq", "kvh"), None, None), P("seq", "kvh", None), P("seq", "kvh", None))
    return jax.shard_map(local, mesh=mesh, in_specs=in_specs, out_specs=out_specs, check_vma=False)
```

```python
import functools

import jax
import jax.numpy as jnp
from jax import lax
from jax.experimental import pallas as pl
from jax.experimental.pallas import tpu as pltpu
from jax.sharding import PartitionSpec as P

BACK = 2
AHEAD = 1
LOG2E = 1.4426950408889634
VMEM_BYTES = 40 * 1024 * 1024
NEG = -1e30

_VMEM = pl.BlockSpec(memory_space=pltpu.VMEM)
_SMEM = pl.BlockSpec(memory_space=pltpu.SMEM)
_HBM = pl.BlockSpec(memory_space=pltpu.HBM)


def order(parts):
    masks = ["mask", *range(parts - 1, 0, -1)][1:]
    return ["far", masks[0], "even", "odd"] + masks[1:]


def regroup(buf):
    wide = buf[...].astype(jnp.float32)
    return [wide[:, group, :].astype(jnp.bfloat16) for group in range(buf.shape[1])]


def prep_kernel(parts, cot_ref, key_ref, value_ref, *rest):
    kv_outs, cot_outs, (key_buf, value_buf, sems) = rest[:4], rest[4 : parts + 4], rest[parts + 4 :]
    heads = cot_ref.shape[1] // parts
    me = lax.axis_index("kvh")
    loads = []
    for number, (ref, buf) in enumerate(((key_ref, key_buf), (value_ref, value_buf))):
        loads.append(pltpu.make_async_copy(ref, buf, sems.at[number]))
        loads[-1].start()
    copies = []
    for mask in range(parts):
        first = pl.multiple_of((me ^ mask) * heads, heads)
        copies.append(
            pltpu.make_async_copy(
                cot_ref.at[:, pl.ds(first, heads), :], cot_outs[mask], sems.at[mask + 2]
            )
        )
        copies[-1].start()
    for number, buf in enumerate((key_buf, value_buf)):
        loads[number].wait()
        for group, block in enumerate(regroup(buf)):
            for kv_out in kv_outs:
                kv_out[number, group] = block
    for copy in copies:
        copy.wait()


def prepare(cotangent, keys, values, parts):
    rows, heads, size = cotangent.shape
    kv_rows, kv_heads, _ = keys.shape
    piece = pltpu.VMEM((rows, heads // parts, size), jnp.bfloat16)
    block = pltpu.VMEM((2, kv_heads, kv_rows, size), jnp.bfloat16)
    operands = [
        pltpu.with_memory_space_constraint(array, pltpu.HBM)
        for array in (cotangent, keys, values)
    ]
    outs = pl.pallas_call(
        functools.partial(prep_kernel, parts),
        out_shape=(block,) * 4 + (piece,) * parts,
        in_specs=[_HBM] * 3,
        out_specs=(_VMEM,) * (parts + 4),
        scratch_shapes=[
            pltpu.VMEM(keys.shape, jnp.bfloat16),
            pltpu.VMEM(values.shape, jnp.bfloat16),
            pltpu.SemaphoreType.DMA((parts + 2,)),
        ],
        compiler_params=pltpu.CompilerParams(vmem_limit_bytes=VMEM_BYTES),
        name="prepare",
    )(*operands)
    return outs[:4], outs[4:]


def bounds(position, lengths, prefixes):
    docs = lengths.shape[0]

    def step(doc, carry):
        start, low, high = carry
        end = start + lengths[doc]
        inside = (position >= start) & (position < end)
        reach = jnp.minimum(end, jnp.maximum(position + 1, start + prefixes[doc]))
        return end, jnp.where(inside, start, low), jnp.where(inside, reach, high)

    zero = jnp.zeros_like(position)
    carry = (jnp.int32(0), zero, zero)
    if docs <= 16:
        for doc in range(docs):
            carry = step(doc, carry)
    else:
        carry = lax.fori_loop(0, docs, step, carry)
    return carry[1], carry[2]


def neighbour_slots(shard):
    odd = shard % 2
    ahead, behind = BACK + 1, BACK - 1
    return jnp.where(odd == 1, behind, ahead), jnp.where(odd == 1, ahead, behind)


def grad_kernel(parts, lengths, prefixes, q_ref, cot_own, kv_own, *rest):
    names = order(parts)
    got, rest = dict(zip(names, rest)), rest[len(names) :]
    dq_refs, rest = rest[:parts], rest[parts:]
    own_out, far_out, even_out, odd_out, window, acc = rest
    rows, heads, size = q_ref.shape
    tokens = rows // parts
    kv_heads = kv_own.shape[1]
    group_size = heads // kv_heads
    span = (BACK + 1 + AHEAD) * rows
    reach = span - rows + tokens
    lanes = tokens * group_size
    scale = size ** (-0.5)
    shard = lax.axis_index("seq")
    me = lax.axis_index("kvh")

    even_slot, odd_slot = neighbour_slots(shard)
    slots = ((BACK, kv_own), (0, got["far"]), (even_slot, got["even"]), (odd_slot, got["odd"]))
    for slot, ref in slots:
        for number in range(2):
            for group in range(kv_heads):
                part = pl.ds(pl.multiple_of(slot * rows, rows), rows)
                window[number, group, part] = ref[number, group]
    acc[...] = jnp.zeros_like(acc)

    contract_last = (((1,), (1,)), ((), ()))
    contract_first = (((0,), (0,)), ((), ()))
    lane_token = lax.broadcasted_iota(jnp.int32, (1, lanes), 1) // group_size
    key_iota = lax.broadcasted_iota(jnp.int32, (reach, lanes), 0)
    for mask in range(parts):
        first = pl.multiple_of((me ^ mask) * tokens, tokens)
        low, high = bounds(shard * rows + first + lane_token, lengths, prefixes)
        origin = (shard - BACK) * rows + first
        low = low - origin
        high = high - origin
        visible = (key_iota >= low) & (key_iota < high)
        here = pl.ds(first, reach)
        for group in range(kv_heads):
            of_group = pl.ds(group * group_size, group_size)
            q = q_ref[pl.ds(first, tokens), of_group].astype(jnp.float32)
            q = q.reshape(lanes, size).astype(jnp.bfloat16)
            cot = (got[mask] if mask else cot_own)[:, of_group].astype(jnp.float32)
            cot = cot.reshape(lanes, size).astype(jnp.bfloat16)
            k = window[0, group, here]
            v = window[1, group, here]
            scores = lax.dot_general(k, q, contract_last, preferred_element_type=jnp.float32)
            scores = jnp.where(visible, scores * (scale * LOG2E), NEG)
            top = jnp.max(scores, axis=0, keepdims=True)
            expo = jnp.exp2(scores - top)
            total = jnp.sum(expo, axis=0, keepdims=True)
            probs = expo * (1.0 / total)
            dprobs = lax.dot_general(v, cot, contract_last, preferred_element_type=jnp.float32)
            delta = jnp.sum(probs * dprobs, axis=0, keepdims=True)
            dscores = (probs * (dprobs - delta)).astype(jnp.bfloat16)
            acc[1, group, here] += jnp.dot(
                probs.astype(jnp.bfloat16), cot, preferred_element_type=jnp.float32
            )
            acc[0, group, here] += jnp.dot(dscores, q, preferred_element_type=jnp.float32)
            dq = lax.dot_general(k, dscores, contract_first, preferred_element_type=jnp.float32)
            dq = jnp.transpose(dq * scale)
            dq_refs[mask][:, of_group] = dq.reshape(tokens, group_size, size).astype(jnp.bfloat16)
    for slot, ref in ((0, far_out), (even_slot, even_out), (odd_slot, odd_out), (BACK, own_out)):
        for group in range(kv_heads):
            part = pl.ds(pl.multiple_of(slot * rows, rows), rows)
            ref[0, group] = (acc[0, group, part] * scale).astype(ref.dtype)
            ref[1, group] = acc[1, group, part].astype(ref.dtype)


def gradients(lengths, prefixes, queries, cot_own, kv_own, got, parts):
    rows, heads, size = queries.shape
    kv_shape = got["far"].shape
    kv_heads = kv_shape[1]
    span = (BACK + 1 + AHEAD) * rows
    half = jax.ShapeDtypeStruct(kv_shape, jnp.bfloat16)
    work = heads * rows * span
    outs = pl.pallas_call(
        functools.partial(grad_kernel, parts),
        out_shape=(jax.ShapeDtypeStruct(got[1].shape, jnp.bfloat16),) * parts
        + (jax.ShapeDtypeStruct(kv_shape, jnp.float32), half, half, half),
        in_specs=[_SMEM, _SMEM] + [_VMEM] * (parts + 5),
        out_specs=(_VMEM,) * (parts + 4),
        scratch_shapes=[
            pltpu.VMEM((2, kv_heads, span, size), jnp.bfloat16),
            pltpu.VMEM((2, kv_heads, span, size), jnp.float32),
        ],
        compiler_params=pltpu.CompilerParams(vmem_limit_bytes=VMEM_BYTES),
        cost_estimate=pl.CostEstimate(
            flops=10 * work * size, bytes_accessed=4 * queries.size * 2, transcendentals=work
        ),
        name="gradients",
    )(lengths, prefixes, queries, cot_own, kv_own, *[got[name] for name in order(parts)])
    return outs[:parts], outs[parts:]


def finish_kernel(parts, *refs):
    names = order(parts)
    got, (dq_own, own, dq_out, dk_out, dv_out) = dict(zip(names, refs)), refs[len(names) :]
    heads = dq_own.shape[1]
    me = lax.axis_index("kvh")
    for mask in range(parts):
        first = pl.multiple_of((me ^ mask) * heads, heads)
        dq_out[:, pl.ds(first, heads), :] = (got[mask] if mask else dq_own)[...]
    for number, ref in enumerate((dk_out, dv_out)):
        sums = []
        for group in range(ref.shape[1]):
            total = own[number, group]
            for other in (got["far"], got["even"], got["odd"]):
                total = total + other[number, group].astype(jnp.float32)
            sums.append(total)
        ref[...] = jnp.stack(sums, axis=1).astype(jnp.bfloat16)


def finish(dq_own, own, got, parts):
    rows, heads, size = dq_own.shape
    _, kv_heads, kv_rows, _ = own.shape
    kv_out = jax.ShapeDtypeStruct((kv_rows, kv_heads, size), jnp.bfloat16)
    return pl.pallas_call(
        functools.partial(finish_kernel, parts),
        out_shape=(
            jax.ShapeDtypeStruct((rows, heads * parts, size), jnp.bfloat16),
            kv_out,
            kv_out,
        ),
        in_specs=[_VMEM] * (parts + 4),
        out_specs=(_VMEM,) * 3,
        compiler_params=pltpu.CompilerParams(vmem_limit_bytes=VMEM_BYTES),
        name="finish",
    )(*[got[name] for name in order(parts)], dq_own, own)


def shifted(block, distance):
    devices = range(lax.axis_size("seq"))
    route = [(i, i + distance) for i in devices if i + distance in devices]
    return lax.ppermute(block, "seq", route)


def paired(block, first):
    count = lax.axis_size("seq")
    route = []
    for i in range(count):
        partner = i + 1 if i % 2 == first else i - 1
        route.append((i, partner if 0 <= partner < count else i))
    return lax.ppermute(block, "seq", route)


def swapped(block, mask):
    return lax.ppermute(block, "kvh", [(i, i ^ mask) for i in range(lax.axis_size("kvh"))])


def exchange(pieces, far, even, odd, distance):
    got = {mask: swapped(piece, mask) for mask, piece in enumerate(pieces, 1)}
    got["far"] = shifted(far, distance)
    got["even"] = paired(even, 0)
    got["odd"] = paired(odd, 1)
    return got


def local(queries, keys, values, output_gradient, doc_lengths, prefix_lengths):
    parts = lax.axis_size("kvh")
    kv, cots = prepare(output_gradient, keys, values, parts)
    got = exchange(cots[1:], *kv[1:], BACK)
    dqs, (own, far, even, odd) = gradients(
        doc_lengths, prefix_lengths, queries, cots[0], kv[0], got, parts
    )
    got = exchange(dqs[1:], far, even, odd, -BACK)
    return finish(dqs[0], own, got, parts)


def solution(mesh):
    in_specs = (
        P("seq", "kvh", None),
        P("seq", "kvh", None),
        P("seq", "kvh", None),
        P(("seq", "kvh"), None, None),
        P(),
        P(),
    )
    out_specs = (P(("seq", "kvh"), None, None), P("seq", "kvh", None), P("seq", "kvh", None))
    return jax.shard_map(local, mesh=mesh, in_specs=in_specs, out_specs=out_specs, check_vma=False)
```

```python
import functools

import jax
import jax.numpy as jnp
from jax import lax
from jax.experimental import pallas as pl
from jax.experimental.pallas import tpu as pltpu
from jax.sharding import PartitionSpec as P

BACK = 2
AHEAD = 1
LOG2E = 1.4426950408889634
VMEM_BYTES = 40 * 1024 * 1024
NEG = -1e30

_VMEM = pl.BlockSpec(memory_space=pltpu.VMEM)
_SMEM = pl.BlockSpec(memory_space=pltpu.SMEM)
_HBM = pl.BlockSpec(memory_space=pltpu.HBM)


def stages(parts):
    rest = list(range(parts - 1, 1, -1))
    return [[0, 1], rest]


def regroup(buf):
    wide = buf[...].astype(jnp.float32)
    return [wide[:, group, :].astype(jnp.bfloat16) for group in range(buf.shape[1])]


def prep_kernel(parts, cot_ref, key_ref, value_ref, *rest):
    kv_outs, cot_outs, (key_buf, value_buf, sems) = rest[:4], rest[4 : parts + 4], rest[parts + 4 :]
    heads = cot_ref.shape[1] // parts
    me = lax.axis_index("kvh")
    loads = []
    for number, (ref, buf) in enumerate(((key_ref, key_buf), (value_ref, value_buf))):
        loads.append(pltpu.make_async_copy(ref, buf, sems.at[number]))
        loads[-1].start()
    copies = []
    for mask in range(parts):
        first = pl.multiple_of((me ^ mask) * heads, heads)
        copies.append(
            pltpu.make_async_copy(
                cot_ref.at[:, pl.ds(first, heads), :], cot_outs[mask], sems.at[mask + 2]
            )
        )
        copies[-1].start()
    for number, buf in enumerate((key_buf, value_buf)):
        loads[number].wait()
        for group, block in enumerate(regroup(buf)):
            for kv_out in kv_outs:
                kv_out[number, group] = block
    for copy in copies:
        copy.wait()


def prepare(cotangent, keys, values, parts):
    rows, heads, size = cotangent.shape
    kv_rows, kv_heads, _ = keys.shape
    piece = pltpu.VMEM((rows, heads // parts, size), jnp.bfloat16)
    block = pltpu.VMEM((2, kv_heads, kv_rows, size), jnp.bfloat16)
    operands = [
        pltpu.with_memory_space_constraint(array, pltpu.HBM)
        for array in (cotangent, keys, values)
    ]
    outs = pl.pallas_call(
        functools.partial(prep_kernel, parts),
        out_shape=(block,) * 4 + (piece,) * parts,
        in_specs=[_HBM] * 3,
        out_specs=(_VMEM,) * (parts + 4),
        scratch_shapes=[
            pltpu.VMEM(keys.shape, jnp.bfloat16),
            pltpu.VMEM(values.shape, jnp.bfloat16),
            pltpu.SemaphoreType.DMA((parts + 2,)),
        ],
        compiler_params=pltpu.CompilerParams(vmem_limit_bytes=VMEM_BYTES),
        name="prepare",
    )(*operands)
    return outs[:4], outs[4:]


def bounds(position, lengths, prefixes):
    docs = lengths.shape[0]

    def step(doc, carry):
        start, low, high = carry
        end = start + lengths[doc]
        inside = (position >= start) & (position < end)
        reach = jnp.minimum(end, jnp.maximum(position + 1, start + prefixes[doc]))
        return end, jnp.where(inside, start, low), jnp.where(inside, reach, high)

    zero = jnp.zeros_like(position)
    carry = (jnp.int32(0), zero, zero)
    if docs <= 16:
        for doc in range(docs):
            carry = step(doc, carry)
    else:
        carry = lax.fori_loop(0, docs, step, carry)
    return carry[1], carry[2]


def neighbour_slots(shard):
    odd = shard % 2
    ahead, behind = BACK + 1, BACK - 1
    return jnp.where(odd == 1, behind, ahead), jnp.where(odd == 1, ahead, behind)


def grad_kernel(masks, parts, is_first, is_last, lengths, prefixes, q_ref, *refs):
    refs = list(refs)
    kv_own, kv_even, kv_far, kv_odd = [refs.pop(0) for _ in range(4)]
    cots = {mask: refs.pop(0) for mask in masks}
    carried = None if is_first else refs.pop(0)
    dqs = {mask: refs.pop(0) for mask in masks}
    outs, (window, acc) = refs[:-2], refs[-2:]
    rows, heads, size = q_ref.shape
    tokens = rows // parts
    kv_heads = kv_own.shape[1]
    group_size = heads // kv_heads
    span = (BACK + 1 + AHEAD) * rows
    reach = span - rows + tokens
    lanes = tokens * group_size
    scale = size ** (-0.5)
    shard = lax.axis_index("seq")
    me = lax.axis_index("kvh")

    even_slot, odd_slot = neighbour_slots(shard)
    for slot, ref in ((BACK, kv_own), (0, kv_far), (even_slot, kv_even), (odd_slot, kv_odd)):
        part = pl.ds(pl.multiple_of(slot * rows, rows), rows)
        for number in range(2):
            for group in range(kv_heads):
                window[number, group, part] = ref[number, group]
    acc[...] = jnp.zeros_like(acc) if is_first else carried[...]

    contract_last = (((1,), (1,)), ((), ()))
    contract_first = (((0,), (0,)), ((), ()))
    lane_token = lax.broadcasted_iota(jnp.int32, (1, lanes), 1) // group_size
    key_iota = lax.broadcasted_iota(jnp.int32, (reach, lanes), 0)
    for mask in masks:
        first = pl.multiple_of((me ^ mask) * tokens, tokens)
        low, high = bounds(shard * rows + first + lane_token, lengths, prefixes)
        origin = (shard - BACK) * rows + first
        low = low - origin
        high = high - origin
        visible = (key_iota >= low) & (key_iota < high)
        here = pl.ds(first, reach)
        for group in range(kv_heads):
            of_group = pl.ds(group * group_size, group_size)
            q = q_ref[pl.ds(first, tokens), of_group].astype(jnp.float32)
            q = q.reshape(lanes, size).astype(jnp.bfloat16)
            cot = cots[mask][:, of_group].astype(jnp.float32)
            cot = cot.reshape(lanes, size).astype(jnp.bfloat16)
            k = window[0, group, here]
            v = window[1, group, here]
            scores = lax.dot_general(k, q, contract_last, preferred_element_type=jnp.float32)
            scores = jnp.where(visible, scores * (scale * LOG2E), NEG)
            top = jnp.max(scores, axis=0, keepdims=True)
            expo = jnp.exp2(scores - top)
            total = jnp.sum(expo, axis=0, keepdims=True)
            probs = expo * (1.0 / total)
            dprobs = lax.dot_general(v, cot, contract_last, preferred_element_type=jnp.float32)
            delta = jnp.sum(probs * dprobs, axis=0, keepdims=True)
            dscores = (probs * (dprobs - delta)).astype(jnp.bfloat16)
            acc[1, group, here] += jnp.dot(
                probs.astype(jnp.bfloat16), cot, preferred_element_type=jnp.float32
            )
            acc[0, group, here] += jnp.dot(dscores, q, preferred_element_type=jnp.float32)
            dq = lax.dot_general(k, dscores, contract_first, preferred_element_type=jnp.float32)
            dq = jnp.transpose(dq * scale)
            dqs[mask][:, of_group] = dq.reshape(tokens, group_size, size).astype(jnp.bfloat16)
    if not is_last:
        outs[0][...] = acc[...]
        return
    for slot, ref in zip((BACK, 0, even_slot, odd_slot), outs):
        part = pl.ds(pl.multiple_of(slot * rows, rows), rows)
        for group in range(kv_heads):
            ref[0, group] = (acc[0, group, part] * scale).astype(ref.dtype)
            ref[1, group] = acc[1, group, part].astype(ref.dtype)


def gradients(masks, parts, lengths, prefixes, queries, cots, blocks, carried):
    rows, heads, size = queries.shape
    is_last = masks == stages(parts)[-1]
    kv_shape = blocks[0].shape
    kv_heads = kv_shape[1]
    span = (BACK + 1 + AHEAD) * rows
    acc_shape = (2, kv_heads, span, size)
    work = heads * rows // parts * span * len(masks)
    outs = [pltpu.VMEM(cots[0].shape, jnp.bfloat16)] * len(masks)
    if is_last:
        outs += [pltpu.VMEM(kv_shape, jnp.float32)] + [pltpu.VMEM(kv_shape, jnp.bfloat16)] * 3
    else:
        outs += [pltpu.VMEM(acc_shape, jnp.float32)]
    operands = [queries, blocks[0], blocks[2], blocks[1], blocks[3], *cots] + ([] if carried is None else [carried])
    outs = pl.pallas_call(
        functools.partial(grad_kernel, masks, parts, carried is None, is_last),
        out_shape=tuple(outs),
        in_specs=[_SMEM, _SMEM] + [_VMEM] * len(operands),
        out_specs=(_VMEM,) * len(outs),
        scratch_shapes=[
            pltpu.VMEM(acc_shape, jnp.bfloat16),
            pltpu.VMEM(acc_shape, jnp.float32),
        ],
        compiler_params=pltpu.CompilerParams(vmem_limit_bytes=VMEM_BYTES),
        cost_estimate=pl.CostEstimate(
            flops=10 * work * size, bytes_accessed=4 * queries.size * 2, transcendentals=work
        ),
        name="gradients",
    )(lengths, prefixes, *operands)
    return outs[: len(masks)], outs[len(masks) :]


def finish_order(parts):
    return ["even", "far", parts - 1, "odd", *range(parts - 2, -1, -1), "own"]


def finish_kernel(parts, *refs):
    *refs, dq_out, dk_out, dv_out = refs
    refs = dict(zip(finish_order(parts), refs))
    dqs = [refs[mask] for mask in range(parts)]
    own, far, even, odd = [refs[name] for name in ("own", "far", "even", "odd")]
    heads = dqs[0].shape[1]
    me = lax.axis_index("kvh")
    for mask in range(parts):
        first = pl.multiple_of((me ^ mask) * heads, heads)
        dq_out[:, pl.ds(first, heads), :] = dqs[mask][...]
    for number, ref in enumerate((dk_out, dv_out)):
        sums = []
        for group in range(ref.shape[1]):
            total = own[number, group]
            for other in (far, even, odd):
                total = total + other[number, group].astype(jnp.float32)
            sums.append(total)
        ref[...] = jnp.stack(sums, axis=1).astype(jnp.bfloat16)


def finish(dqs, partials):
    parts = len(dqs)
    rows, heads, size = dqs[0].shape
    _, kv_heads, kv_rows, _ = partials[0].shape
    kv_out = jax.ShapeDtypeStruct((kv_rows, kv_heads, size), jnp.bfloat16)
    operands = dict(enumerate(dqs)) | dict(zip(("own", "far", "even", "odd"), partials))
    return pl.pallas_call(
        functools.partial(finish_kernel, parts),
        out_shape=(
            jax.ShapeDtypeStruct((rows, heads * parts, size), jnp.bfloat16),
            kv_out,
            kv_out,
        ),
        in_specs=[_VMEM] * (parts + 4),
        out_specs=(_VMEM,) * 3,
        compiler_params=pltpu.CompilerParams(vmem_limit_bytes=VMEM_BYTES),
        name="finish",
    )(*[operands[name] for name in finish_order(parts)])


def shifted(block, distance):
    count = lax.axis_size("seq")
    return lax.ppermute(block, "seq", [(i, (i + distance) % count) for i in range(count)])


def paired(block, first):
    count = lax.axis_size("seq")
    route = []
    for i in range(count):
        partner = i + 1 if i % 2 == first else i - 1
        route.append((i, partner if 0 <= partner < count else i))
    return lax.ppermute(block, "seq", route)


def swapped(block, mask):
    return lax.ppermute(block, "kvh", [(i, i ^ mask) for i in range(lax.axis_size("kvh"))])


def neighbours(far, even, odd, distance):
    return [shifted(far, distance), paired(even, 0), paired(odd, 1)]


def local(queries, keys, values, output_gradient, doc_lengths, prefix_lengths):
    parts = lax.axis_size("kvh")
    kv, cots = prepare(output_gradient, keys, values, parts)
    blocks = [kv[0]] + neighbours(*kv[1:], BACK)
    cots = [cots[0]] + [swapped(cots[mask], mask) for mask in range(1, parts)]
    dqs, carried = {}, [None]
    for masks in stages(parts):
        found, carried = gradients(
            masks, parts, doc_lengths, prefix_lengths, queries,
            [cots[mask] for mask in masks], blocks, carried[0],
        )
        for mask, dq in zip(masks, found):
            dqs[mask] = swapped(dq, mask) if mask else dq
    partials = [carried[0]] + neighbours(*carried[1:], -BACK)
    return finish([dqs[mask] for mask in range(parts)], partials)


def solution(mesh):
    in_specs = (
        P("seq", "kvh", None),
        P("seq", "kvh", None),
        P("seq", "kvh", None),
        P(("seq", "kvh"), None, None),
        P(),
        P(),
    )
    out_specs = (P(("seq", "kvh"), None, None), P("seq", "kvh", None), P("seq", "kvh", None))
    return jax.shard_map(local, mesh=mesh, in_specs=in_specs, out_specs=out_specs, check_vma=False)
```

```python
import functools

import jax
import jax.numpy as jnp
from jax import lax
from jax.experimental import pallas as pl
from jax.experimental.pallas import tpu as pltpu
from jax.sharding import PartitionSpec as P

BACK = 2
AHEAD = 1
LOG2E = 1.4426950408889634
VMEM_BYTES = 40 * 1024 * 1024
NEG = -1e30

_VMEM = pl.BlockSpec(memory_space=pltpu.VMEM)
_SMEM = pl.BlockSpec(memory_space=pltpu.SMEM)
_HBM = pl.BlockSpec(memory_space=pltpu.HBM)


def stages(parts):
    rest = list(range(parts - 1, 1, -1))
    return [[0, 1], rest]


def regroup(buf):
    wide = buf[...].astype(jnp.float32)
    return [wide[:, group, :].astype(jnp.bfloat16) for group in range(buf.shape[1])]


def prep_kernel(parts, lengths_ref, prefixes_ref, cot_ref, key_ref, value_ref, *rest):
    kv_outs, cot_outs, rest = rest[:4], rest[4 : parts + 4], rest[parts + 4 :]
    range_out, key_buf, value_buf, lengths, prefixes, sems, scalar_sems = rest
    heads = cot_ref.shape[1] // parts
    me = lax.axis_index("kvh")
    scalars = [
        pltpu.make_async_copy(lengths_ref, lengths, scalar_sems.at[0]),
        pltpu.make_async_copy(prefixes_ref, prefixes, scalar_sems.at[1]),
    ]
    for copy in scalars:
        copy.start()
    loads = []
    for number, (ref, buf) in enumerate(((key_ref, key_buf), (value_ref, value_buf))):
        loads.append(pltpu.make_async_copy(ref, buf, sems.at[number]))
        loads[-1].start()
    copies = []
    for mask in range(parts):
        first = pl.multiple_of((me ^ mask) * heads, heads)
        copies.append(
            pltpu.make_async_copy(
                cot_ref.at[:, pl.ds(first, heads), :], cot_outs[mask], sems.at[mask + 2]
            )
        )
        copies[-1].start()
    for number, buf in enumerate((key_buf, value_buf)):
        loads[number].wait()
        for group, block in enumerate(regroup(buf)):
            for kv_out in kv_outs:
                kv_out[number, group] = block
    for copy in scalars:
        copy.wait()
    rows = key_buf.shape[0]
    tokens = rows // parts
    lanes = range_out.shape[2]
    lane_token = lax.broadcasted_iota(jnp.int32, (1, lanes), 1) // (lanes // tokens)
    shard = lax.axis_index("seq")
    for mask in range(parts):
        first = (me ^ mask) * tokens
        low, high = bounds(shard * rows + first + lane_token, lengths, prefixes)
        origin = (shard - BACK) * rows + first
        range_out[mask, 0:1, :] = low - origin
        range_out[mask, 1:2, :] = high - origin
    for copy in copies:
        copy.wait()


def prepare(lengths, prefixes, cotangent, keys, values, parts):
    rows, heads, size = cotangent.shape
    kv_rows, kv_heads, _ = keys.shape
    lanes = kv_rows // parts * (heads // parts // kv_heads)
    piece = pltpu.VMEM((rows, heads // parts, size), jnp.bfloat16)
    block = pltpu.VMEM((2, kv_heads, kv_rows, size), jnp.bfloat16)
    operands = [
        pltpu.with_memory_space_constraint(array, pltpu.HBM)
        for array in (lengths, prefixes, cotangent, keys, values)
    ]
    outs = pl.pallas_call(
        functools.partial(prep_kernel, parts),
        out_shape=(block,) * 4 + (piece,) * parts + (pltpu.VMEM((parts, 2, lanes), jnp.int32),),
        in_specs=[_HBM] * 5,
        out_specs=(_VMEM,) * (parts + 5),
        scratch_shapes=[
            pltpu.VMEM(keys.shape, jnp.bfloat16),
            pltpu.VMEM(values.shape, jnp.bfloat16),
            pltpu.SMEM(lengths.shape, jnp.int32),
            pltpu.SMEM(prefixes.shape, jnp.int32),
            pltpu.SemaphoreType.DMA((parts + 2,)),
            pltpu.SemaphoreType.DMA((2,)),
        ],
        compiler_params=pltpu.CompilerParams(vmem_limit_bytes=VMEM_BYTES),
        name="prepare",
    )(*operands)
    return outs[:4], outs[4:-1], outs[-1]


def bounds(position, lengths, prefixes):
    docs = lengths.shape[0]

    def step(doc, carry):
        start, low, high = carry
        end = start + lengths[doc]
        inside = (position >= start) & (position < end)
        reach = jnp.minimum(end, jnp.maximum(position + 1, start + prefixes[doc]))
        return end, jnp.where(inside, start, low), jnp.where(inside, reach, high)

    zero = jnp.zeros_like(position)
    carry = (jnp.int32(0), zero, zero)
    if docs <= 16:
        for doc in range(docs):
            carry = step(doc, carry)
    else:
        carry = lax.fori_loop(0, docs, step, carry)
    return carry[1], carry[2]


def neighbour_slots(shard):
    odd = shard % 2
    ahead, behind = BACK + 1, BACK - 1
    return jnp.where(odd == 1, behind, ahead), jnp.where(odd == 1, ahead, behind)


def grad_kernel(masks, parts, is_first, is_last, range_ref, q_ref, *refs):
    refs = list(refs)
    kv_own, kv_even, kv_far, kv_odd = [refs.pop(0) for _ in range(4)]
    cots = [refs.pop(0) for _ in masks]
    carried = None if is_first else refs.pop(0)
    dqs = [refs.pop(0) for _ in masks]
    outs, (window, acc, q_rows, cot_rows, dq_rows) = refs[:-5], refs[-5:]
    rows, heads, size = q_ref.shape
    tokens = rows // parts
    kv_heads = kv_own.shape[1]
    group_size = heads // kv_heads
    span = (BACK + 1 + AHEAD) * rows
    reach = span - rows + tokens
    lanes = tokens * group_size
    scale = size ** (-0.5)
    shard = lax.axis_index("seq")
    me = lax.axis_index("kvh")

    even_slot, odd_slot = neighbour_slots(shard)
    for slot, ref in ((BACK, kv_own), (0, kv_far), (even_slot, kv_even), (odd_slot, kv_odd)):
        part = pl.ds(pl.multiple_of(slot * rows, rows), rows)
        for number in range(2):
            for group in range(kv_heads):
                window[number, group, part] = ref[number, group]
    acc[...] = jnp.zeros_like(acc) if is_first else carried[...]
    for place, mask in enumerate(masks):
        first = pl.multiple_of((me ^ mask) * tokens, tokens)
        for group in range(kv_heads):
            of_group = pl.ds(group * group_size, group_size)
            item = place * kv_heads + group
            q = q_ref[pl.ds(first, tokens), of_group].astype(jnp.float32)
            q_rows[item] = q.reshape(lanes, size).astype(jnp.bfloat16)
            cot = cots[place][:, of_group].astype(jnp.float32)
            cot_rows[item] = cot.reshape(lanes, size).astype(jnp.bfloat16)

    contract_last = (((1,), (1,)), ((), ()))
    contract_first = (((0,), (0,)), ((), ()))
    key_iota = lax.broadcasted_iota(jnp.int32, (reach, lanes), 0)
    step = masks[1] - masks[0] if len(masks) > 1 else 0

    def work(item, _):
        group = lax.rem(item, kv_heads)
        mask = masks[0] + step * lax.div(item, kv_heads)
        here = pl.ds(pl.multiple_of((me ^ mask) * tokens, tokens), reach)
        low, high = range_ref[mask, 0:1, :], range_ref[mask, 1:2, :]
        visible = (key_iota >= low) & (key_iota < high)
        q, cot = q_rows[item], cot_rows[item]
        k, v = window[0, group, here], window[1, group, here]
        scores = lax.dot_general(k, q, contract_last, preferred_element_type=jnp.float32)
        scores = jnp.where(visible, scores * (scale * LOG2E), NEG)
        top = jnp.max(scores, axis=0, keepdims=True)
        expo = jnp.exp2(scores - top)
        total = jnp.sum(expo, axis=0, keepdims=True)
        probs = expo * (1.0 / total)
        dprobs = lax.dot_general(v, cot, contract_last, preferred_element_type=jnp.float32)
        delta = jnp.sum(probs * dprobs, axis=0, keepdims=True)
        dscores = (probs * (dprobs - delta)).astype(jnp.bfloat16)
        acc[1, group, here] += jnp.dot(
            probs.astype(jnp.bfloat16), cot, preferred_element_type=jnp.float32
        )
        acc[0, group, here] += jnp.dot(dscores, q, preferred_element_type=jnp.float32)
        dq = lax.dot_general(k, dscores, contract_first, preferred_element_type=jnp.float32)
        dq_rows[item] = jnp.transpose(dq * scale)
        return 0

    lax.fori_loop(0, len(masks) * kv_heads, work, 0)
    for place in range(len(masks)):
        for group in range(kv_heads):
            dq = dq_rows[place * kv_heads + group].reshape(tokens, group_size, size)
            dqs[place][:, pl.ds(group * group_size, group_size)] = dq.astype(jnp.bfloat16)
    if not is_last:
        outs[0][...] = acc[...]
        return
    for slot, ref in zip((BACK, 0, even_slot, odd_slot), outs):
        part = pl.ds(pl.multiple_of(slot * rows, rows), rows)
        for group in range(kv_heads):
            ref[0, group] = (acc[0, group, part] * scale).astype(ref.dtype)
            ref[1, group] = acc[1, group, part].astype(ref.dtype)


def gradients(masks, parts, ranges, queries, cots, blocks, carried):
    rows, heads, size = queries.shape
    is_last = masks == stages(parts)[-1]
    kv_shape = blocks[0].shape
    kv_heads = kv_shape[1]
    span = (BACK + 1 + AHEAD) * rows
    acc_shape = (2, kv_heads, span, size)
    row_shape = (len(masks) * kv_heads, rows // parts * (heads // kv_heads), size)
    work = heads * rows // parts * span * len(masks)
    outs = [pltpu.VMEM(cots[0].shape, jnp.bfloat16)] * len(masks)
    if is_last:
        outs += [pltpu.VMEM(kv_shape, jnp.float32)] + [pltpu.VMEM(kv_shape, jnp.bfloat16)] * 3
    else:
        outs += [pltpu.VMEM(acc_shape, jnp.float32)]
    own, far, even, odd = blocks
    operands = [ranges, queries, own, even, far, odd, *cots]
    operands += [] if carried is None else [carried]
    outs = pl.pallas_call(
        functools.partial(grad_kernel, masks, parts, carried is None, is_last),
        out_shape=tuple(outs),
        in_specs=[_VMEM] * len(operands),
        out_specs=(_VMEM,) * len(outs),
        scratch_shapes=[
            pltpu.VMEM(acc_shape, jnp.bfloat16),
            pltpu.VMEM(acc_shape, jnp.float32),
            pltpu.VMEM(row_shape, jnp.bfloat16),
            pltpu.VMEM(row_shape, jnp.bfloat16),
            pltpu.VMEM(row_shape, jnp.float32),
        ],
        compiler_params=pltpu.CompilerParams(vmem_limit_bytes=VMEM_BYTES),
        cost_estimate=pl.CostEstimate(
            flops=10 * work * size, bytes_accessed=4 * queries.size * 2, transcendentals=work
        ),
        name="gradients",
    )(*operands)
    return outs[: len(masks)], outs[len(masks) :]


def finish_order(parts):
    return ["even", "far", parts - 1, "odd", *range(parts - 2, -1, -1), "own"]


def finish_kernel(parts, *refs):
    *refs, dq_out, dk_out, dv_out = refs
    refs = dict(zip(finish_order(parts), refs))
    dqs = [refs[mask] for mask in range(parts)]
    own, far, even, odd = [refs[name] for name in ("own", "far", "even", "odd")]
    heads = dqs[0].shape[1]
    me = lax.axis_index("kvh")
    for mask in range(parts):
        first = pl.multiple_of((me ^ mask) * heads, heads)
        dq_out[:, pl.ds(first, heads), :] = dqs[mask][...]
    for number, ref in enumerate((dk_out, dv_out)):
        sums = []
        for group in range(ref.shape[1]):
            total = own[number, group]
            for other in (far, even, odd):
                total = total + other[number, group].astype(jnp.float32)
            sums.append(total)
        ref[...] = jnp.stack(sums, axis=1).astype(jnp.bfloat16)


def finish(dqs, partials):
    parts = len(dqs)
    rows, heads, size = dqs[0].shape
    _, kv_heads, kv_rows, _ = partials[0].shape
    kv_out = jax.ShapeDtypeStruct((kv_rows, kv_heads, size), jnp.bfloat16)
    operands = dict(enumerate(dqs)) | dict(zip(("own", "far", "even", "odd"), partials))
    return pl.pallas_call(
        functools.partial(finish_kernel, parts),
        out_shape=(
            jax.ShapeDtypeStruct((rows, heads * parts, size), jnp.bfloat16),
            kv_out,
            kv_out,
        ),
        in_specs=[_VMEM] * (parts + 4),
        out_specs=(_VMEM,) * 3,
        compiler_params=pltpu.CompilerParams(vmem_limit_bytes=VMEM_BYTES),
        name="finish",
    )(*[operands[name] for name in finish_order(parts)])


def shifted(block, distance):
    count = lax.axis_size("seq")
    return lax.ppermute(block, "seq", [(i, (i + distance) % count) for i in range(count)])


def paired(block, first):
    count = lax.axis_size("seq")
    route = []
    for i in range(count):
        partner = i + 1 if i % 2 == first else i - 1
        route.append((i, partner if 0 <= partner < count else i))
    return lax.ppermute(block, "seq", route)


def swapped(block, mask):
    return lax.ppermute(block, "kvh", [(i, i ^ mask) for i in range(lax.axis_size("kvh"))])


def neighbours(far, even, odd, distance):
    return [shifted(far, distance), paired(even, 0), paired(odd, 1)]


def local(queries, keys, values, output_gradient, doc_lengths, prefix_lengths):
    parts = lax.axis_size("kvh")
    kv, cots, ranges = prepare(
        doc_lengths, prefix_lengths, output_gradient, keys, values, parts
    )
    blocks = [kv[0]] + neighbours(*kv[1:], BACK)
    cots = [cots[0]] + [swapped(cots[mask], mask) for mask in range(1, parts)]
    dqs, carried = {}, [None]
    for masks in stages(parts):
        found, carried = gradients(
            masks, parts, ranges, queries, [cots[mask] for mask in masks], blocks, carried[0]
        )
        for mask, dq in zip(masks, found):
            dqs[mask] = swapped(dq, mask) if mask else dq
    partials = [carried[0]] + neighbours(*carried[1:], -BACK)
    return finish([dqs[mask] for mask in range(parts)], partials)


def solution(mesh):
    in_specs = (
        P("seq", "kvh", None),
        P("seq", "kvh", None),
        P("seq", "kvh", None),
        P(("seq", "kvh"), None, None),
        P(),
        P(),
    )
    out_specs = (P(("seq", "kvh"), None, None), P("seq", "kvh", None), P("seq", "kvh", None))
    return jax.shard_map(local, mesh=mesh, in_specs=in_specs, out_specs=out_specs, check_vma=False)
```

```python
import functools

import jax
import jax.numpy as jnp
from jax import lax
from jax.experimental import pallas as pl
from jax.experimental.pallas import tpu as pltpu
from jax.sharding import PartitionSpec as P

BACK = 2
AHEAD = 1
LOG2E = 1.4426950408889634
VMEM_BYTES = 40 * 1024 * 1024
NEG = -1e30
TILE = 8

_VMEM = pl.BlockSpec(memory_space=pltpu.VMEM)
_SMEM = pl.BlockSpec(memory_space=pltpu.SMEM)
_HBM = pl.BlockSpec(memory_space=pltpu.HBM)


def stages(parts):
    rest = list(range(parts - 1, 1, -1))
    return [[0, 1], rest]


def regroup(buf):
    wide = buf[...].astype(jnp.float32)
    return [wide[:, group, :].astype(jnp.bfloat16) for group in range(buf.shape[1])]


def prep_kernel(parts, lengths_ref, prefixes_ref, cot_ref, key_ref, value_ref, *rest):
    kv_outs, cot_outs, rest = rest[:4], rest[4 : parts + 4], rest[parts + 4 :]
    range_out, key_buf, value_buf, lengths, prefixes, sems, scalar_sems = rest
    heads = cot_ref.shape[1] // parts
    me = lax.axis_index("kvh")
    scalars = [
        pltpu.make_async_copy(lengths_ref, lengths, scalar_sems.at[0]),
        pltpu.make_async_copy(prefixes_ref, prefixes, scalar_sems.at[1]),
    ]
    for copy in scalars:
        copy.start()
    loads = []
    for number, (ref, buf) in enumerate(((key_ref, key_buf), (value_ref, value_buf))):
        loads.append(pltpu.make_async_copy(ref, buf, sems.at[number]))
        loads[-1].start()
    copies = []
    for mask in range(parts):
        first = pl.multiple_of((me ^ mask) * heads, heads)
        copies.append(
            pltpu.make_async_copy(
                cot_ref.at[:, pl.ds(first, heads), :], cot_outs[mask], sems.at[mask + 2]
            )
        )
        copies[-1].start()
    for number, buf in enumerate((key_buf, value_buf)):
        loads[number].wait()
        for group, block in enumerate(regroup(buf)):
            for kv_out in kv_outs:
                kv_out[number, group] = block
    for copy in scalars:
        copy.wait()
    rows = key_buf.shape[0]
    tokens = rows // parts
    lanes = range_out.shape[2]
    lane_token = lax.broadcasted_iota(jnp.int32, (1, lanes), 1) // (lanes // tokens)
    shard = lax.axis_index("seq")
    for mask in range(parts):
        first = (me ^ mask) * tokens
        low, high = bounds(shard * rows + first + lane_token, lengths, prefixes)
        origin = (shard - BACK) * rows + first
        range_out[mask, 0:1, :] = low - origin
        range_out[mask, 1:2, :] = high - origin
    for copy in copies:
        copy.wait()


def prepare(lengths, prefixes, cotangent, keys, values, parts):
    rows, heads, size = cotangent.shape
    kv_rows, kv_heads, _ = keys.shape
    lanes = kv_rows // parts * (heads // parts // kv_heads)
    piece = pltpu.VMEM((rows, heads // parts, size), jnp.bfloat16)
    block = pltpu.VMEM((2, kv_heads, kv_rows, size), jnp.bfloat16)
    operands = [
        pltpu.with_memory_space_constraint(array, pltpu.HBM)
        for array in (lengths, prefixes, cotangent, keys, values)
    ]
    outs = pl.pallas_call(
        functools.partial(prep_kernel, parts),
        out_shape=(block,) * 4 + (piece,) * parts + (pltpu.VMEM((parts, 2, lanes), jnp.int32),),
        in_specs=[_HBM] * 5,
        out_specs=(_VMEM,) * (parts + 5),
        scratch_shapes=[
            pltpu.VMEM(keys.shape, jnp.bfloat16),
            pltpu.VMEM(values.shape, jnp.bfloat16),
            pltpu.SMEM(lengths.shape, jnp.int32),
            pltpu.SMEM(prefixes.shape, jnp.int32),
            pltpu.SemaphoreType.DMA((parts + 2,)),
            pltpu.SemaphoreType.DMA((2,)),
        ],
        compiler_params=pltpu.CompilerParams(vmem_limit_bytes=VMEM_BYTES),
        name="prepare",
    )(*operands)
    return outs[:4], outs[4:-1], outs[-1]


def bounds(position, lengths, prefixes):
    docs = lengths.shape[0]

    def step(doc, carry):
        start, low, high = carry
        end = start + lengths[doc]
        inside = (position >= start) & (position < end)
        reach = jnp.minimum(end, jnp.maximum(position + 1, start + prefixes[doc]))
        return end, jnp.where(inside, start, low), jnp.where(inside, reach, high)

    zero = jnp.zeros_like(position)
    carry = (jnp.int32(0), zero, zero)
    if docs <= 16:
        for doc in range(docs):
            carry = step(doc, carry)
    else:
        carry = lax.fori_loop(0, docs, step, carry)
    return carry[1], carry[2]


def neighbour_slots(shard):
    odd = shard % 2
    ahead, behind = BACK + 1, BACK - 1
    return jnp.where(odd == 1, behind, ahead), jnp.where(odd == 1, ahead, behind)


def grad_kernel(masks, parts, is_first, is_last, range_ref, q_ref, *refs):
    refs = list(refs)
    kv_own, kv_odd, kv_even, kv_far = [refs.pop(0) for _ in range(4)]
    cots = [refs.pop(0) for _ in masks]
    carried = None if is_first else refs.pop(0)
    dqs = [refs.pop(0) for _ in masks]
    outs, (window, acc, score_buf, dprob_buf, prob_buf, dscore_buf) = refs[:-6], refs[-6:]
    rows, heads, size = q_ref.shape
    tokens = rows // parts
    kv_heads = kv_own.shape[1]
    group_size = heads // kv_heads
    span = (BACK + 1 + AHEAD) * rows
    reach = span - rows + tokens
    lanes = tokens * group_size
    scale = size ** (-0.5)
    shard = lax.axis_index("seq")
    me = lax.axis_index("kvh")

    even_slot, odd_slot = neighbour_slots(shard)
    for slot, ref in ((BACK, kv_own), (0, kv_far), (even_slot, kv_even), (odd_slot, kv_odd)):
        part = pl.ds(pl.multiple_of(slot * rows, rows), rows)
        for number in range(2):
            for group in range(kv_heads):
                window[number, group, part] = ref[number, group]
    acc[...] = jnp.zeros_like(acc) if is_first else carried[...]

    contract_last = (((1,), (1,)), ((), ()))
    contract_first = (((0,), (0,)), ((), ()))
    sublane = lax.broadcasted_iota(jnp.int32, (TILE, lanes), 0)
    items = [(place, group) for place in range(len(masks)) for group in range(kv_heads)]

    def operands(item):
        place, group = items[item]
        first = pl.multiple_of((me ^ masks[place]) * tokens, tokens)
        of_group = pl.ds(group * group_size, group_size)
        q = q_ref[pl.ds(first, tokens), of_group].astype(jnp.float32)
        cot = cots[place][:, of_group].astype(jnp.float32)
        return (
            pl.ds(first, reach),
            q.reshape(lanes, size).astype(jnp.bfloat16),
            cot.reshape(lanes, size).astype(jnp.bfloat16),
        )

    def scores_of(item):
        place, group = items[item]
        slot = item % 2
        here, q, cot = operands(item)
        scores = lax.dot_general(
            window[0, group, here], q, contract_last, preferred_element_type=jnp.float32
        )
        low = range_ref[masks[place], 0:1, :] - sublane
        high = range_ref[masks[place], 1:2, :] - sublane
        top = jnp.full((TILE, lanes), NEG, jnp.float32)
        for row in range(0, reach, TILE):
            visible = (low <= row) & (high > row)
            tile = jnp.where(visible, scores[row : row + TILE] * (scale * LOG2E), NEG)
            top = jnp.maximum(top, tile)
            score_buf[slot, row : row + TILE] = tile
        dprob_buf[slot] = lax.dot_general(
            window[1, group, here], cot, contract_last, preferred_element_type=jnp.float32
        )
        return jnp.max(top, axis=0, keepdims=True)

    def softmax_of(item, top):
        slot = item % 2
        total = jnp.zeros((TILE, lanes), jnp.float32)
        delta = jnp.zeros((TILE, lanes), jnp.float32)
        for row in range(0, reach, TILE):
            tile = slice(row, row + TILE)
            expo = jnp.exp2(score_buf[slot, tile] - top)
            total = total + expo
            delta = delta + expo * dprob_buf[slot, tile]
            score_buf[slot, tile] = expo
        inverse = 1.0 / jnp.sum(total, axis=0, keepdims=True)
        delta = jnp.sum(delta, axis=0, keepdims=True) * inverse
        for row in range(0, reach, 2 * TILE):
            tile = slice(row, row + 2 * TILE)
            probs = score_buf[slot, tile] * inverse
            dscores = probs * (dprob_buf[slot, tile] - delta)
            prob_buf[slot, tile] = probs.astype(jnp.bfloat16)
            dscore_buf[slot, tile] = dscores.astype(jnp.bfloat16)

    def gradients_of(item):
        place, group = items[item]
        slot = item % 2
        here, q, cot = operands(item)
        dscores = dscore_buf[slot]
        acc[1, group, here] += jnp.dot(prob_buf[slot], cot, preferred_element_type=jnp.float32)
        acc[0, group, here] += jnp.dot(dscores, q, preferred_element_type=jnp.float32)
        dq = lax.dot_general(
            window[0, group, here], dscores, contract_first, preferred_element_type=jnp.float32
        )
        dq = jnp.transpose(dq * scale).reshape(tokens, group_size, size)
        dqs[place][:, pl.ds(group * group_size, group_size)] = dq.astype(jnp.bfloat16)

    top = scores_of(0)
    for item in range(len(items)):
        later = scores_of(item + 1) if item + 1 < len(items) else None
        softmax_of(item, top)
        gradients_of(item)
        top = later

    if not is_last:
        outs[0][...] = acc[...]
        return
    for slot, ref in zip((BACK, 0, even_slot, odd_slot), outs):
        part = pl.ds(pl.multiple_of(slot * rows, rows), rows)
        for group in range(kv_heads):
            ref[0, group] = (acc[0, group, part] * scale).astype(ref.dtype)
            ref[1, group] = acc[1, group, part].astype(ref.dtype)


def gradients(masks, parts, ranges, queries, cots, blocks, carried):
    rows, heads, size = queries.shape
    is_last = masks == stages(parts)[-1]
    kv_shape = blocks[0].shape
    kv_heads = kv_shape[1]
    span = (BACK + 1 + AHEAD) * rows
    acc_shape = (2, kv_heads, span, size)
    tokens = rows // parts
    tile_shape = (2, span - rows + tokens, tokens * (heads // kv_heads))
    work = heads * rows // parts * span * len(masks)
    outs = [pltpu.VMEM(cots[0].shape, jnp.bfloat16)] * len(masks)
    if is_last:
        outs += [pltpu.VMEM(kv_shape, jnp.float32)] + [pltpu.VMEM(kv_shape, jnp.bfloat16)] * 3
    else:
        outs += [pltpu.VMEM(acc_shape, jnp.float32)]
    own, far, even, odd = blocks
    operands = [ranges, queries, own, odd, even, far, *cots]
    operands += [] if carried is None else [carried]
    outs = pl.pallas_call(
        functools.partial(grad_kernel, masks, parts, carried is None, is_last),
        out_shape=tuple(outs),
        in_specs=[_VMEM] * len(operands),
        out_specs=(_VMEM,) * len(outs),
        scratch_shapes=[
            pltpu.VMEM(acc_shape, jnp.bfloat16),
            pltpu.VMEM(acc_shape, jnp.float32),
            pltpu.VMEM(tile_shape, jnp.float32),
            pltpu.VMEM(tile_shape, jnp.float32),
            pltpu.VMEM(tile_shape, jnp.bfloat16),
            pltpu.VMEM(tile_shape, jnp.bfloat16),
        ],
        compiler_params=pltpu.CompilerParams(vmem_limit_bytes=VMEM_BYTES),
        cost_estimate=pl.CostEstimate(
            flops=10 * work * size, bytes_accessed=4 * queries.size * 2, transcendentals=work
        ),
        name="gradients",
    )(*operands)
    return outs[: len(masks)], outs[len(masks) :]


def finish_order(parts):
    return ["odd", parts - 1, "even", "far", *range(parts - 2, -1, -1), "own"]


def finish_kernel(parts, *refs):
    *refs, dq_out, dk_out, dv_out = refs
    refs = dict(zip(finish_order(parts), refs))
    dqs = [refs[mask] for mask in range(parts)]
    own, far, even, odd = [refs[name] for name in ("own", "far", "even", "odd")]
    heads = dqs[0].shape[1]
    me = lax.axis_index("kvh")
    for mask in range(parts):
        first = pl.multiple_of((me ^ mask) * heads, heads)
        dq_out[:, pl.ds(first, heads), :] = dqs[mask][...]
    for number, ref in enumerate((dk_out, dv_out)):
        sums = []
        for group in range(ref.shape[1]):
            total = own[number, group]
            for other in (far, even, odd):
                total = total + other[number, group].astype(jnp.float32)
            sums.append(total)
        ref[...] = jnp.stack(sums, axis=1).astype(jnp.bfloat16)


def finish(dqs, partials):
    parts = len(dqs)
    rows, heads, size = dqs[0].shape
    _, kv_heads, kv_rows, _ = partials[0].shape
    kv_out = jax.ShapeDtypeStruct((kv_rows, kv_heads, size), jnp.bfloat16)
    operands = dict(enumerate(dqs)) | dict(zip(("own", "far", "even", "odd"), partials))
    return pl.pallas_call(
        functools.partial(finish_kernel, parts),
        out_shape=(
            jax.ShapeDtypeStruct((rows, heads * parts, size), jnp.bfloat16),
            kv_out,
            kv_out,
        ),
        in_specs=[_VMEM] * (parts + 4),
        out_specs=(_VMEM,) * 3,
        compiler_params=pltpu.CompilerParams(vmem_limit_bytes=VMEM_BYTES),
        name="finish",
    )(*[operands[name] for name in finish_order(parts)])


def shifted(block, distance):
    count = lax.axis_size("seq")
    return lax.ppermute(block, "seq", [(i, (i + distance) % count) for i in range(count)])


def paired(block, first):
    count = lax.axis_size("seq")
    route = []
    for i in range(count):
        partner = i + 1 if i % 2 == first else i - 1
        route.append((i, partner if 0 <= partner < count else i))
    return lax.ppermute(block, "seq", route)


def swapped(block, mask):
    return lax.ppermute(block, "kvh", [(i, i ^ mask) for i in range(lax.axis_size("kvh"))])


def neighbours(far, even, odd, distance):
    return [shifted(far, distance), paired(even, 0), paired(odd, 1)]


def local(queries, keys, values, output_gradient, doc_lengths, prefix_lengths):
    parts = lax.axis_size("kvh")
    kv, cots, ranges = prepare(
        doc_lengths, prefix_lengths, output_gradient, keys, values, parts
    )
    blocks = [kv[0]] + neighbours(*kv[1:], BACK)
    cots = [cots[0]] + [swapped(cots[mask], mask) for mask in range(1, parts)]
    dqs, carried = {}, [None]
    for masks in stages(parts):
        found, carried = gradients(
            masks, parts, ranges, queries, [cots[mask] for mask in masks], blocks, carried[0]
        )
        for mask, dq in zip(masks, found):
            dqs[mask] = swapped(dq, mask) if mask else dq
    partials = [carried[0]] + neighbours(*carried[1:], -BACK)
    return finish([dqs[mask] for mask in range(parts)], partials)


def solution(mesh):
    in_specs = (
        P("seq", "kvh", None),
        P("seq", "kvh", None),
        P("seq", "kvh", None),
        P(("seq", "kvh"), None, None),
        P(),
        P(),
    )
    out_specs = (P(("seq", "kvh"), None, None), P("seq", "kvh", None), P("seq", "kvh", None))
    return jax.shard_map(local, mesh=mesh, in_specs=in_specs, out_specs=out_specs, check_vma=False)
```

```python
import functools

import jax
import jax.numpy as jnp
from jax import lax
from jax.experimental import pallas as pl
from jax.experimental.pallas import tpu as pltpu
from jax.sharding import PartitionSpec as P

BACK = 2
AHEAD = 1
LOG2E = 1.4426950408889634
VMEM_BYTES = 40 * 1024 * 1024
NEG = -1e30
TILE = 8

_VMEM = pl.BlockSpec(memory_space=pltpu.VMEM)
_SMEM = pl.BlockSpec(memory_space=pltpu.SMEM)
_HBM = pl.BlockSpec(memory_space=pltpu.HBM)


def stages(parts):
    rest = list(range(parts - 1, 1, -1))
    return [[0, 1, *rest[:-1]], rest[-1:]]


def regroup(buf):
    wide = buf[...].astype(jnp.float32)
    return [wide[:, group, :].astype(jnp.bfloat16) for group in range(buf.shape[1])]


def prep_kernel(parts, lengths_ref, prefixes_ref, cot_ref, key_ref, value_ref, *rest):
    kv_outs, cot_outs, rest = rest[:3], rest[3 : parts + 3], rest[parts + 3 :]
    range_out, key_buf, value_buf, lengths, prefixes, sems, scalar_sems = rest
    heads = cot_ref.shape[1] // parts
    me = lax.axis_index("kvh")
    scalars = [
        pltpu.make_async_copy(lengths_ref, lengths, scalar_sems.at[0]),
        pltpu.make_async_copy(prefixes_ref, prefixes, scalar_sems.at[1]),
    ]
    for copy in scalars:
        copy.start()
    loads = []
    for number, (ref, buf) in enumerate(((key_ref, key_buf), (value_ref, value_buf))):
        loads.append(pltpu.make_async_copy(ref, buf, sems.at[number]))
        loads[-1].start()
    copies = []
    for mask in range(parts):
        first = pl.multiple_of((me ^ mask) * heads, heads)
        copies.append(
            pltpu.make_async_copy(
                cot_ref.at[:, pl.ds(first, heads), :], cot_outs[mask], sems.at[mask + 2]
            )
        )
        copies[-1].start()
    for number, buf in enumerate((key_buf, value_buf)):
        loads[number].wait()
        for group, block in enumerate(regroup(buf)):
            for kv_out in kv_outs:
                kv_out[number, group] = block
    for copy in scalars:
        copy.wait()
    rows = key_buf.shape[0]
    tokens = rows // parts
    lanes = range_out.shape[2]
    lane_token = lax.broadcasted_iota(jnp.int32, (1, lanes), 1) // (lanes // tokens)
    shard = lax.axis_index("seq")
    for mask in range(parts):
        first = (me ^ mask) * tokens
        low, high = bounds(shard * rows + first + lane_token, lengths, prefixes)
        origin = (shard - BACK) * rows + first
        range_out[mask, 0:1, :] = low - origin
        range_out[mask, 1:2, :] = high - origin
    for copy in copies:
        copy.wait()


def prepare(lengths, prefixes, cotangent, keys, values, parts):
    rows, heads, size = cotangent.shape
    kv_rows, kv_heads, _ = keys.shape
    lanes = kv_rows // parts * (heads // parts // kv_heads)
    piece = pltpu.VMEM((rows, heads // parts, size), jnp.bfloat16)
    block = pltpu.VMEM((2, kv_heads, kv_rows, size), jnp.bfloat16)
    operands = [
        pltpu.with_memory_space_constraint(array, pltpu.HBM)
        for array in (lengths, prefixes, cotangent, keys, values)
    ]
    outs = pl.pallas_call(
        functools.partial(prep_kernel, parts),
        out_shape=(block,) * 3 + (piece,) * parts + (pltpu.VMEM((parts, 2, lanes), jnp.int32),),
        in_specs=[_HBM] * 5,
        out_specs=(_VMEM,) * (parts + 4),
        scratch_shapes=[
            pltpu.VMEM(keys.shape, jnp.bfloat16),
            pltpu.VMEM(values.shape, jnp.bfloat16),
            pltpu.SMEM(lengths.shape, jnp.int32),
            pltpu.SMEM(prefixes.shape, jnp.int32),
            pltpu.SemaphoreType.DMA((parts + 2,)),
            pltpu.SemaphoreType.DMA((2,)),
        ],
        compiler_params=pltpu.CompilerParams(vmem_limit_bytes=VMEM_BYTES),
        name="prepare",
    )(*operands)
    return outs[:3], outs[3:-1], outs[-1]


def bounds(position, lengths, prefixes):
    docs = lengths.shape[0]

    def step(doc, carry):
        start, low, high = carry
        end = start + lengths[doc]
        inside = (position >= start) & (position < end)
        reach = jnp.minimum(end, jnp.maximum(position + 1, start + prefixes[doc]))
        return end, jnp.where(inside, start, low), jnp.where(inside, reach, high)

    zero = jnp.zeros_like(position)
    carry = (jnp.int32(0), zero, zero)
    if docs <= 16:
        for doc in range(docs):
            carry = step(doc, carry)
    else:
        carry = lax.fori_loop(0, docs, step, carry)
    return carry[1], carry[2]


def neighbour_slots(shard):
    odd = shard % 2
    ahead, behind = BACK + 1, BACK - 1
    return jnp.where(odd == 1, behind, ahead), jnp.where(odd == 1, ahead, behind)


def grad_kernel(masks, parts, is_first, is_last, range_ref, q_ref, *refs):
    refs = list(refs)
    kv_own, kv_even, kv_far, kv_odd = [refs.pop(0) for _ in range(4)]
    cots = [refs.pop(0) for _ in masks]
    carried = None if is_first else refs.pop(0)
    dqs = [refs.pop(0) for _ in masks]
    outs, (window, acc, score_buf, dprob_buf, prob_buf, dscore_buf) = refs[:-6], refs[-6:]
    rows, heads, size = q_ref.shape
    tokens = rows // parts
    kv_heads = kv_own.shape[1]
    group_size = heads // kv_heads
    span = (BACK + 1 + AHEAD) * rows
    reach = span - rows + tokens
    lanes = tokens * group_size
    scale = size ** (-0.5)
    shard = lax.axis_index("seq")
    me = lax.axis_index("kvh")

    even_slot, odd_slot = neighbour_slots(shard)
    for slot, ref in ((BACK, kv_own), (0, kv_far), (even_slot, kv_even), (odd_slot, kv_odd)):
        part = pl.ds(pl.multiple_of(slot * rows, rows), rows)
        for number in range(2):
            for group in range(kv_heads):
                window[number, group, part] = ref[number, group]
    acc[...] = jnp.zeros_like(acc) if is_first else carried[...]

    contract_last = (((1,), (1,)), ((), ()))
    contract_first = (((0,), (0,)), ((), ()))
    sublane = lax.broadcasted_iota(jnp.int32, (TILE, lanes), 0)
    items = [(place, group) for place in range(len(masks)) for group in range(kv_heads)]

    def operands(item):
        place, group = items[item]
        first = pl.multiple_of((me ^ masks[place]) * tokens, tokens)
        of_group = pl.ds(group * group_size, group_size)
        q = q_ref[pl.ds(first, tokens), of_group].astype(jnp.float32)
        cot = cots[place][:, of_group].astype(jnp.float32)
        return (
            pl.ds(first, reach),
            q.reshape(lanes, size).astype(jnp.bfloat16),
            cot.reshape(lanes, size).astype(jnp.bfloat16),
        )

    def scores_of(item):
        place, group = items[item]
        slot = item % 2
        here, q, cot = operands(item)
        scores = lax.dot_general(
            window[0, group, here], q, contract_last, preferred_element_type=jnp.float32
        )
        low = range_ref[masks[place], 0:1, :] - sublane
        high = range_ref[masks[place], 1:2, :] - sublane
        top = jnp.full((TILE, lanes), NEG, jnp.float32)
        for row in range(0, reach, TILE):
            visible = (low <= row) & (high > row)
            tile = jnp.where(visible, scores[row : row + TILE] * (scale * LOG2E), NEG)
            top = jnp.maximum(top, tile)
            score_buf[slot, row : row + TILE] = tile
        dprob_buf[slot] = lax.dot_general(
            window[1, group, here], cot, contract_last, preferred_element_type=jnp.float32
        )
        return jnp.max(top, axis=0, keepdims=True)

    def softmax_of(item, top):
        slot = item % 2
        total = jnp.zeros((TILE, lanes), jnp.float32)
        delta = jnp.zeros((TILE, lanes), jnp.float32)
        for row in range(0, reach, TILE):
            tile = slice(row, row + TILE)
            expo = jnp.exp2(score_buf[slot, tile] - top)
            total = total + expo
            delta = delta + expo * dprob_buf[slot, tile]
            score_buf[slot, tile] = expo
        inverse = 1.0 / jnp.sum(total, axis=0, keepdims=True)
        delta = jnp.sum(delta, axis=0, keepdims=True) * inverse
        for row in range(0, reach, 2 * TILE):
            tile = slice(row, row + 2 * TILE)
            probs = score_buf[slot, tile] * inverse
            dscores = probs * (dprob_buf[slot, tile] - delta)
            prob_buf[slot, tile] = probs.astype(jnp.bfloat16)
            dscore_buf[slot, tile] = dscores.astype(jnp.bfloat16)

    def gradients_of(item):
        place, group = items[item]
        slot = item % 2
        here, q, cot = operands(item)
        dscores = dscore_buf[slot]
        acc[1, group, here] += jnp.dot(prob_buf[slot], cot, preferred_element_type=jnp.float32)
        acc[0, group, here] += jnp.dot(dscores, q, preferred_element_type=jnp.float32)
        dq = lax.dot_general(
            window[0, group, here], dscores, contract_first, preferred_element_type=jnp.float32
        )
        dq = jnp.transpose(dq * scale).reshape(tokens, group_size, size)
        dqs[place][:, pl.ds(group * group_size, group_size)] = dq.astype(jnp.bfloat16)

    top = scores_of(0)
    for item in range(len(items)):
        later = scores_of(item + 1) if item + 1 < len(items) else None
        softmax_of(item, top)
        gradients_of(item)
        top = later

    if not is_last:
        outs[0][...] = acc[...]
        return
    for slot, ref in zip((BACK, 0, even_slot, odd_slot), outs):
        part = pl.ds(pl.multiple_of(slot * rows, rows), rows)
        for group in range(kv_heads):
            ref[0, group] = (acc[0, group, part] * scale).astype(ref.dtype)
            ref[1, group] = acc[1, group, part].astype(ref.dtype)


def gradients(masks, parts, ranges, queries, cots, blocks, carried):
    rows, heads, size = queries.shape
    is_last = masks == stages(parts)[-1]
    kv_shape = blocks[0].shape
    kv_heads = kv_shape[1]
    span = (BACK + 1 + AHEAD) * rows
    acc_shape = (2, kv_heads, span, size)
    tokens = rows // parts
    tile_shape = (2, span - rows + tokens, tokens * (heads // kv_heads))
    work = heads * rows // parts * span * len(masks)
    outs = [pltpu.VMEM(cots[0].shape, jnp.bfloat16)] * len(masks)
    if is_last:
        outs += [pltpu.VMEM(kv_shape, jnp.float32)] + [pltpu.VMEM(kv_shape, jnp.bfloat16)] * 3
    else:
        outs += [pltpu.VMEM(acc_shape, jnp.float32)]
    own, far, even, odd = blocks
    operands = [ranges, queries, own, even, far, odd, *cots]
    operands += [] if carried is None else [carried]
    outs = pl.pallas_call(
        functools.partial(grad_kernel, masks, parts, carried is None, is_last),
        out_shape=tuple(outs),
        in_specs=[_VMEM] * len(operands),
        out_specs=(_VMEM,) * len(outs),
        scratch_shapes=[
            pltpu.VMEM(acc_shape, jnp.bfloat16),
            pltpu.VMEM(acc_shape, jnp.float32),
            pltpu.VMEM(tile_shape, jnp.float32),
            pltpu.VMEM(tile_shape, jnp.float32),
            pltpu.VMEM(tile_shape, jnp.bfloat16),
            pltpu.VMEM(tile_shape, jnp.bfloat16),
        ],
        compiler_params=pltpu.CompilerParams(vmem_limit_bytes=VMEM_BYTES),
        cost_estimate=pl.CostEstimate(
            flops=10 * work * size, bytes_accessed=4 * queries.size * 2, transcendentals=work
        ),
        name="gradients",
    )(*operands)
    return outs[: len(masks)], outs[len(masks) :]


def finish_order(parts):
    return ["odd", "far", parts - 1, "even", *range(parts - 2, -1, -1), "own"]


def finish_kernel(parts, *refs):
    *refs, dq_out, dk_out, dv_out = refs
    refs = dict(zip(finish_order(parts), refs))
    dqs = [refs[mask] for mask in range(parts)]
    own, far, even, odd = [refs[name] for name in ("own", "far", "even", "odd")]
    heads = dqs[0].shape[1]
    me = lax.axis_index("kvh")
    for mask in range(parts):
        first = pl.multiple_of((me ^ mask) * heads, heads)
        dq_out[:, pl.ds(first, heads), :] = dqs[mask][...]
    for number, ref in enumerate((dk_out, dv_out)):
        sums = []
        for group in range(ref.shape[1]):
            total = own[number, group]
            for other in (far, even, odd):
                total = total + other[number, group].astype(jnp.float32)
            sums.append(total)
        ref[...] = jnp.stack(sums, axis=1).astype(jnp.bfloat16)


def finish(dqs, partials):
    parts = len(dqs)
    rows, heads, size = dqs[0].shape
    _, kv_heads, kv_rows, _ = partials[0].shape
    kv_out = jax.ShapeDtypeStruct((kv_rows, kv_heads, size), jnp.bfloat16)
    operands = dict(enumerate(dqs)) | dict(zip(("own", "far", "even", "odd"), partials))
    return pl.pallas_call(
        functools.partial(finish_kernel, parts),
        out_shape=(
            jax.ShapeDtypeStruct((rows, heads * parts, size), jnp.bfloat16),
            kv_out,
            kv_out,
        ),
        in_specs=[_VMEM] * (parts + 4),
        out_specs=(_VMEM,) * 3,
        compiler_params=pltpu.CompilerParams(vmem_limit_bytes=VMEM_BYTES),
        name="finish",
    )(*[operands[name] for name in finish_order(parts)])


def shifted(block, distance):
    count = lax.axis_size("seq")
    return lax.ppermute(block, "seq", [(i, (i + distance) % count) for i in range(count)])


def paired(block):
    return lax.ppermute(block, "seq", [(i, i ^ 1) for i in range(lax.axis_size("seq"))])


def ringed(block):
    count = lax.axis_size("seq")
    route = []
    for i in range(count):
        target = i + 2 if i % 2 == 0 else i - 2
        route.append((i, min(max(target, 0), count - 1)))
    return lax.ppermute(block, "seq", route)


def swapped(block, mask):
    return lax.ppermute(block, "kvh", [(i, i ^ mask) for i in range(lax.axis_size("kvh"))])


def local(queries, keys, values, output_gradient, doc_lengths, prefix_lengths):
    parts = lax.axis_size("kvh")
    kv, cots, ranges = prepare(
        doc_lengths, prefix_lengths, output_gradient, keys, values, parts
    )
    even = paired(kv[2])
    blocks = [kv[0], shifted(kv[1], BACK), even, ringed(even)]
    cots = [cots[0]] + [swapped(cots[mask], mask) for mask in range(1, parts)]
    dqs, carried = {}, [None]
    for masks in stages(parts):
        found, carried = gradients(
            masks, parts, ranges, queries, [cots[mask] for mask in masks], blocks, carried[0]
        )
        for mask, dq in zip(masks, found):
            dqs[mask] = swapped(dq, mask) if mask else dq
    own, far, even, odd = carried
    partials = [own, shifted(far, -BACK), paired(even), ringed(paired(odd))]
    return finish([dqs[mask] for mask in range(parts)], partials)


def solution(mesh):
    in_specs = (
        P("seq", "kvh", None),
        P("seq", "kvh", None),
        P("seq", "kvh", None),
        P(("seq", "kvh"), None, None),
        P(),
        P(),
    )
    out_specs = (P(("seq", "kvh"), None, None), P("seq", "kvh", None), P("seq", "kvh", None))
    return jax.shard_map(local, mesh=mesh, in_specs=in_specs, out_specs=out_specs, check_vma=False)
```

```python
import functools

import jax
import jax.numpy as jnp
from jax import lax
from jax.experimental import pallas as pl
from jax.experimental.pallas import tpu as pltpu
from jax.sharding import PartitionSpec as P

BACK = 2
AHEAD = 1
LOG2E = 1.4426950408889634
VMEM_BYTES = 40 * 1024 * 1024
NEG = -1e30
TILE = 8

_VMEM = pl.BlockSpec(memory_space=pltpu.VMEM)
_SMEM = pl.BlockSpec(memory_space=pltpu.SMEM)
_HBM = pl.BlockSpec(memory_space=pltpu.HBM)


def stages(parts):
    rest = list(range(parts - 1, 1, -1))
    return [[0, 1, *rest[:-1]], rest[-1:]]


def regroup(buf):
    wide = buf[...].astype(jnp.float32)
    return [wide[:, group, :].astype(jnp.bfloat16) for group in range(buf.shape[1])]


def prep_kernel(parts, lengths_ref, prefixes_ref, cot_ref, key_ref, value_ref, *rest):
    kv_outs, cot_outs, rest = rest[:3], rest[3 : parts + 3], rest[parts + 3 :]
    range_out, key_buf, value_buf, lengths, prefixes, sems, scalar_sems = rest
    heads = cot_ref.shape[1] // parts
    me = lax.axis_index("kvh")
    scalars = [
        pltpu.make_async_copy(lengths_ref, lengths, scalar_sems.at[0]),
        pltpu.make_async_copy(prefixes_ref, prefixes, scalar_sems.at[1]),
    ]
    for copy in scalars:
        copy.start()
    loads = []
    for number, (ref, buf) in enumerate(((key_ref, key_buf), (value_ref, value_buf))):
        loads.append(pltpu.make_async_copy(ref, buf, sems.at[number]))
        loads[-1].start()
    copies = []
    for mask in range(parts):
        first = pl.multiple_of((me ^ mask) * heads, heads)
        copies.append(
            pltpu.make_async_copy(
                cot_ref.at[:, pl.ds(first, heads), :], cot_outs[mask], sems.at[mask + 2]
            )
        )
        copies[-1].start()
    for number, buf in enumerate((key_buf, value_buf)):
        loads[number].wait()
        for group, block in enumerate(regroup(buf)):
            for kv_out in kv_outs:
                kv_out[number, group] = block
    for copy in scalars:
        copy.wait()
    rows = key_buf.shape[0]
    tokens = rows // parts
    lanes = range_out.shape[2]
    lane_token = lax.broadcasted_iota(jnp.int32, (1, lanes), 1) // (lanes // tokens)
    shard = lax.axis_index("seq")
    for mask in range(parts):
        first = (me ^ mask) * tokens
        low, high = bounds(shard * rows + first + lane_token, lengths, prefixes)
        origin = (shard - BACK) * rows + first
        range_out[mask, 0:1, :] = low - origin
        range_out[mask, 1:2, :] = high - origin
    for copy in copies:
        copy.wait()


def prepare(lengths, prefixes, cotangent, keys, values, parts):
    rows, heads, size = cotangent.shape
    kv_rows, kv_heads, _ = keys.shape
    lanes = kv_rows // parts * (heads // parts // kv_heads)
    piece = pltpu.VMEM((rows, heads // parts, size), jnp.bfloat16)
    block = pltpu.VMEM((2, kv_heads, kv_rows, size), jnp.bfloat16)
    operands = [
        pltpu.with_memory_space_constraint(array, pltpu.HBM)
        for array in (lengths, prefixes, cotangent, keys, values)
    ]
    outs = pl.pallas_call(
        functools.partial(prep_kernel, parts),
        out_shape=(block,) * 3 + (piece,) * parts + (pltpu.VMEM((parts, 2, lanes), jnp.int32),),
        in_specs=[_HBM] * 5,
        out_specs=(_VMEM,) * (parts + 4),
        scratch_shapes=[
            pltpu.VMEM(keys.shape, jnp.bfloat16),
            pltpu.VMEM(values.shape, jnp.bfloat16),
            pltpu.SMEM(lengths.shape, jnp.int32),
            pltpu.SMEM(prefixes.shape, jnp.int32),
            pltpu.SemaphoreType.DMA((parts + 2,)),
            pltpu.SemaphoreType.DMA((2,)),
        ],
        compiler_params=pltpu.CompilerParams(vmem_limit_bytes=VMEM_BYTES),
        name="prepare",
    )(*operands)
    return outs[:3], outs[3:-1], outs[-1]


def bounds(position, lengths, prefixes):
    docs = lengths.shape[0]

    def step(doc, carry):
        start, low, high = carry
        end = start + lengths[doc]
        inside = (position >= start) & (position < end)
        reach = jnp.minimum(end, jnp.maximum(position + 1, start + prefixes[doc]))
        return end, jnp.where(inside, start, low), jnp.where(inside, reach, high)

    zero = jnp.zeros_like(position)
    carry = (jnp.int32(0), zero, zero)
    if docs <= 16:
        for doc in range(docs):
            carry = step(doc, carry)
    else:
        carry = lax.fori_loop(0, docs, step, carry)
    return carry[1], carry[2]


def neighbour_slots(shard):
    odd = shard % 2
    ahead, behind = BACK + 1, BACK - 1
    return jnp.where(odd == 1, behind, ahead), jnp.where(odd == 1, ahead, behind)


def grad_kernel(masks, parts, is_first, is_last, range_ref, q_ref, *refs):
    refs = list(refs)
    kv_own, kv_even, kv_far, kv_odd = [refs.pop(0) for _ in range(4)]
    cots = [refs.pop(0) for _ in masks]
    carried = None if is_first else refs.pop(0)
    dqs = [refs.pop(0) for _ in masks]
    outs, (window, acc, score_buf, dprob_buf, prob_buf, dscore_buf) = refs[:-6], refs[-6:]
    rows, heads, size = q_ref.shape
    tokens = rows // parts
    kv_heads = kv_own.shape[1]
    group_size = heads // kv_heads
    span = (BACK + 1 + AHEAD) * rows
    reach = span - rows + tokens
    lanes = tokens * group_size
    scale = size ** (-0.5)
    shard = lax.axis_index("seq")
    me = lax.axis_index("kvh")

    even_slot, odd_slot = neighbour_slots(shard)
    for slot, ref in ((BACK, kv_own), (0, kv_far), (even_slot, kv_even), (odd_slot, kv_odd)):
        part = pl.ds(pl.multiple_of(slot * rows, rows), rows)
        for number in range(2):
            for group in range(kv_heads):
                window[number, group, part] = ref[number, group]
    acc[...] = jnp.zeros_like(acc) if is_first else carried[...]

    contract_last = (((1,), (1,)), ((), ()))
    contract_first = (((0,), (0,)), ((), ()))
    sublane = lax.broadcasted_iota(jnp.int32, (TILE, lanes), 0)
    items = [(place, group) for place in range(len(masks)) for group in range(kv_heads)]

    def operands(item):
        place, group = items[item]
        first = pl.multiple_of((me ^ masks[place]) * tokens, tokens)
        of_group = pl.ds(group * group_size, group_size)
        q = q_ref[pl.ds(first, tokens), of_group].astype(jnp.float32)
        cot = cots[place][:, of_group].astype(jnp.float32)
        return (
            pl.ds(first, reach),
            q.reshape(lanes, size).astype(jnp.bfloat16),
            cot.reshape(lanes, size).astype(jnp.bfloat16),
        )

    def scores_of(item):
        place, group = items[item]
        slot = item % 2
        here, q, cot = operands(item)
        scores = lax.dot_general(
            window[0, group, here], q, contract_last, preferred_element_type=jnp.float32
        )
        low = range_ref[masks[place], 0:1, :] - sublane
        high = range_ref[masks[place], 1:2, :] - sublane
        top = jnp.full((TILE, lanes), NEG, jnp.float32)
        for row in range(0, reach, TILE):
            visible = (low <= row) & (high > row)
            tile = jnp.where(visible, scores[row : row + TILE] * (scale * LOG2E), NEG)
            top = jnp.maximum(top, tile)
            score_buf[slot, row : row + TILE] = tile
        dprob_buf[slot] = lax.dot_general(
            window[1, group, here], cot, contract_last, preferred_element_type=jnp.float32
        )
        return jnp.max(top, axis=0, keepdims=True)

    def softmax_of(item, top):
        slot = item % 2
        total = jnp.zeros((TILE, lanes), jnp.float32)
        delta = jnp.zeros((TILE, lanes), jnp.float32)
        for row in range(0, reach, TILE):
            tile = slice(row, row + TILE)
            expo = jnp.exp2(score_buf[slot, tile] - top)
            total = total + expo
            delta = delta + expo * dprob_buf[slot, tile]
            score_buf[slot, tile] = expo
        inverse = 1.0 / jnp.sum(total, axis=0, keepdims=True)
        delta = jnp.sum(delta, axis=0, keepdims=True) * inverse
        for row in range(0, reach, 2 * TILE):
            tile = slice(row, row + 2 * TILE)
            probs = score_buf[slot, tile] * inverse
            dscores = probs * (dprob_buf[slot, tile] - delta)
            prob_buf[slot, tile] = probs.astype(jnp.bfloat16)
            dscore_buf[slot, tile] = dscores.astype(jnp.bfloat16)

    def gradients_of(item):
        place, group = items[item]
        slot = item % 2
        here, q, cot = operands(item)
        dscores = dscore_buf[slot]
        acc[1, group, here] += jnp.dot(prob_buf[slot], cot, preferred_element_type=jnp.float32)
        acc[0, group, here] += jnp.dot(dscores, q, preferred_element_type=jnp.float32)
        dq = lax.dot_general(
            window[0, group, here], dscores, contract_first, preferred_element_type=jnp.float32
        )
        dq = jnp.transpose(dq * scale).reshape(tokens, group_size, size)
        dqs[place][:, pl.ds(group * group_size, group_size)] = dq.astype(jnp.bfloat16)

    top = scores_of(0)
    for item in range(len(items)):
        later = scores_of(item + 1) if item + 1 < len(items) else None
        softmax_of(item, top)
        gradients_of(item)
        top = later

    if not is_last:
        outs[0][...] = acc[...]
        return
    for slot, ref in zip((BACK, 0, even_slot, odd_slot), outs):
        part = pl.ds(pl.multiple_of(slot * rows, rows), rows)
        for group in range(kv_heads):
            ref[0, group] = (acc[0, group, part] * scale).astype(ref.dtype)
            ref[1, group] = acc[1, group, part].astype(ref.dtype)


def gradients(masks, parts, ranges, queries, cots, blocks, carried):
    rows, heads, size = queries.shape
    is_last = masks == stages(parts)[-1]
    kv_shape = blocks[0].shape
    kv_heads = kv_shape[1]
    span = (BACK + 1 + AHEAD) * rows
    acc_shape = (2, kv_heads, span, size)
    tokens = rows // parts
    tile_shape = (2, span - rows + tokens, tokens * (heads // kv_heads))
    work = heads * rows // parts * span * len(masks)
    outs = [pltpu.VMEM(cots[0].shape, jnp.bfloat16)] * len(masks)
    if is_last:
        outs += [pltpu.VMEM(kv_shape, jnp.float32)] + [pltpu.VMEM(kv_shape, jnp.bfloat16)] * 3
    else:
        outs += [pltpu.VMEM(acc_shape, jnp.float32)]
    own, far, even, odd = blocks
    operands = [ranges, queries, own, even, far, odd, *cots]
    operands += [] if carried is None else [carried]
    outs = pl.pallas_call(
        functools.partial(grad_kernel, masks, parts, carried is None, is_last),
        out_shape=tuple(outs),
        in_specs=[_VMEM] * len(operands),
        out_specs=(_VMEM,) * len(outs),
        scratch_shapes=[
            pltpu.VMEM(acc_shape, jnp.bfloat16),
            pltpu.VMEM(acc_shape, jnp.float32),
            pltpu.VMEM(tile_shape, jnp.float32),
            pltpu.VMEM(tile_shape, jnp.float32),
            pltpu.VMEM(tile_shape, jnp.bfloat16),
            pltpu.VMEM(tile_shape, jnp.bfloat16),
        ],
        compiler_params=pltpu.CompilerParams(vmem_limit_bytes=VMEM_BYTES),
        cost_estimate=pl.CostEstimate(
            flops=10 * work * size, bytes_accessed=4 * queries.size * 2, transcendentals=work
        ),
        name="gradients",
    )(*operands)
    return outs[: len(masks)], outs[len(masks) :]


def finish_order(parts):
    return ["odd", "far", parts - 1, "even", *range(parts - 2, -1, -1), "own"]


def finish_kernel(parts, *refs):
    *refs, dq_out, dk_out, dv_out = refs
    refs = dict(zip(finish_order(parts), refs))
    dqs = [refs[mask] for mask in range(parts)]
    own, far, even, odd = [refs[name] for name in ("own", "far", "even", "odd")]
    heads = dqs[0].shape[1]
    me = lax.axis_index("kvh")
    for mask in range(parts):
        first = pl.multiple_of((me ^ mask) * heads, heads)
        dq_out[:, pl.ds(first, heads), :] = dqs[mask][...]
    for number, ref in enumerate((dk_out, dv_out)):
        sums = []
        for group in range(ref.shape[1]):
            total = own[number, group]
            for other in (far, even, odd):
                total = total + other[number, group].astype(jnp.float32)
            sums.append(total)
        ref[...] = jnp.stack(sums, axis=1).astype(jnp.bfloat16)


def finish(dqs, partials):
    parts = len(dqs)
    rows, heads, size = dqs[0].shape
    _, kv_heads, kv_rows, _ = partials[0].shape
    kv_out = jax.ShapeDtypeStruct((kv_rows, kv_heads, size), jnp.bfloat16)
    operands = dict(enumerate(dqs)) | dict(zip(("own", "far", "even", "odd"), partials))
    return pl.pallas_call(
        functools.partial(finish_kernel, parts),
        out_shape=(
            jax.ShapeDtypeStruct((rows, heads * parts, size), jnp.bfloat16),
            kv_out,
            kv_out,
        ),
        in_specs=[_VMEM] * (parts + 4),
        out_specs=(_VMEM,) * 3,
        compiler_params=pltpu.CompilerParams(vmem_limit_bytes=VMEM_BYTES),
        name="finish",
    )(*[operands[name] for name in finish_order(parts)])


def shifted(block, distance):
    count = lax.axis_size("seq")
    route = [(i, (i + distance) % count) for i in range(count)]
    if distance < 0:
        route = [(i, target) for i, target in route if target < i]
    return lax.ppermute(block, "seq", route)


def paired(block):
    return lax.ppermute(block, "seq", [(i, i ^ 1) for i in range(lax.axis_size("seq"))])


def ringed(block):
    count = lax.axis_size("seq")
    route = []
    for i in range(count):
        target = i + 2 if i % 2 == 0 else i - 2
        route.append((i, min(max(target, 0), count - 1)))
    return lax.ppermute(block, "seq", route)


def swapped(block, mask):
    return lax.ppermute(block, "kvh", [(i, i ^ mask) for i in range(lax.axis_size("kvh"))])


def local(queries, keys, values, output_gradient, doc_lengths, prefix_lengths):
    parts = lax.axis_size("kvh")
    kv, cots, ranges = prepare(
        doc_lengths, prefix_lengths, output_gradient, keys, values, parts
    )
    even = paired(kv[2])
    blocks = [kv[0], shifted(kv[1], BACK), even, ringed(even)]
    cots = [cots[0]] + [swapped(cots[mask], mask) for mask in range(1, parts)]
    dqs, carried = {}, [None]
    for masks in stages(parts):
        found, carried = gradients(
            masks, parts, ranges, queries, [cots[mask] for mask in masks], blocks, carried[0]
        )
        for mask, dq in zip(masks, found):
            dqs[mask] = swapped(dq, mask) if mask else dq
    own, far, even, odd = carried
    partials = [own, shifted(far, -BACK), paired(even), ringed(paired(odd))]
    return finish([dqs[mask] for mask in range(parts)], partials)


def solution(mesh):
    in_specs = (
        P("seq", "kvh", None),
        P("seq", "kvh", None),
        P("seq", "kvh", None),
        P(("seq", "kvh"), None, None),
        P(),
        P(),
    )
    out_specs = (P(("seq", "kvh"), None, None), P("seq", "kvh", None), P("seq", "kvh", None))
    return jax.shard_map(local, mesh=mesh, in_specs=in_specs, out_specs=out_specs, check_vma=False)
```

```python
import functools

import jax
import jax.numpy as jnp
from jax import lax
from jax.experimental import pallas as pl
from jax.experimental.pallas import tpu as pltpu
from jax.sharding import PartitionSpec as P

BACK = 2
AHEAD = 1
LOG2E = 1.4426950408889634
VMEM_BYTES = 40 * 1024 * 1024
NEG = -1e30
TILE = 8

_VMEM = pl.BlockSpec(memory_space=pltpu.VMEM)
_SMEM = pl.BlockSpec(memory_space=pltpu.SMEM)
_HBM = pl.BlockSpec(memory_space=pltpu.HBM)


def stages(parts):
    rest = list(range(parts - 1, 1, -1))
    return [[0, 1, *rest[:-1]], rest[-1:]]


def regroup(buf):
    wide = buf[...].astype(jnp.float32)
    return [wide[:, group, :].astype(jnp.bfloat16) for group in range(buf.shape[1])]


def prep_kernel(parts, lengths_ref, prefixes_ref, cot_ref, key_ref, value_ref, *rest):
    kv_outs, cot_outs, rest = rest[:3], rest[3 : parts + 3], rest[parts + 3 :]
    range_out, key_buf, value_buf, lengths, prefixes, sems, scalar_sems = rest
    heads = cot_ref.shape[1] // parts
    me = lax.axis_index("kvh")
    scalars = [
        pltpu.make_async_copy(lengths_ref, lengths, scalar_sems.at[0]),
        pltpu.make_async_copy(prefixes_ref, prefixes, scalar_sems.at[1]),
    ]
    for copy in scalars:
        copy.start()
    loads = []
    for number, (ref, buf) in enumerate(((key_ref, key_buf), (value_ref, value_buf))):
        loads.append(pltpu.make_async_copy(ref, buf, sems.at[number]))
        loads[-1].start()
    copies = []
    for mask in range(parts):
        first = pl.multiple_of((me ^ mask) * heads, heads)
        copies.append(
            pltpu.make_async_copy(
                cot_ref.at[:, pl.ds(first, heads), :], cot_outs[mask], sems.at[mask + 2]
            )
        )
        copies[-1].start()
    for number, buf in enumerate((key_buf, value_buf)):
        loads[number].wait()
        for group, block in enumerate(regroup(buf)):
            for kv_out in kv_outs:
                kv_out[number, group] = block
    for copy in scalars:
        copy.wait()
    rows = key_buf.shape[0]
    tokens = rows // parts
    lanes = range_out.shape[2]
    lane_token = lax.broadcasted_iota(jnp.int32, (1, lanes), 1) // (lanes // tokens)
    shard = lax.axis_index("seq")
    for mask in range(parts):
        first = (me ^ mask) * tokens
        low, high = bounds(shard * rows + first + lane_token, lengths, prefixes)
        origin = (shard - BACK) * rows + first
        range_out[mask, 0:1, :] = low - origin
        range_out[mask, 1:2, :] = high - origin
    for copy in copies:
        copy.wait()


def prepare(lengths, prefixes, cotangent, keys, values, parts):
    rows, heads, size = cotangent.shape
    kv_rows, kv_heads, _ = keys.shape
    lanes = kv_rows // parts * (heads // parts // kv_heads)
    piece = pltpu.VMEM((rows, heads // parts, size), jnp.bfloat16)
    block = pltpu.VMEM((2, kv_heads, kv_rows, size), jnp.bfloat16)
    operands = [
        pltpu.with_memory_space_constraint(array, pltpu.HBM)
        for array in (lengths, prefixes, cotangent, keys, values)
    ]
    outs = pl.pallas_call(
        functools.partial(prep_kernel, parts),
        out_shape=(block,) * 3 + (piece,) * parts + (pltpu.VMEM((parts, 2, lanes), jnp.int32),),
        in_specs=[_HBM] * 5,
        out_specs=(_VMEM,) * (parts + 4),
        scratch_shapes=[
            pltpu.VMEM(keys.shape, jnp.bfloat16),
            pltpu.VMEM(values.shape, jnp.bfloat16),
            pltpu.SMEM(lengths.shape, jnp.int32),
            pltpu.SMEM(prefixes.shape, jnp.int32),
            pltpu.SemaphoreType.DMA((parts + 2,)),
            pltpu.SemaphoreType.DMA((2,)),
        ],
        compiler_params=pltpu.CompilerParams(vmem_limit_bytes=VMEM_BYTES),
        name="prepare",
    )(*operands)
    return outs[:3], outs[3:-1], outs[-1]


def bounds(position, lengths, prefixes):
    docs = lengths.shape[0]

    def step(doc, carry):
        start, low, high = carry
        end = start + lengths[doc]
        inside = (position >= start) & (position < end)
        reach = jnp.minimum(end, jnp.maximum(position + 1, start + prefixes[doc]))
        return end, jnp.where(inside, start, low), jnp.where(inside, reach, high)

    zero = jnp.zeros_like(position)
    carry = (jnp.int32(0), zero, zero)
    if docs <= 16:
        for doc in range(docs):
            carry = step(doc, carry)
    else:
        carry = lax.fori_loop(0, docs, step, carry)
    return carry[1], carry[2]


def neighbour_slots(shard):
    odd = shard % 2
    ahead, behind = BACK + 1, BACK - 1
    return jnp.where(odd == 1, behind, ahead), jnp.where(odd == 1, ahead, behind)


def grad_kernel(masks, parts, is_first, is_last, range_ref, q_ref, *refs):
    refs = list(refs)
    kv_own, kv_even, kv_far, kv_odd = [refs.pop(0) for _ in range(4)]
    cots = [refs.pop(0) for _ in masks]
    carried = None if is_first else refs.pop(0)
    dqs = [refs.pop(0) for _ in masks]
    outs, (window, acc, score_buf, dprob_buf, prob_buf, dscore_buf) = refs[:-6], refs[-6:]
    rows, heads, size = q_ref.shape
    tokens = rows // parts
    kv_heads = kv_own.shape[1]
    group_size = heads // kv_heads
    span = (BACK + 1 + AHEAD) * rows
    reach = span - rows + tokens
    lanes = tokens * group_size
    scale = size ** (-0.5)
    shard = lax.axis_index("seq")
    me = lax.axis_index("kvh")

    even_slot, odd_slot = neighbour_slots(shard)
    for slot, ref in ((BACK, kv_own), (0, kv_far), (even_slot, kv_even), (odd_slot, kv_odd)):
        part = pl.ds(pl.multiple_of(slot * rows, rows), rows)
        for number in range(2):
            for group in range(kv_heads):
                window[number, group, part] = ref[number, group]
    acc[...] = jnp.zeros_like(acc) if is_first else carried[...]

    contract_last = (((1,), (1,)), ((), ()))
    contract_first = (((0,), (0,)), ((), ()))
    sublane = lax.broadcasted_iota(jnp.int32, (TILE, lanes), 0)
    items = [(place, group) for place in range(len(masks)) for group in range(kv_heads)]

    def operands(item):
        place, group = items[item]
        first = pl.multiple_of((me ^ masks[place]) * tokens, tokens)
        of_group = pl.ds(group * group_size, group_size)
        q = q_ref[pl.ds(first, tokens), of_group].astype(jnp.float32)
        cot = cots[place][:, of_group].astype(jnp.float32)
        return (
            pl.ds(first, reach),
            q.reshape(lanes, size).astype(jnp.bfloat16),
            cot.reshape(lanes, size).astype(jnp.bfloat16),
        )

    def scores_of(item):
        place, group = items[item]
        slot = item % 2
        here, q, cot = operands(item)
        scores = lax.dot_general(
            window[0, group, here], q, contract_last, preferred_element_type=jnp.float32
        )
        low = range_ref[masks[place], 0:1, :] - sublane
        high = range_ref[masks[place], 1:2, :] - sublane
        top = jnp.full((TILE, lanes), NEG, jnp.float32)
        for row in range(0, reach, TILE):
            visible = (low <= row) & (high > row)
            tile = jnp.where(visible, scores[row : row + TILE] * (scale * LOG2E), NEG)
            top = jnp.maximum(top, tile)
            score_buf[slot, row : row + TILE] = tile
        dprob_buf[slot] = lax.dot_general(
            window[1, group, here], cot, contract_last, preferred_element_type=jnp.float32
        )
        return jnp.max(top, axis=0, keepdims=True)

    def softmax_of(item, top):
        slot = item % 2
        total = jnp.zeros((TILE, lanes), jnp.float32)
        delta = jnp.zeros((TILE, lanes), jnp.float32)
        for row in range(0, reach, TILE):
            tile = slice(row, row + TILE)
            expo = jnp.exp2(score_buf[slot, tile] - top)
            total = total + expo
            delta = delta + expo * dprob_buf[slot, tile]
            score_buf[slot, tile] = expo
        inverse = 1.0 / jnp.sum(total, axis=0, keepdims=True)
        delta = jnp.sum(delta, axis=0, keepdims=True) * inverse
        for row in range(0, reach, 2 * TILE):
            tile = slice(row, row + 2 * TILE)
            probs = score_buf[slot, tile] * inverse
            dscores = probs * (dprob_buf[slot, tile] - delta)
            prob_buf[slot, tile] = probs.astype(jnp.bfloat16)
            dscore_buf[slot, tile] = dscores.astype(jnp.bfloat16)

    def gradients_of(item):
        place, group = items[item]
        slot = item % 2
        here, q, cot = operands(item)
        dscores = dscore_buf[slot]
        acc[1, group, here] += jnp.dot(prob_buf[slot], cot, preferred_element_type=jnp.float32)
        acc[0, group, here] += jnp.dot(dscores, q, preferred_element_type=jnp.float32)
        dq = lax.dot_general(
            window[0, group, here], dscores, contract_first, preferred_element_type=jnp.float32
        )
        dq = jnp.transpose(dq * scale).reshape(tokens, group_size, size)
        dqs[place][:, pl.ds(group * group_size, group_size)] = dq.astype(jnp.bfloat16)

    top = scores_of(0)
    for item in range(len(items)):
        later = scores_of(item + 1) if item + 1 < len(items) else None
        softmax_of(item, top)
        gradients_of(item)
        top = later

    if not is_last:
        outs[0][...] = acc[...]
        return
    is_odd = (shard % 2).astype(jnp.float32)
    weights = (1.0, 1.0 - is_odd, is_odd, 1.0, 1.0)
    for slot, weight, ref in zip((BACK, 0, 0, even_slot, odd_slot), weights, outs):
        part = pl.ds(pl.multiple_of(slot * rows, rows), rows)
        for group in range(kv_heads):
            ref[0, group] = (acc[0, group, part] * (scale * weight)).astype(ref.dtype)
            ref[1, group] = (acc[1, group, part] * weight).astype(ref.dtype)


def gradients(masks, parts, ranges, queries, cots, blocks, carried):
    rows, heads, size = queries.shape
    is_last = masks == stages(parts)[-1]
    kv_shape = blocks[0].shape
    kv_heads = kv_shape[1]
    span = (BACK + 1 + AHEAD) * rows
    acc_shape = (2, kv_heads, span, size)
    tokens = rows // parts
    tile_shape = (2, span - rows + tokens, tokens * (heads // kv_heads))
    work = heads * rows // parts * span * len(masks)
    outs = [pltpu.VMEM(cots[0].shape, jnp.bfloat16)] * len(masks)
    if is_last:
        outs += [pltpu.VMEM(kv_shape, jnp.float32)] + [pltpu.VMEM(kv_shape, jnp.bfloat16)] * 4
    else:
        outs += [pltpu.VMEM(acc_shape, jnp.float32)]
    own, far, even, odd = blocks
    operands = [ranges, queries, own, even, far, odd, *cots]
    operands += [] if carried is None else [carried]
    outs = pl.pallas_call(
        functools.partial(grad_kernel, masks, parts, carried is None, is_last),
        out_shape=tuple(outs),
        in_specs=[_VMEM] * len(operands),
        out_specs=(_VMEM,) * len(outs),
        scratch_shapes=[
            pltpu.VMEM(acc_shape, jnp.bfloat16),
            pltpu.VMEM(acc_shape, jnp.float32),
            pltpu.VMEM(tile_shape, jnp.float32),
            pltpu.VMEM(tile_shape, jnp.float32),
            pltpu.VMEM(tile_shape, jnp.bfloat16),
            pltpu.VMEM(tile_shape, jnp.bfloat16),
        ],
        compiler_params=pltpu.CompilerParams(vmem_limit_bytes=VMEM_BYTES),
        cost_estimate=pl.CostEstimate(
            flops=10 * work * size, bytes_accessed=4 * queries.size * 2, transcendentals=work
        ),
        name="gradients",
    )(*operands)
    return outs[: len(masks)], outs[len(masks) :]


def add_kernel(left, right, out):
    out[...] = (left[...].astype(jnp.float32) + right[...].astype(jnp.float32)).astype(out.dtype)


def add(left, right):
    return pl.pallas_call(
        add_kernel,
        out_shape=pltpu.VMEM(left.shape, left.dtype),
        in_specs=[_VMEM] * 2,
        out_specs=_VMEM,
        compiler_params=pltpu.CompilerParams(vmem_limit_bytes=VMEM_BYTES),
        name="add",
    )(left, right)


def finish_order(parts):
    return [1, "odd", "far", *range(2, parts - 1), "even", parts - 1, 0, "own"]


def finish_kernel(parts, *refs):
    *refs, dq_out, dk_out, dv_out = refs
    refs = dict(zip(finish_order(parts), refs))
    dqs = [refs[mask] for mask in range(parts)]
    own, far, even, odd = [refs[name] for name in ("own", "far", "even", "odd")]
    heads = dqs[0].shape[1]
    me = lax.axis_index("kvh")
    for mask in range(parts):
        first = pl.multiple_of((me ^ mask) * heads, heads)
        dq_out[:, pl.ds(first, heads), :] = dqs[mask][...]
    for number, ref in enumerate((dk_out, dv_out)):
        sums = []
        for group in range(ref.shape[1]):
            total = own[number, group]
            for other in (far, even, odd):
                total = total + other[number, group].astype(jnp.float32)
            sums.append(total)
        ref[...] = jnp.stack(sums, axis=1).astype(jnp.bfloat16)


def finish(dqs, partials):
    parts = len(dqs)
    rows, heads, size = dqs[0].shape
    _, kv_heads, kv_rows, _ = partials[0].shape
    kv_out = jax.ShapeDtypeStruct((kv_rows, kv_heads, size), jnp.bfloat16)
    operands = dict(enumerate(dqs)) | dict(zip(("own", "far", "even", "odd"), partials))
    return pl.pallas_call(
        functools.partial(finish_kernel, parts),
        out_shape=(
            jax.ShapeDtypeStruct((rows, heads * parts, size), jnp.bfloat16),
            kv_out,
            kv_out,
        ),
        in_specs=[_VMEM] * (parts + 4),
        out_specs=(_VMEM,) * 3,
        compiler_params=pltpu.CompilerParams(vmem_limit_bytes=VMEM_BYTES),
        name="finish",
    )(*[operands[name] for name in finish_order(parts)])


def shifted(block, distance):
    count = lax.axis_size("seq")
    return lax.ppermute(block, "seq", [(i, (i + distance) % count) for i in range(count)])


def paired(block):
    return lax.ppermute(block, "seq", [(i, i ^ 1) for i in range(lax.axis_size("seq"))])


def ringed(block, direction=1):
    count = lax.axis_size("seq")
    route = []
    for i in range(count):
        target = i + 2 if i % 2 == 0 else i - 2
        route.append((i, min(max(target, 0), count - 1))[::direction])
    return lax.ppermute(block, "seq", route)


def swapped(block, mask):
    return lax.ppermute(block, "kvh", [(i, i ^ mask) for i in range(lax.axis_size("kvh"))])


def local(queries, keys, values, output_gradient, doc_lengths, prefix_lengths):
    parts = lax.axis_size("kvh")
    kv, cots, ranges = prepare(
        doc_lengths, prefix_lengths, output_gradient, keys, values, parts
    )
    even = paired(kv[2])
    blocks = [kv[0], shifted(kv[1], BACK), even, ringed(even)]
    cots = [cots[0]] + [swapped(cots[mask], mask) for mask in range(1, parts)]
    dqs, carried = {}, [None]
    for masks in stages(parts):
        found, carried = gradients(
            masks, parts, ranges, queries, [cots[mask] for mask in masks], blocks, carried[0]
        )
        for mask, dq in zip(masks, found):
            dqs[mask] = swapped(dq, mask) if mask else dq
    own, far_even, far_odd, even, odd = carried
    relayed = add(paired(odd), far_odd)
    partials = [own, ringed(far_even, -1), paired(even), ringed(relayed)]
    return finish([dqs[mask] for mask in range(parts)], partials)


def solution(mesh):
    in_specs = (
        P("seq", "kvh", None),
        P("seq", "kvh", None),
        P("seq", "kvh", None),
        P(("seq", "kvh"), None, None),
        P(),
        P(),
    )
    out_specs = (P(("seq", "kvh"), None, None), P("seq", "kvh", None), P("seq", "kvh", None))
    return jax.shard_map(local, mesh=mesh, in_specs=in_specs, out_specs=out_specs, check_vma=False)
```

```python
import functools

import jax
import jax.numpy as jnp
from jax import lax
from jax.experimental import pallas as pl
from jax.experimental.pallas import tpu as pltpu
from jax.sharding import PartitionSpec as P

BACK = 2
AHEAD = 1
LOG2E = 1.4426950408889634
VMEM_BYTES = 40 * 1024 * 1024
NEG = -1e30
TILE = 8
RECEIVED = ("rest", "far", "even", "odd", "core")

_VMEM = pl.BlockSpec(memory_space=pltpu.VMEM)
_SMEM = pl.BlockSpec(memory_space=pltpu.SMEM)
_HBM = pl.BlockSpec(memory_space=pltpu.HBM)


def stages(parts, kv_heads):
    rest = list(range(parts - 1, 1, -1))
    every = list(range(kv_heads))
    return [(every, [0, 1, *rest[:-1]]), (every, rest[-1:])]


def regroup(buf):
    wide = buf[...].astype(jnp.float32)
    return [wide[:, group, :].astype(jnp.bfloat16) for group in range(buf.shape[1])]


def prep_kernel(parts, lengths_ref, prefixes_ref, cot_ref, key_ref, value_ref, *rest):
    kv_heads = key_ref.shape[1]
    kv_outs, rest = rest[: kv_heads + 2], rest[kv_heads + 2 :]
    cot_outs, rest = rest[:parts], rest[parts:]
    range_out, key_buf, value_buf, lengths, prefixes, sems, scalar_sems = rest
    heads = cot_ref.shape[1] // parts
    me = lax.axis_index("kvh")
    scalars = [
        pltpu.make_async_copy(lengths_ref, lengths, scalar_sems.at[0]),
        pltpu.make_async_copy(prefixes_ref, prefixes, scalar_sems.at[1]),
    ]
    for copy in scalars:
        copy.start()
    loads = []
    for number, (ref, buf) in enumerate(((key_ref, key_buf), (value_ref, value_buf))):
        loads.append(pltpu.make_async_copy(ref, buf, sems.at[number]))
        loads[-1].start()
    copies = []
    for mask in range(parts):
        first = pl.multiple_of((me ^ mask) * heads, heads)
        copies.append(
            pltpu.make_async_copy(
                cot_ref.at[:, pl.ds(first, heads), :], cot_outs[mask], sems.at[mask + 2]
            )
        )
        copies[-1].start()
    for number, buf in enumerate((key_buf, value_buf)):
        loads[number].wait()
        for group, block in enumerate(regroup(buf)):
            for kv_out in kv_outs[:2]:
                kv_out[number, group] = block
            kv_outs[2 + group][number] = block
    for copy in scalars:
        copy.wait()
    rows = key_buf.shape[0]
    tokens = rows // parts
    lanes = range_out.shape[2]
    lane_token = lax.broadcasted_iota(jnp.int32, (1, lanes), 1) // (lanes // tokens)
    shard = lax.axis_index("seq")
    for mask in range(parts):
        first = (me ^ mask) * tokens
        low, high = bounds(shard * rows + first + lane_token, lengths, prefixes)
        origin = (shard - BACK) * rows + first
        range_out[mask, 0:1, :] = low - origin
        range_out[mask, 1:2, :] = high - origin
    for copy in copies:
        copy.wait()


def prepare(lengths, prefixes, cotangent, keys, values, parts):
    rows, heads, size = cotangent.shape
    kv_rows, kv_heads, _ = keys.shape
    lanes = kv_rows // parts * (heads // parts // kv_heads)
    piece = pltpu.VMEM((rows, heads // parts, size), jnp.bfloat16)
    block = pltpu.VMEM((2, kv_heads, kv_rows, size), jnp.bfloat16)
    head_block = pltpu.VMEM((2, kv_rows, size), jnp.bfloat16)
    operands = [
        pltpu.with_memory_space_constraint(array, pltpu.HBM)
        for array in (lengths, prefixes, cotangent, keys, values)
    ]
    outs = pl.pallas_call(
        functools.partial(prep_kernel, parts),
        out_shape=(block,) * 2
        + (head_block,) * kv_heads
        + (piece,) * parts
        + (pltpu.VMEM((parts, 2, lanes), jnp.int32),),
        in_specs=[_HBM] * 5,
        out_specs=(_VMEM,) * (parts + kv_heads + 3),
        scratch_shapes=[
            pltpu.VMEM(keys.shape, jnp.bfloat16),
            pltpu.VMEM(values.shape, jnp.bfloat16),
            pltpu.SMEM(lengths.shape, jnp.int32),
            pltpu.SMEM(prefixes.shape, jnp.int32),
            pltpu.SemaphoreType.DMA((parts + 2,)),
            pltpu.SemaphoreType.DMA((2,)),
        ],
        compiler_params=pltpu.CompilerParams(vmem_limit_bytes=VMEM_BYTES),
        name="prepare",
    )(*operands)
    return outs[: kv_heads + 2], outs[kv_heads + 2 : -1], outs[-1]


def bounds(position, lengths, prefixes):
    docs = lengths.shape[0]

    def step(doc, carry):
        start, low, high = carry
        end = start + lengths[doc]
        inside = (position >= start) & (position < end)
        reach = jnp.minimum(end, jnp.maximum(position + 1, start + prefixes[doc]))
        return end, jnp.where(inside, start, low), jnp.where(inside, reach, high)

    zero = jnp.zeros_like(position)
    carry = (jnp.int32(0), zero, zero)
    if docs <= 16:
        for doc in range(docs):
            carry = step(doc, carry)
    else:
        carry = lax.fori_loop(0, docs, step, carry)
    return carry[1], carry[2]


def neighbour_slots(shard):
    odd = shard % 2
    ahead, behind = BACK + 1, BACK - 1
    return jnp.where(odd == 1, behind, ahead), jnp.where(odd == 1, ahead, behind)


def received_counts(kv_heads, heads_here, masks):
    core = sum(mask < 2 for mask in masks)
    return {
        "far": 1, "even": kv_heads, "odd": len(heads_here), "core": core, "rest": len(masks) - core,
    }


def grad_kernel(heads_here, masks, parts, is_last, range_ref, q_ref, kv_own, *refs):
    refs = list(refs)

    def take(count):
        taken = refs[:count]
        del refs[:count]
        return taken

    rows, heads, size = q_ref.shape
    tokens = rows // parts
    kv_heads = kv_own.shape[1]
    counts = received_counts(kv_heads, heads_here, masks)
    got = {name: take(counts[name]) for name in RECEIVED}
    kv_far = got["far"][0]
    kv_evens, kv_odds = [got["even"][head] for head in heads_here], got["odd"]
    cots = got["core"] + got["rest"]
    group_size = heads // kv_heads
    carried = take(kv_heads) if is_last else []
    dqs = take(len(masks))
    outs, (window, acc, score_buf, dprob_buf, prob_buf, dscore_buf) = refs[:-6], refs[-6:]
    span = (BACK + 1 + AHEAD) * rows
    reach = span - rows + tokens
    lanes = tokens * group_size
    scale = size ** (-0.5)
    shard = lax.axis_index("seq")
    me = lax.axis_index("kvh")

    even_slot, odd_slot = neighbour_slots(shard)
    for local_head, head in enumerate(heads_here):
        for slot, ref in (
            (BACK, kv_own.at[:, head]),
            (0, kv_far.at[:, head]),
            (even_slot, kv_evens[local_head]),
            (odd_slot, kv_odds[local_head]),
        ):
            part = pl.ds(pl.multiple_of(slot * rows, rows), rows)
            for number in range(2):
                window[number, local_head, part] = ref[number]
    if is_last:
        for local_head, ref in enumerate(carried):
            acc[:, local_head] = ref[...]
    else:
        acc[...] = jnp.zeros_like(acc)

    contract_last = (((1,), (1,)), ((), ()))
    contract_first = (((0,), (0,)), ((), ()))
    sublane = lax.broadcasted_iota(jnp.int32, (TILE, lanes), 0)
    items = [(place, local) for place in range(len(masks)) for local in range(len(heads_here))]

    def operands(item):
        place, group = items[item]
        first = pl.multiple_of((me ^ masks[place]) * tokens, tokens)
        of_group = pl.ds(heads_here[group] * group_size, group_size)
        q = q_ref[pl.ds(first, tokens), of_group].astype(jnp.float32)
        cot = cots[place][:, of_group].astype(jnp.float32)
        return (
            pl.ds(first, reach),
            q.reshape(lanes, size).astype(jnp.bfloat16),
            cot.reshape(lanes, size).astype(jnp.bfloat16),
        )

    def scores_of(item):
        place, group = items[item]
        slot = item % 2
        here, q, cot = operands(item)
        scores = lax.dot_general(
            window[0, group, here], q, contract_last, preferred_element_type=jnp.float32
        )
        low = range_ref[masks[place], 0:1, :] - sublane
        high = range_ref[masks[place], 1:2, :] - sublane
        top = jnp.full((TILE, lanes), NEG, jnp.float32)
        for row in range(0, reach, TILE):
            visible = (low <= row) & (high > row)
            tile = jnp.where(visible, scores[row : row + TILE] * (scale * LOG2E), NEG)
            top = jnp.maximum(top, tile)
            score_buf[slot, row : row + TILE] = tile
        dprob_buf[slot] = lax.dot_general(
            window[1, group, here], cot, contract_last, preferred_element_type=jnp.float32
        )
        return jnp.max(top, axis=0, keepdims=True)

    def softmax_of(item, top):
        slot = item % 2
        total = jnp.zeros((TILE, lanes), jnp.float32)
        delta = jnp.zeros((TILE, lanes), jnp.float32)
        for row in range(0, reach, TILE):
            tile = slice(row, row + TILE)
            expo = jnp.exp2(score_buf[slot, tile] - top)
            total = total + expo
            delta = delta + expo * dprob_buf[slot, tile]
            score_buf[slot, tile] = expo
        inverse = 1.0 / jnp.sum(total, axis=0, keepdims=True)
        delta = jnp.sum(delta, axis=0, keepdims=True) * inverse
        for row in range(0, reach, 2 * TILE):
            tile = slice(row, row + 2 * TILE)
            probs = score_buf[slot, tile] * inverse
            dscores = probs * (dprob_buf[slot, tile] - delta)
            prob_buf[slot, tile] = probs.astype(jnp.bfloat16)
            dscore_buf[slot, tile] = dscores.astype(jnp.bfloat16)

    def gradients_of(item):
        place, group = items[item]
        slot = item % 2
        here, q, cot = operands(item)
        dscores = dscore_buf[slot]
        acc[1, group, here] += jnp.dot(prob_buf[slot], cot, preferred_element_type=jnp.float32)
        acc[0, group, here] += jnp.dot(dscores, q, preferred_element_type=jnp.float32)
        dq = lax.dot_general(
            window[0, group, here], dscores, contract_first, preferred_element_type=jnp.float32
        )
        dq = jnp.transpose(dq * scale).reshape(tokens, group_size, size)
        head = heads_here[group]
        dqs[place][:, pl.ds(head * group_size, group_size)] = dq.astype(jnp.bfloat16)

    top = scores_of(0)
    for item in range(len(items)):
        later = scores_of(item + 1) if item + 1 < len(items) else None
        softmax_of(item, top)
        gradients_of(item)
        top = later

    if not is_last:
        for local_head, ref in enumerate(outs):
            ref[...] = acc[:, local_head]
        return
    is_odd = (shard % 2).astype(jnp.float32)
    weights = (1.0, 1.0 - is_odd, is_odd, 1.0, 1.0)
    for slot, weight, ref in zip((BACK, 0, 0, even_slot, odd_slot), weights, outs):
        part = pl.ds(pl.multiple_of(slot * rows, rows), rows)
        for group in range(kv_heads):
            ref[0, group] = (acc[0, group, part] * (scale * weight)).astype(ref.dtype)
            ref[1, group] = (acc[1, group, part] * weight).astype(ref.dtype)


def gradients(heads_here, masks, parts, ranges, queries, cots, own, far, evens, odds, carried):
    rows, heads, size = queries.shape
    kv_shape = own.shape
    kv_heads = kv_shape[1]
    is_last = len(carried) == kv_heads
    group_size = heads // kv_heads
    span = (BACK + 1 + AHEAD) * rows
    acc_shape = (2, len(heads_here), span, size)
    tokens = rows // parts
    tile_shape = (2, span - rows + tokens, tokens * group_size)
    work = group_size * len(heads_here) * tokens * span * len(masks)
    outs = [pltpu.VMEM((tokens, heads, size), jnp.bfloat16)] * len(masks)
    core = received_counts(kv_heads, heads_here, masks)["core"]
    got = {"far": [far], "even": evens, "odd": odds, "core": cots[:core], "rest": cots[core:]}
    operands = [ranges, queries, own] + [array for name in RECEIVED for array in got[name]]
    if is_last:
        outs += [pltpu.VMEM(kv_shape, jnp.float32)] + [pltpu.VMEM(kv_shape, jnp.bfloat16)] * 4
        operands += carried
    else:
        outs += [pltpu.VMEM((2, span, size), jnp.float32)] * len(heads_here)
    outs = pl.pallas_call(
        functools.partial(grad_kernel, heads_here, masks, parts, is_last),
        out_shape=tuple(outs),
        in_specs=[_VMEM] * len(operands),
        out_specs=(_VMEM,) * len(outs),
        scratch_shapes=[
            pltpu.VMEM(acc_shape, jnp.bfloat16),
            pltpu.VMEM(acc_shape, jnp.float32),
            pltpu.VMEM(tile_shape, jnp.float32),
            pltpu.VMEM(tile_shape, jnp.float32),
            pltpu.VMEM(tile_shape, jnp.bfloat16),
            pltpu.VMEM(tile_shape, jnp.bfloat16),
        ],
        compiler_params=pltpu.CompilerParams(vmem_limit_bytes=VMEM_BYTES),
        cost_estimate=pl.CostEstimate(
            flops=10 * work * size, bytes_accessed=4 * queries.size * 2, transcendentals=work
        ),
        name="gradients",
    )(*operands)
    return outs[: len(masks)], outs[len(masks) :]


def add_kernel(left, right, out):
    out[...] = (left[...].astype(jnp.float32) + right[...].astype(jnp.float32)).astype(out.dtype)


def add(left, right):
    return pl.pallas_call(
        add_kernel,
        out_shape=pltpu.VMEM(left.shape, left.dtype),
        in_specs=[_VMEM] * 2,
        out_specs=_VMEM,
        compiler_params=pltpu.CompilerParams(vmem_limit_bytes=VMEM_BYTES),
        name="add",
    )(left, right)


def finish_order(parts):
    return [1, "odd", "far", *range(2, parts - 1), "even", parts - 1, 0, "own"]


def finish_kernel(parts, *refs):
    *refs, dq_out, dk_out, dv_out = refs
    refs = dict(zip(finish_order(parts), refs))
    dqs = [refs[mask] for mask in range(parts)]
    own, far, even, odd = [refs[name] for name in ("own", "far", "even", "odd")]
    heads = dqs[0].shape[1]
    me = lax.axis_index("kvh")
    for mask in range(parts):
        first = pl.multiple_of((me ^ mask) * heads, heads)
        dq_out[:, pl.ds(first, heads), :] = dqs[mask][...]
    for number, ref in enumerate((dk_out, dv_out)):
        sums = []
        for group in range(ref.shape[1]):
            total = own[number, group]
            for other in (far, even, odd):
                total = total + other[number, group].astype(jnp.float32)
            sums.append(total)
        ref[...] = jnp.stack(sums, axis=1).astype(jnp.bfloat16)


def finish(dqs, partials):
    parts = len(dqs)
    rows, heads, size = dqs[0].shape
    _, kv_heads, kv_rows, _ = partials[0].shape
    kv_out = jax.ShapeDtypeStruct((kv_rows, kv_heads, size), jnp.bfloat16)
    operands = dict(enumerate(dqs)) | dict(zip(("own", "far", "even", "odd"), partials))
    return pl.pallas_call(
        functools.partial(finish_kernel, parts),
        out_shape=(
            jax.ShapeDtypeStruct((rows, heads * parts, size), jnp.bfloat16),
            kv_out,
            kv_out,
        ),
        in_specs=[_VMEM] * (parts + 4),
        out_specs=(_VMEM,) * 3,
        compiler_params=pltpu.CompilerParams(vmem_limit_bytes=VMEM_BYTES),
        name="finish",
    )(*[operands[name] for name in finish_order(parts)])


def shifted(block, distance):
    count = lax.axis_size("seq")
    return lax.ppermute(block, "seq", [(i, (i + distance) % count) for i in range(count)])


def paired(block):
    return lax.ppermute(block, "seq", [(i, i ^ 1) for i in range(lax.axis_size("seq"))])


def ringed(block, direction=1):
    count = lax.axis_size("seq")
    route = []
    for i in range(count):
        target = i + 2 if i % 2 == 0 else i - 2
        route.append((i, min(max(target, 0), count - 1))[::direction])
    return lax.ppermute(block, "seq", route)


def swapped(block, mask):
    return lax.ppermute(block, "kvh", [(i, i ^ mask) for i in range(lax.axis_size("kvh"))])


def local(queries, keys, values, output_gradient, doc_lengths, prefix_lengths):
    parts = lax.axis_size("kvh")
    kv, cots, ranges = prepare(
        doc_lengths, prefix_lengths, output_gradient, keys, values, parts
    )
    own, far = kv[0], shifted(kv[1], BACK)
    evens = [paired(block) for block in kv[2:]]
    odds = [ringed(block) for block in evens]
    cots = [cots[0]] + [swapped(cots[mask], mask) for mask in range(1, parts)]
    dqs, carried = {}, []
    for heads_here, masks in stages(parts, len(evens)):
        found, left = gradients(
            heads_here, masks, parts, ranges, queries, [cots[mask] for mask in masks], own, far,
            evens, [odds[head] for head in heads_here],
            list(carried),
        )
        carried = left
        for mask, dq in zip(masks, found):
            dqs[mask] = dq
    dqs = {mask: swapped(dq, mask) if mask else dq for mask, dq in dqs.items()}
    own, far_even, far_odd, even, odd = carried
    relayed = add(paired(odd), far_odd)
    partials = [own, ringed(far_even, -1), paired(even), ringed(relayed)]
    return finish([dqs[mask] for mask in range(parts)], partials)


def solution(mesh):
    in_specs = (
        P("seq", "kvh", None),
        P("seq", "kvh", None),
        P("seq", "kvh", None),
        P(("seq", "kvh"), None, None),
        P(),
        P(),
    )
    out_specs = (P(("seq", "kvh"), None, None), P("seq", "kvh", None), P("seq", "kvh", None))
    return jax.shard_map(local, mesh=mesh, in_specs=in_specs, out_specs=out_specs, check_vma=False)
```

```python
import functools

import jax
import jax.numpy as jnp
from jax import lax
from jax.experimental import pallas as pl
from jax.experimental.pallas import tpu as pltpu
from jax.sharding import PartitionSpec as P

BACK = 2
AHEAD = 1
LOG2E = 1.4426950408889634
VMEM_BYTES = 40 * 1024 * 1024
NEG = -1e30
TILE = 8

_VMEM = pl.BlockSpec(memory_space=pltpu.VMEM)
_SMEM = pl.BlockSpec(memory_space=pltpu.SMEM)
_HBM = pl.BlockSpec(memory_space=pltpu.HBM)


def stages(parts):
    rest = list(range(parts - 1, 1, -1))
    return [[0, 1, *rest[:-1]], rest[-1:]]


def regroup(buf):
    wide = buf[...].astype(jnp.float32)
    return [wide[:, group, :].astype(jnp.bfloat16) for group in range(buf.shape[1])]


def pack_kernel(key_ref, value_ref, *rest):
    kv_outs, (key_buf, value_buf, sems) = rest[:-3], rest[-3:]
    loads = []
    for number, (ref, buf) in enumerate(((key_ref, key_buf), (value_ref, value_buf))):
        loads.append(pltpu.make_async_copy(ref, buf, sems.at[number]))
        loads[-1].start()
    for number, buf in enumerate((key_buf, value_buf)):
        loads[number].wait()
        for group, block in enumerate(regroup(buf)):
            for kv_out in kv_outs:
                kv_out[number, group] = block


def pack(keys, values):
    kv_rows, kv_heads, size = keys.shape
    block = pltpu.VMEM((2, kv_heads, kv_rows, size), jnp.bfloat16)
    return pl.pallas_call(
        pack_kernel,
        out_shape=(block,) * 3,
        in_specs=[_HBM] * 2,
        out_specs=(_VMEM,) * 3,
        scratch_shapes=[
            pltpu.VMEM(keys.shape, jnp.bfloat16),
            pltpu.VMEM(values.shape, jnp.bfloat16),
            pltpu.SemaphoreType.DMA((2,)),
        ],
        compiler_params=pltpu.CompilerParams(vmem_limit_bytes=VMEM_BYTES),
        name="pack",
    )(*[pltpu.with_memory_space_constraint(array, pltpu.HBM) for array in (keys, values)])


def prep_kernel(parts, kv_rows, lengths_ref, prefixes_ref, cot_ref, kv_ref, *rest):
    cot_outs, (range_out, lengths, prefixes, sems, scalar_sems) = rest[:parts], rest[parts:]
    heads = cot_ref.shape[1] // parts
    me = lax.axis_index("kvh")
    scalars = [
        pltpu.make_async_copy(lengths_ref, lengths, scalar_sems.at[0]),
        pltpu.make_async_copy(prefixes_ref, prefixes, scalar_sems.at[1]),
    ]
    for copy in scalars:
        copy.start()
    copies = []
    for mask in range(parts):
        first = pl.multiple_of((me ^ mask) * heads, heads)
        copies.append(
            pltpu.make_async_copy(
                cot_ref.at[:, pl.ds(first, heads), :], cot_outs[mask], sems.at[mask]
            )
        )
        copies[-1].start()
    for copy in scalars:
        copy.wait()
    tokens = kv_rows // parts
    lanes = range_out.shape[2]
    lane_token = lax.broadcasted_iota(jnp.int32, (1, lanes), 1) // (lanes // tokens)
    shard = lax.axis_index("seq")
    for mask in range(parts):
        first = (me ^ mask) * tokens
        low, high = bounds(shard * kv_rows + first + lane_token, lengths, prefixes)
        origin = (shard - BACK) * kv_rows + first
        range_out[mask, 0:1, :] = low - origin
        range_out[mask, 1:2, :] = high - origin
    for copy in copies:
        copy.wait()


def prepare(lengths, prefixes, cotangent, kv, parts):
    rows, heads, size = cotangent.shape
    _, kv_heads, kv_rows, _ = kv.shape
    lanes = kv_rows // parts * (heads // parts // kv_heads)
    piece = pltpu.VMEM((rows, heads // parts, size), jnp.bfloat16)
    operands = [
        pltpu.with_memory_space_constraint(array, pltpu.HBM)
        for array in (lengths, prefixes, cotangent)
    ]
    outs = pl.pallas_call(
        functools.partial(prep_kernel, parts, kv_rows),
        out_shape=(piece,) * parts + (pltpu.VMEM((parts, 2, lanes), jnp.int32),),
        in_specs=[_HBM] * 3 + [pl.BlockSpec(memory_space=pl.ANY)],
        out_specs=(_VMEM,) * (parts + 1),
        scratch_shapes=[
            pltpu.SMEM(lengths.shape, jnp.int32),
            pltpu.SMEM(prefixes.shape, jnp.int32),
            pltpu.SemaphoreType.DMA((parts,)),
            pltpu.SemaphoreType.DMA((2,)),
        ],
        compiler_params=pltpu.CompilerParams(vmem_limit_bytes=VMEM_BYTES),
        name="prepare",
    )(*operands, kv)
    return outs[:-1], outs[-1]


def bounds(position, lengths, prefixes):
    docs = lengths.shape[0]

    def step(doc, carry):
        start, low, high = carry
        end = start + lengths[doc]
        inside = (position >= start) & (position < end)
        reach = jnp.minimum(end, jnp.maximum(position + 1, start + prefixes[doc]))
        return end, jnp.where(inside, start, low), jnp.where(inside, reach, high)

    zero = jnp.zeros_like(position)
    carry = (jnp.int32(0), zero, zero)
    if docs <= 16:
        for doc in range(docs):
            carry = step(doc, carry)
    else:
        carry = lax.fori_loop(0, docs, step, carry)
    return carry[1], carry[2]


def neighbour_slots(shard):
    odd = shard % 2
    ahead, behind = BACK + 1, BACK - 1
    return jnp.where(odd == 1, behind, ahead), jnp.where(odd == 1, ahead, behind)


def grad_kernel(masks, parts, is_first, is_last, range_ref, q_ref, *refs):
    refs = list(refs)
    kv_own, kv_even, kv_far, kv_odd = [refs.pop(0) for _ in range(4)]
    cots = [refs.pop(0) for _ in masks]
    carried = None if is_first else refs.pop(0)
    dqs = [refs.pop(0) for _ in masks]
    outs, (window, acc, score_buf, dprob_buf, prob_buf, dscore_buf) = refs[:-6], refs[-6:]
    rows, heads, size = q_ref.shape
    tokens = rows // parts
    kv_heads = kv_own.shape[1]
    group_size = heads // kv_heads
    span = (BACK + 1 + AHEAD) * rows
    reach = span - rows + tokens
    lanes = tokens * group_size
    scale = size ** (-0.5)
    shard = lax.axis_index("seq")
    me = lax.axis_index("kvh")

    even_slot, odd_slot = neighbour_slots(shard)
    for slot, ref in ((BACK, kv_own), (0, kv_far), (even_slot, kv_even), (odd_slot, kv_odd)):
        part = pl.ds(pl.multiple_of(slot * rows, rows), rows)
        for number in range(2):
            for group in range(kv_heads):
                window[number, group, part] = ref[number, group]
    acc[...] = jnp.zeros_like(acc) if is_first else carried[...]

    contract_last = (((1,), (1,)), ((), ()))
    contract_first = (((0,), (0,)), ((), ()))
    sublane = lax.broadcasted_iota(jnp.int32, (TILE, lanes), 0)
    items = [(place, group) for place in range(len(masks)) for group in range(kv_heads)]

    def operands(item):
        place, group = items[item]
        first = pl.multiple_of((me ^ masks[place]) * tokens, tokens)
        of_group = pl.ds(group * group_size, group_size)
        q = q_ref[pl.ds(first, tokens), of_group].astype(jnp.float32)
        cot = cots[place][:, of_group].astype(jnp.float32)
        return (
            pl.ds(first, reach),
            q.reshape(lanes, size).astype(jnp.bfloat16),
            cot.reshape(lanes, size).astype(jnp.bfloat16),
        )

    def scores_of(item):
        place, group = items[item]
        slot = item % 2
        here, q, cot = operands(item)
        scores = lax.dot_general(
            window[0, group, here], q, contract_last, preferred_element_type=jnp.float32
        )
        low = range_ref[masks[place], 0:1, :] - sublane
        high = range_ref[masks[place], 1:2, :] - sublane
        top = jnp.full((TILE, lanes), NEG, jnp.float32)
        for row in range(0, reach, TILE):
            visible = (low <= row) & (high > row)
            tile = jnp.where(visible, scores[row : row + TILE] * (scale * LOG2E), NEG)
            top = jnp.maximum(top, tile)
            score_buf[slot, row : row + TILE] = tile
        dprob_buf[slot] = lax.dot_general(
            window[1, group, here], cot, contract_last, preferred_element_type=jnp.float32
        )
        return jnp.max(top, axis=0, keepdims=True)

    def softmax_of(item, top):
        slot = item % 2
        total = jnp.zeros((TILE, lanes), jnp.float32)
        delta = jnp.zeros((TILE, lanes), jnp.float32)
        for row in range(0, reach, TILE):
            tile = slice(row, row + TILE)
            expo = jnp.exp2(score_buf[slot, tile] - top)
            total = total + expo
            delta = delta + expo * dprob_buf[slot, tile]
            score_buf[slot, tile] = expo
        inverse = 1.0 / jnp.sum(total, axis=0, keepdims=True)
        delta = jnp.sum(delta, axis=0, keepdims=True) * inverse
        for row in range(0, reach, 2 * TILE):
            tile = slice(row, row + 2 * TILE)
            probs = score_buf[slot, tile] * inverse
            dscores = probs * (dprob_buf[slot, tile] - delta)
            prob_buf[slot, tile] = probs.astype(jnp.bfloat16)
            dscore_buf[slot, tile] = dscores.astype(jnp.bfloat16)

    def gradients_of(item):
        place, group = items[item]
        slot = item % 2
        here, q, cot = operands(item)
        dscores = dscore_buf[slot]
        acc[1, group, here] += jnp.dot(prob_buf[slot], cot, preferred_element_type=jnp.float32)
        acc[0, group, here] += jnp.dot(dscores, q, preferred_element_type=jnp.float32)
        dq = lax.dot_general(
            window[0, group, here], dscores, contract_first, preferred_element_type=jnp.float32
        )
        dq = jnp.transpose(dq * scale).reshape(tokens, group_size, size)
        dqs[place][:, pl.ds(group * group_size, group_size)] = dq.astype(jnp.bfloat16)

    top = scores_of(0)
    for item in range(len(items)):
        later = scores_of(item + 1) if item + 1 < len(items) else None
        softmax_of(item, top)
        gradients_of(item)
        top = later

    if not is_last:
        outs[0][...] = acc[...]
        return
    is_odd = (shard % 2).astype(jnp.float32)
    weights = (1.0, 1.0 - is_odd, is_odd, 1.0, 1.0)
    for slot, weight, ref in zip((BACK, 0, 0, even_slot, odd_slot), weights, outs):
        part = pl.ds(pl.multiple_of(slot * rows, rows), rows)
        for group in range(kv_heads):
            ref[0, group] = (acc[0, group, part] * (scale * weight)).astype(ref.dtype)
            ref[1, group] = (acc[1, group, part] * weight).astype(ref.dtype)


def gradients(masks, parts, ranges, queries, cots, blocks, carried):
    rows, heads, size = queries.shape
    is_last = masks == stages(parts)[-1]
    kv_shape = blocks[0].shape
    kv_heads = kv_shape[1]
    span = (BACK + 1 + AHEAD) * rows
    acc_shape = (2, kv_heads, span, size)
    tokens = rows // parts
    tile_shape = (2, span - rows + tokens, tokens * (heads // kv_heads))
    work = heads * rows // parts * span * len(masks)
    outs = [pltpu.VMEM(cots[0].shape, jnp.bfloat16)] * len(masks)
    if is_last:
        outs += [pltpu.VMEM(kv_shape, jnp.float32)] + [pltpu.VMEM(kv_shape, jnp.bfloat16)] * 4
    else:
        outs += [pltpu.VMEM(acc_shape, jnp.float32)]
    own, far, even, odd = blocks
    operands = [ranges, queries, own, even, far, odd, *cots]
    operands += [] if carried is None else [carried]
    outs = pl.pallas_call(
        functools.partial(grad_kernel, masks, parts, carried is None, is_last),
        out_shape=tuple(outs),
        in_specs=[_VMEM] * len(operands),
        out_specs=(_VMEM,) * len(outs),
        scratch_shapes=[
            pltpu.VMEM(acc_shape, jnp.bfloat16),
            pltpu.VMEM(acc_shape, jnp.float32),
            pltpu.VMEM(tile_shape, jnp.float32),
            pltpu.VMEM(tile_shape, jnp.float32),
            pltpu.VMEM(tile_shape, jnp.bfloat16),
            pltpu.VMEM(tile_shape, jnp.bfloat16),
        ],
        compiler_params=pltpu.CompilerParams(vmem_limit_bytes=VMEM_BYTES),
        cost_estimate=pl.CostEstimate(
            flops=10 * work * size, bytes_accessed=4 * queries.size * 2, transcendentals=work
        ),
        name="gradients",
    )(*operands)
    return outs[: len(masks)], outs[len(masks) :]


def add_kernel(left, right, out):
    out[...] = (left[...].astype(jnp.float32) + right[...].astype(jnp.float32)).astype(out.dtype)


def add(left, right):
    return pl.pallas_call(
        add_kernel,
        out_shape=pltpu.VMEM(left.shape, left.dtype),
        in_specs=[_VMEM] * 2,
        out_specs=_VMEM,
        compiler_params=pltpu.CompilerParams(vmem_limit_bytes=VMEM_BYTES),
        name="add",
    )(left, right)


def finish_order(parts):
    return [1, "odd", "far", *range(2, parts - 1), "even", parts - 1, 0, "own"]


def finish_kernel(parts, *refs):
    *refs, dq_out, dk_out, dv_out, dk_buf, dv_buf, sems = refs
    refs = dict(zip(finish_order(parts), refs))
    heads = refs[0].shape[1]
    me = lax.axis_index("kvh")
    copies = []
    for mask in range(parts):
        first = pl.multiple_of((me ^ mask) * heads, heads)
        copies.append(
            pltpu.make_async_copy(refs[mask], dq_out.at[:, pl.ds(first, heads), :], sems.at[mask])
        )
        copies[-1].start()
    for number, (buf, ref) in enumerate(((dk_buf, dk_out), (dv_buf, dv_out))):
        sums = []
        for group in range(buf.shape[1]):
            total = refs["own"][number, group]
            for name in ("far", "even", "odd"):
                total = total + refs[name][number, group].astype(jnp.float32)
            sums.append(total)
        buf[...] = jnp.stack(sums, axis=1).astype(jnp.bfloat16)
        copies.append(pltpu.make_async_copy(buf, ref, sems.at[parts + number]))
        copies[-1].start()
    for copy in copies:
        copy.wait()


def finish(dqs, partials):
    parts = len(dqs)
    rows, heads, size = dqs[0].shape
    _, kv_heads, kv_rows, _ = partials[0].shape
    kv_shape = (kv_rows, kv_heads, size)
    kv_out = jax.ShapeDtypeStruct(kv_shape, jnp.bfloat16)
    operands = dict(enumerate(dqs)) | dict(zip(("own", "far", "even", "odd"), partials))
    return pl.pallas_call(
        functools.partial(finish_kernel, parts),
        out_shape=(
            jax.ShapeDtypeStruct((rows, heads * parts, size), jnp.bfloat16),
            kv_out,
            kv_out,
        ),
        in_specs=[_VMEM] * (parts + 4),
        out_specs=(_HBM,) * 3,
        scratch_shapes=[
            pltpu.VMEM(kv_shape, jnp.bfloat16),
            pltpu.VMEM(kv_shape, jnp.bfloat16),
            pltpu.SemaphoreType.DMA((parts + 2,)),
        ],
        compiler_params=pltpu.CompilerParams(vmem_limit_bytes=VMEM_BYTES),
        name="finish",
    )(*[operands[name] for name in finish_order(parts)])


def shifted(block, distance):
    count = lax.axis_size("seq")
    return lax.ppermute(block, "seq", [(i, (i + distance) % count) for i in range(count)])


def paired(block):
    return lax.ppermute(block, "seq", [(i, i ^ 1) for i in range(lax.axis_size("seq"))])


def ringed(block, direction=1):
    count = lax.axis_size("seq")
    route = []
    for i in range(count):
        target = i + 2 if i % 2 == 0 else i - 2
        route.append((i, min(max(target, 0), count - 1))[::direction])
    return lax.ppermute(block, "seq", route)


def swapped(block, mask):
    return lax.ppermute(block, "kvh", [(i, i ^ mask) for i in range(lax.axis_size("kvh"))])


def local(queries, keys, values, output_gradient, doc_lengths, prefix_lengths):
    parts = lax.axis_size("kvh")
    kv = pack(keys, values)
    cots, ranges = prepare(doc_lengths, prefix_lengths, output_gradient, kv[0], parts)
    even = paired(kv[2])
    blocks = [kv[0], shifted(kv[1], BACK), even, ringed(even)]
    cots = [cots[0]] + [swapped(cots[mask], mask) for mask in range(1, parts)]
    dqs, carried = {}, [None]
    for masks in stages(parts):
        found, carried = gradients(
            masks, parts, ranges, queries, [cots[mask] for mask in masks], blocks, carried[0]
        )
        for mask, dq in zip(masks, found):
            dqs[mask] = swapped(dq, mask) if mask else dq
    own, far_even, far_odd, even, odd = carried
    relayed = add(paired(odd), far_odd)
    partials = [own, ringed(far_even, -1), paired(even), ringed(relayed)]
    return finish([dqs[mask] for mask in range(parts)], partials)


def solution(mesh):
    in_specs = (
        P("seq", "kvh", None),
        P("seq", "kvh", None),
        P("seq", "kvh", None),
        P(("seq", "kvh"), None, None),
        P(),
        P(),
    )
    out_specs = (P(("seq", "kvh"), None, None), P("seq", "kvh", None), P("seq", "kvh", None))
    return jax.shard_map(local, mesh=mesh, in_specs=in_specs, out_specs=out_specs, check_vma=False)
```

```python
import functools

import jax
import jax.numpy as jnp
from jax import lax
from jax.experimental import pallas as pl
from jax.experimental.pallas import tpu as pltpu
from jax.sharding import PartitionSpec as P

BACK = 2
AHEAD = 1
LOG2E = 1.4426950408889634
VMEM_BYTES = 40 * 1024 * 1024
NEG = -1e30
TILE = 8
ALIGN = 16
WIDTHS = (160, 288)

_VMEM = pl.BlockSpec(memory_space=pltpu.VMEM)
_SMEM = pl.BlockSpec(memory_space=pltpu.SMEM)
_HBM = pl.BlockSpec(memory_space=pltpu.HBM)


def stages(parts):
    rest = list(range(parts - 1, 1, -1))
    return [[0, 1, *rest[:-1]], rest[-1:]]


def regroup(buf):
    wide = buf[...].astype(jnp.float32)
    return [wide[:, group, :].astype(jnp.bfloat16) for group in range(buf.shape[1])]


def prep_kernel(parts, lengths_ref, prefixes_ref, cot_ref, key_ref, value_ref, *rest):
    kv_outs, cot_outs, rest = rest[:3], rest[3 : parts + 3], rest[parts + 3 :]
    range_out, key_buf, value_buf, lengths, prefixes, sems, scalar_sems = rest
    heads = cot_ref.shape[1] // parts
    me = lax.axis_index("kvh")
    scalars = [
        pltpu.make_async_copy(lengths_ref, lengths, scalar_sems.at[0]),
        pltpu.make_async_copy(prefixes_ref, prefixes, scalar_sems.at[1]),
    ]
    for copy in scalars:
        copy.start()
    loads = []
    for number, (ref, buf) in enumerate(((key_ref, key_buf), (value_ref, value_buf))):
        loads.append(pltpu.make_async_copy(ref, buf, sems.at[number]))
        loads[-1].start()
    copies = []
    for mask in range(parts):
        first = pl.multiple_of((me ^ mask) * heads, heads)
        copies.append(
            pltpu.make_async_copy(
                cot_ref.at[:, pl.ds(first, heads), :], cot_outs[mask], sems.at[mask + 2]
            )
        )
        copies[-1].start()
    for number, buf in enumerate((key_buf, value_buf)):
        loads[number].wait()
        for group, block in enumerate(regroup(buf)):
            for kv_out in kv_outs:
                kv_out[number, group] = block
    for copy in scalars:
        copy.wait()
    rows = key_buf.shape[0]
    tokens = rows // parts
    lanes = range_out.shape[2]
    lane_token = lax.broadcasted_iota(jnp.int32, (1, lanes), 1) // (lanes // tokens)
    shard = lax.axis_index("seq")
    for mask in range(parts):
        first = (me ^ mask) * tokens
        low, high = bounds(shard * rows + first + lane_token, lengths, prefixes)
        origin = (shard - BACK) * rows + first
        range_out[mask, 0:1, :] = low - origin
        range_out[mask, 1:2, :] = high - origin
    for copy in copies:
        copy.wait()


def prepare(lengths, prefixes, cotangent, keys, values, parts):
    rows, heads, size = cotangent.shape
    kv_rows, kv_heads, _ = keys.shape
    lanes = kv_rows // parts * (heads // parts // kv_heads)
    piece = pltpu.VMEM((rows, heads // parts, size), jnp.bfloat16)
    block = pltpu.VMEM((2, kv_heads, kv_rows, size), jnp.bfloat16)
    operands = [
        pltpu.with_memory_space_constraint(array, pltpu.HBM)
        for array in (lengths, prefixes, cotangent, keys, values)
    ]
    outs = pl.pallas_call(
        functools.partial(prep_kernel, parts),
        out_shape=(block,) * 3 + (piece,) * parts + (pltpu.VMEM((parts, 2, lanes), jnp.int32),),
        in_specs=[_HBM] * 5,
        out_specs=(_VMEM,) * (parts + 4),
        scratch_shapes=[
            pltpu.VMEM(keys.shape, jnp.bfloat16),
            pltpu.VMEM(values.shape, jnp.bfloat16),
            pltpu.SMEM(lengths.shape, jnp.int32),
            pltpu.SMEM(prefixes.shape, jnp.int32),
            pltpu.SemaphoreType.DMA((parts + 2,)),
            pltpu.SemaphoreType.DMA((2,)),
        ],
        compiler_params=pltpu.CompilerParams(vmem_limit_bytes=VMEM_BYTES),
        name="prepare",
    )(*operands)
    return outs[:3], outs[3:-1], outs[-1]


def bounds(position, lengths, prefixes):
    docs = lengths.shape[0]

    def step(doc, carry):
        start, low, high = carry
        end = start + lengths[doc]
        inside = (position >= start) & (position < end)
        reach = jnp.minimum(end, jnp.maximum(position + 1, start + prefixes[doc]))
        return end, jnp.where(inside, start, low), jnp.where(inside, reach, high)

    zero = jnp.zeros_like(position)
    carry = (jnp.int32(0), zero, zero)
    if docs <= 16:
        for doc in range(docs):
            carry = step(doc, carry)
    else:
        carry = lax.fori_loop(0, docs, step, carry)
    return carry[1], carry[2]


def neighbour_slots(shard):
    odd = shard % 2
    ahead, behind = BACK + 1, BACK - 1
    return jnp.where(odd == 1, behind, ahead), jnp.where(odd == 1, ahead, behind)


def grad_kernel(masks, parts, is_first, is_last, range_ref, q_ref, *refs):
    refs = list(refs)
    kv_own, kv_even, kv_far, kv_odd = [refs.pop(0) for _ in range(4)]
    cots = [refs.pop(0) for _ in masks]
    carried = None if is_first else refs.pop(0)
    dqs = [refs.pop(0) for _ in masks]
    outs, (window, acc, score_buf, dprob_buf, prob_buf, dscore_buf) = refs[:-6], refs[-6:]
    rows, heads, size = q_ref.shape
    tokens = rows // parts
    kv_heads = kv_own.shape[1]
    group_size = heads // kv_heads
    span = (BACK + 1 + AHEAD) * rows
    reach = span - rows + tokens
    lanes = tokens * group_size
    scale = size ** (-0.5)
    shard = lax.axis_index("seq")
    me = lax.axis_index("kvh")

    even_slot, odd_slot = neighbour_slots(shard)
    for slot, ref in ((BACK, kv_own), (0, kv_far), (even_slot, kv_even), (odd_slot, kv_odd)):
        part = pl.ds(pl.multiple_of(slot * rows, rows), rows)
        for number in range(2):
            for group in range(kv_heads):
                window[number, group, part] = ref[number, group]
    acc[...] = jnp.zeros_like(acc) if is_first else carried[...]

    contract_last = (((1,), (1,)), ((), ()))
    contract_first = (((0,), (0,)), ((), ()))
    sublane = lax.broadcasted_iota(jnp.int32, (TILE, lanes), 0)
    items = [(place, group) for place in range(len(masks)) for group in range(kv_heads)]

    def operands(item, starts, width):
        place, group = items[item]
        first = pl.multiple_of((me ^ masks[place]) * tokens, tokens)
        of_group = pl.ds(group * group_size, group_size)
        q = q_ref[pl.ds(first, tokens), of_group].astype(jnp.float32)
        cot = cots[place][:, of_group].astype(jnp.float32)
        return (
            pl.ds(pl.multiple_of(first + starts[place], ALIGN), width),
            q.reshape(lanes, size).astype(jnp.bfloat16),
            cot.reshape(lanes, size).astype(jnp.bfloat16),
        )

    def scores_of(item, starts, width):
        place, group = items[item]
        slot = item % 2
        here, q, cot = operands(item, starts, width)
        scores = lax.dot_general(
            window[0, group, here], q, contract_last, preferred_element_type=jnp.float32
        )
        low = range_ref[masks[place], 0:1, :] - starts[place] - sublane
        high = range_ref[masks[place], 1:2, :] - starts[place] - sublane
        top = jnp.full((TILE, lanes), NEG, jnp.float32)
        for row in range(0, width, TILE):
            visible = (low <= row) & (high > row)
            tile = jnp.where(visible, scores[row : row + TILE] * (scale * LOG2E), NEG)
            top = jnp.maximum(top, tile)
            score_buf[slot, row : row + TILE] = tile
        dprob_buf[slot, :width] = lax.dot_general(
            window[1, group, here], cot, contract_last, preferred_element_type=jnp.float32
        )
        return jnp.max(top, axis=0, keepdims=True)

    def softmax_of(item, top, width):
        slot = item % 2
        total = jnp.zeros((TILE, lanes), jnp.float32)
        delta = jnp.zeros((TILE, lanes), jnp.float32)
        for row in range(0, width, TILE):
            tile = slice(row, row + TILE)
            expo = jnp.exp2(score_buf[slot, tile] - top)
            total = total + expo
            delta = delta + expo * dprob_buf[slot, tile]
            score_buf[slot, tile] = expo
        inverse = 1.0 / jnp.sum(total, axis=0, keepdims=True)
        delta = jnp.sum(delta, axis=0, keepdims=True) * inverse
        for row in range(0, width, 2 * TILE):
            tile = slice(row, row + 2 * TILE)
            probs = score_buf[slot, tile] * inverse
            dscores = probs * (dprob_buf[slot, tile] - delta)
            prob_buf[slot, tile] = probs.astype(jnp.bfloat16)
            dscore_buf[slot, tile] = dscores.astype(jnp.bfloat16)

    def gradients_of(item, starts, width):
        place, group = items[item]
        slot = item % 2
        here, q, cot = operands(item, starts, width)
        probs, dscores = prob_buf[slot, :width], dscore_buf[slot, :width]
        acc[1, group, here] += jnp.dot(probs, cot, preferred_element_type=jnp.float32)
        acc[0, group, here] += jnp.dot(dscores, q, preferred_element_type=jnp.float32)
        dq = lax.dot_general(
            window[0, group, here], dscores, contract_first, preferred_element_type=jnp.float32
        )
        dq = jnp.transpose(dq * scale).reshape(tokens, group_size, size)
        dqs[place][:, pl.ds(group * group_size, group_size)] = dq.astype(jnp.bfloat16)

    lowest = [jnp.min(range_ref[mask, 0:1, :]) & -ALIGN for mask in masks]
    needed = [jnp.max(range_ref[mask, 1:2, :]) - low for mask, low in zip(masks, lowest)]
    needed = functools.reduce(jnp.maximum, needed)

    def all_items(width):
        starts = [jnp.clip(low, 0, reach - width) for low in lowest]
        top = scores_of(0, starts, width)
        for item in range(len(items)):
            later = scores_of(item + 1, starts, width) if item + 1 < len(items) else None
            softmax_of(item, top, width)
            gradients_of(item, starts, width)
            top = later

    widths = [width for width in WIDTHS if width < reach] + [reach]
    for floor, width in zip([-1] + widths, widths):
        fits = needed > floor
        if width < reach:
            fits = fits & (needed <= width)
        pl.when(fits)(functools.partial(all_items, width))

    if not is_last:
        outs[0][...] = acc[...]
        return
    is_odd = (shard % 2).astype(jnp.float32)
    weights = (1.0, 1.0 - is_odd, is_odd, 1.0, 1.0)
    for slot, weight, ref in zip((BACK, 0, 0, even_slot, odd_slot), weights, outs):
        part = pl.ds(pl.multiple_of(slot * rows, rows), rows)
        for group in range(kv_heads):
            ref[0, group] = (acc[0, group, part] * (scale * weight)).astype(ref.dtype)
            ref[1, group] = (acc[1, group, part] * weight).astype(ref.dtype)


def gradients(masks, parts, ranges, queries, cots, blocks, carried):
    rows, heads, size = queries.shape
    is_last = masks == stages(parts)[-1]
    kv_shape = blocks[0].shape
    kv_heads = kv_shape[1]
    span = (BACK + 1 + AHEAD) * rows
    acc_shape = (2, kv_heads, span, size)
    tokens = rows // parts
    tile_shape = (2, span - rows + tokens, tokens * (heads // kv_heads))
    work = heads * rows // parts * span * len(masks)
    outs = [pltpu.VMEM(cots[0].shape, jnp.bfloat16)] * len(masks)
    if is_last:
        outs += [pltpu.VMEM(kv_shape, jnp.float32)] + [pltpu.VMEM(kv_shape, jnp.bfloat16)] * 4
    else:
        outs += [pltpu.VMEM(acc_shape, jnp.float32)]
    own, far, even, odd = blocks
    operands = [ranges, queries, own, even, far, odd, *cots]
    operands += [] if carried is None else [carried]
    outs = pl.pallas_call(
        functools.partial(grad_kernel, masks, parts, carried is None, is_last),
        out_shape=tuple(outs),
        in_specs=[_VMEM] * len(operands),
        out_specs=(_VMEM,) * len(outs),
        scratch_shapes=[
            pltpu.VMEM(acc_shape, jnp.bfloat16),
            pltpu.VMEM(acc_shape, jnp.float32),
            pltpu.VMEM(tile_shape, jnp.float32),
            pltpu.VMEM(tile_shape, jnp.float32),
            pltpu.VMEM(tile_shape, jnp.bfloat16),
            pltpu.VMEM(tile_shape, jnp.bfloat16),
        ],
        compiler_params=pltpu.CompilerParams(vmem_limit_bytes=VMEM_BYTES),
        cost_estimate=pl.CostEstimate(
            flops=10 * work * size, bytes_accessed=4 * queries.size * 2, transcendentals=work
        ),
        name="gradients",
    )(*operands)
    return outs[: len(masks)], outs[len(masks) :]


def add_kernel(left, right, out):
    out[...] = (left[...].astype(jnp.float32) + right[...].astype(jnp.float32)).astype(out.dtype)


def add(left, right):
    return pl.pallas_call(
        add_kernel,
        out_shape=pltpu.VMEM(left.shape, left.dtype),
        in_specs=[_VMEM] * 2,
        out_specs=_VMEM,
        compiler_params=pltpu.CompilerParams(vmem_limit_bytes=VMEM_BYTES),
        name="add",
    )(left, right)


def finish_order(parts):
    return [1, "odd", "far", *range(2, parts - 1), "even", parts - 1, 0, "own"]


def finish_kernel(parts, *refs):
    *refs, dq_out, dk_out, dv_out = refs
    refs = dict(zip(finish_order(parts), refs))
    dqs = [refs[mask] for mask in range(parts)]
    own, far, even, odd = [refs[name] for name in ("own", "far", "even", "odd")]
    heads = dqs[0].shape[1]
    me = lax.axis_index("kvh")
    for mask in range(parts):
        first = pl.multiple_of((me ^ mask) * heads, heads)
        dq_out[:, pl.ds(first, heads), :] = dqs[mask][...]
    for number, ref in enumerate((dk_out, dv_out)):
        sums = []
        for group in range(ref.shape[1]):
            total = own[number, group]
            for other in (far, even, odd):
                total = total + other[number, group].astype(jnp.float32)
            sums.append(total)
        ref[...] = jnp.stack(sums, axis=1).astype(jnp.bfloat16)


def finish(dqs, partials):
    parts = len(dqs)
    rows, heads, size = dqs[0].shape
    _, kv_heads, kv_rows, _ = partials[0].shape
    kv_out = jax.ShapeDtypeStruct((kv_rows, kv_heads, size), jnp.bfloat16)
    operands = dict(enumerate(dqs)) | dict(zip(("own", "far", "even", "odd"), partials))
    return pl.pallas_call(
        functools.partial(finish_kernel, parts),
        out_shape=(
            jax.ShapeDtypeStruct((rows, heads * parts, size), jnp.bfloat16),
            kv_out,
            kv_out,
        ),
        in_specs=[_VMEM] * (parts + 4),
        out_specs=(_VMEM,) * 3,
        compiler_params=pltpu.CompilerParams(vmem_limit_bytes=VMEM_BYTES),
        name="finish",
    )(*[operands[name] for name in finish_order(parts)])


def shifted(block, distance):
    devices = range(lax.axis_size("seq"))
    route = [(i, i + distance) for i in devices if i + distance in devices]
    return lax.ppermute(block, "seq", route)


def paired(block):
    return lax.ppermute(block, "seq", [(i, i ^ 1) for i in range(lax.axis_size("seq"))])


def ringed(block, direction=1):
    count = lax.axis_size("seq")
    route = []
    for i in range(count):
        target = i + 2 if i % 2 == 0 else i - 2
        route.append((i, min(max(target, 0), count - 1))[::direction])
    return lax.ppermute(block, "seq", route)


def swapped(block, mask):
    return lax.ppermute(block, "kvh", [(i, i ^ mask) for i in range(lax.axis_size("kvh"))])


def local(queries, keys, values, output_gradient, doc_lengths, prefix_lengths):
    parts = lax.axis_size("kvh")
    kv, cots, ranges = prepare(
        doc_lengths, prefix_lengths, output_gradient, keys, values, parts
    )
    even = paired(kv[2])
    blocks = [kv[0], shifted(kv[1], BACK), even, ringed(even)]
    cots = [cots[0]] + [swapped(cots[mask], mask) for mask in range(1, parts)]
    dqs, carried = {}, [None]
    for masks in stages(parts):
        found, carried = gradients(
            masks, parts, ranges, queries, [cots[mask] for mask in masks], blocks, carried[0]
        )
        for mask, dq in zip(masks, found):
            dqs[mask] = swapped(dq, mask) if mask else dq
    own, far_even, far_odd, even, odd = carried
    relayed = add(paired(odd), far_odd)
    partials = [own, ringed(far_even, -1), paired(even), ringed(relayed)]
    return finish([dqs[mask] for mask in range(parts)], partials)


def solution(mesh):
    in_specs = (
        P("seq", "kvh", None),
        P("seq", "kvh", None),
        P("seq", "kvh", None),
        P(("seq", "kvh"), None, None),
        P(),
        P(),
    )
    out_specs = (P(("seq", "kvh"), None, None), P("seq", "kvh", None), P("seq", "kvh", None))
    return jax.shard_map(local, mesh=mesh, in_specs=in_specs, out_specs=out_specs, check_vma=False)
```

```python
import functools

import jax
import jax.numpy as jnp
from jax import lax
from jax.experimental import pallas as pl
from jax.experimental.pallas import tpu as pltpu
from jax.sharding import PartitionSpec as P

BACK = 2
AHEAD = 1
LOG2E = 1.4426950408889634
VMEM_BYTES = 40 * 1024 * 1024
NEG = -1e30
TILE = 8
ALIGN = 16
WIDTHS = (176, 304)

_VMEM = pl.BlockSpec(memory_space=pltpu.VMEM)
_SMEM = pl.BlockSpec(memory_space=pltpu.SMEM)
_HBM = pl.BlockSpec(memory_space=pltpu.HBM)


def stages(parts):
    rest = list(range(parts - 1, 1, -1))
    return [[0, 1, *rest[:-1]], rest[-1:]]


def regroup(buf):
    wide = buf[...].astype(jnp.float32)
    return [wide[:, group, :].astype(jnp.bfloat16) for group in range(buf.shape[1])]


def prep_kernel(parts, lengths_ref, prefixes_ref, cot_ref, key_ref, value_ref, *rest):
    kv_outs, cot_outs, rest = rest[:2], rest[2 : parts + 2], rest[parts + 2 :]
    range_out, key_buf, value_buf, lengths, prefixes, sems, scalar_sems = rest
    heads = cot_ref.shape[1] // parts
    me = lax.axis_index("kvh")
    scalars = [
        pltpu.make_async_copy(lengths_ref, lengths, scalar_sems.at[0]),
        pltpu.make_async_copy(prefixes_ref, prefixes, scalar_sems.at[1]),
    ]
    for copy in scalars:
        copy.start()
    loads = []
    for number, (ref, buf) in enumerate(((key_ref, key_buf), (value_ref, value_buf))):
        loads.append(pltpu.make_async_copy(ref, buf, sems.at[number]))
        loads[-1].start()
    copies = []
    for mask in range(parts):
        first = pl.multiple_of((me ^ mask) * heads, heads)
        copies.append(
            pltpu.make_async_copy(
                cot_ref.at[:, pl.ds(first, heads), :], cot_outs[mask], sems.at[mask + 2]
            )
        )
        copies[-1].start()
    for number, buf in enumerate((key_buf, value_buf)):
        loads[number].wait()
        for group, block in enumerate(regroup(buf)):
            for kv_out in kv_outs:
                kv_out[number, group] = block
    for copy in scalars:
        copy.wait()
    rows = key_buf.shape[0]
    tokens = rows // parts
    lanes = range_out.shape[2]
    lane_token = lax.broadcasted_iota(jnp.int32, (1, lanes), 1) // (lanes // tokens)
    shard = lax.axis_index("seq")
    for mask in range(parts):
        first = (me ^ mask) * tokens
        low, high = bounds(shard * rows + first + lane_token, lengths, prefixes)
        origin = (shard - BACK) * rows + first
        range_out[mask, 0:1, :] = low - origin
        range_out[mask, 1:2, :] = high - origin
    for copy in copies:
        copy.wait()


def prepare(lengths, prefixes, cotangent, keys, values, parts):
    rows, heads, size = cotangent.shape
    kv_rows, kv_heads, _ = keys.shape
    lanes = kv_rows // parts * (heads // parts // kv_heads)
    piece = pltpu.VMEM((rows, heads // parts, size), jnp.bfloat16)
    block = pltpu.VMEM((2, kv_heads, kv_rows, size), jnp.bfloat16)
    operands = [
        pltpu.with_memory_space_constraint(array, pltpu.HBM)
        for array in (lengths, prefixes, cotangent, keys, values)
    ]
    outs = pl.pallas_call(
        functools.partial(prep_kernel, parts),
        out_shape=(block,) * 2 + (piece,) * parts + (pltpu.VMEM((parts, 2, lanes), jnp.int32),),
        in_specs=[_HBM] * 5,
        out_specs=(_VMEM,) * (parts + 3),
        scratch_shapes=[
            pltpu.VMEM(keys.shape, jnp.bfloat16),
            pltpu.VMEM(values.shape, jnp.bfloat16),
            pltpu.SMEM(lengths.shape, jnp.int32),
            pltpu.SMEM(prefixes.shape, jnp.int32),
            pltpu.SemaphoreType.DMA((parts + 2,)),
            pltpu.SemaphoreType.DMA((2,)),
        ],
        compiler_params=pltpu.CompilerParams(vmem_limit_bytes=VMEM_BYTES),
        name="prepare",
    )(*operands)
    return outs[:2], outs[2:-1], outs[-1]


def pack_kernel(key_ref, value_ref, out):
    for number, ref in enumerate((key_ref, value_ref)):
        for group, block in enumerate(regroup(ref)):
            out[number, group] = block


def pack(keys, values):
    kv_rows, kv_heads, size = keys.shape
    return pl.pallas_call(
        pack_kernel,
        out_shape=pltpu.VMEM((2, kv_heads, kv_rows, size), jnp.bfloat16),
        in_specs=[_VMEM] * 2,
        out_specs=_VMEM,
        compiler_params=pltpu.CompilerParams(vmem_limit_bytes=VMEM_BYTES),
        name="pack",
    )(keys, values)


def bounds(position, lengths, prefixes):
    docs = lengths.shape[0]

    def step(doc, carry):
        start, low, high = carry
        end = start + lengths[doc]
        inside = (position >= start) & (position < end)
        reach = jnp.minimum(end, jnp.maximum(position + 1, start + prefixes[doc]))
        return end, jnp.where(inside, start, low), jnp.where(inside, reach, high)

    zero = jnp.zeros_like(position)
    carry = (jnp.int32(0), zero, zero)
    if docs <= 16:
        for doc in range(docs):
            carry = step(doc, carry)
    else:
        carry = lax.fori_loop(0, docs, step, carry)
    return carry[1], carry[2]


def neighbour_slots(shard):
    odd = shard % 2
    ahead, behind = BACK + 1, BACK - 1
    return jnp.where(odd == 1, behind, ahead), jnp.where(odd == 1, ahead, behind)


def grad_kernel(masks, parts, is_first, is_last, range_ref, q_ref, *refs):
    refs = list(refs)
    kv_own, kv_even, kv_far, kv_odd = [refs.pop(0) for _ in range(4)]
    cots = [refs.pop(0) for _ in masks]
    carried = None if is_first else refs.pop(0)
    dqs = [refs.pop(0) for _ in masks]
    outs, (window, acc, score_buf, dprob_buf, prob_buf, dscore_buf) = refs[:-6], refs[-6:]
    rows, heads, size = q_ref.shape
    tokens = rows // parts
    kv_heads = kv_own.shape[1]
    group_size = heads // kv_heads
    span = (BACK + 1 + AHEAD) * rows
    reach = span - rows + tokens
    lanes = tokens * group_size
    scale = size ** (-0.5)
    shard = lax.axis_index("seq")
    me = lax.axis_index("kvh")

    even_slot, odd_slot = neighbour_slots(shard)
    for slot, ref in ((BACK, kv_own), (0, kv_far), (even_slot, kv_even), (odd_slot, kv_odd)):
        part = pl.ds(pl.multiple_of(slot * rows, rows), rows)
        for number in range(2):
            for group in range(kv_heads):
                window[number, group, part] = ref[number, group]
    acc[...] = jnp.zeros_like(acc) if is_first else carried[...]

    contract_last = (((1,), (1,)), ((), ()))
    contract_first = (((0,), (0,)), ((), ()))
    sublane = lax.broadcasted_iota(jnp.int32, (TILE, lanes), 0)
    items = [(place, group) for place in range(len(masks)) for group in range(kv_heads)]

    def operands(item, starts, width):
        place, group = items[item]
        first = pl.multiple_of((me ^ masks[place]) * tokens, tokens)
        of_group = pl.ds(group * group_size, group_size)
        q = q_ref[pl.ds(first, tokens), of_group].astype(jnp.float32)
        cot = cots[place][:, of_group].astype(jnp.float32)
        return (
            pl.ds(pl.multiple_of(first + starts[place], ALIGN), width),
            q.reshape(lanes, size).astype(jnp.bfloat16),
            cot.reshape(lanes, size).astype(jnp.bfloat16),
        )

    def scores_of(item, starts, width):
        place, group = items[item]
        slot = item % 2
        here, q, cot = operands(item, starts, width)
        scores = lax.dot_general(
            window[0, group, here], q, contract_last, preferred_element_type=jnp.float32
        )
        low = range_ref[masks[place], 0:1, :] - starts[place] - sublane
        high = range_ref[masks[place], 1:2, :] - starts[place] - sublane
        top = jnp.full((TILE, lanes), NEG, jnp.float32)
        for row in range(0, width, TILE):
            visible = (low <= row) & (high > row)
            tile = jnp.where(visible, scores[row : row + TILE] * (scale * LOG2E), NEG)
            top = jnp.maximum(top, tile)
            score_buf[slot, row : row + TILE] = tile
        dprob_buf[slot, :width] = lax.dot_general(
            window[1, group, here], cot, contract_last, preferred_element_type=jnp.float32
        )
        return jnp.max(top, axis=0, keepdims=True)

    def softmax_of(item, top, width):
        slot = item % 2
        total = jnp.zeros((TILE, lanes), jnp.float32)
        delta = jnp.zeros((TILE, lanes), jnp.float32)
        for row in range(0, width, TILE):
            tile = slice(row, row + TILE)
            expo = jnp.exp2(score_buf[slot, tile] - top)
            total = total + expo
            delta = delta + expo * dprob_buf[slot, tile]
            score_buf[slot, tile] = expo
        inverse = 1.0 / jnp.sum(total, axis=0, keepdims=True)
        delta = jnp.sum(delta, axis=0, keepdims=True) * inverse
        for row in range(0, width, 2 * TILE):
            tile = slice(row, row + 2 * TILE)
            probs = score_buf[slot, tile] * inverse
            dscores = probs * (dprob_buf[slot, tile] - delta)
            prob_buf[slot, tile] = probs.astype(jnp.bfloat16)
            dscore_buf[slot, tile] = dscores.astype(jnp.bfloat16)

    def gradients_of(item, starts, width):
        place, group = items[item]
        slot = item % 2
        here, q, cot = operands(item, starts, width)
        probs, dscores = prob_buf[slot, :width], dscore_buf[slot, :width]
        acc[1, group, here] += jnp.dot(probs, cot, preferred_element_type=jnp.float32)
        acc[0, group, here] += jnp.dot(dscores, q, preferred_element_type=jnp.float32)
        dq = lax.dot_general(
            window[0, group, here], dscores, contract_first, preferred_element_type=jnp.float32
        )
        dq = jnp.transpose(dq * scale).reshape(tokens, group_size, size)
        dqs[place][:, pl.ds(group * group_size, group_size)] = dq.astype(jnp.bfloat16)

    lowest = [jnp.min(range_ref[mask, 0:1, :]) & -ALIGN for mask in masks]
    needed = [jnp.max(range_ref[mask, 1:2, :]) - low for mask, low in zip(masks, lowest)]
    needed = functools.reduce(jnp.maximum, needed)

    def all_items(width):
        starts = [jnp.clip(low, 0, reach - width) for low in lowest]
        top = scores_of(0, starts, width)
        for item in range(len(items)):
            later = scores_of(item + 1, starts, width) if item + 1 < len(items) else None
            softmax_of(item, top, width)
            gradients_of(item, starts, width)
            top = later

    widths = [width for width in WIDTHS if width < reach] + [reach]
    for floor, width in zip([-1] + widths, widths):
        fits = needed > floor
        if width < reach:
            fits = fits & (needed <= width)
        pl.when(fits)(functools.partial(all_items, width))

    if not is_last:
        outs[0][...] = acc[...]
        return
    is_odd = (shard % 2).astype(jnp.float32)
    weights = (1.0, 1.0 - is_odd, is_odd, 1.0, 1.0)
    for slot, weight, ref in zip((BACK, 0, 0, even_slot, odd_slot), weights, outs):
        part = pl.ds(pl.multiple_of(slot * rows, rows), rows)
        for group in range(kv_heads):
            ref[0, group] = (acc[0, group, part] * (scale * weight)).astype(ref.dtype)
            ref[1, group] = (acc[1, group, part] * weight).astype(ref.dtype)


def gradients(masks, parts, ranges, queries, cots, blocks, carried):
    rows, heads, size = queries.shape
    is_last = masks == stages(parts)[-1]
    kv_shape = blocks[0].shape
    kv_heads = kv_shape[1]
    span = (BACK + 1 + AHEAD) * rows
    acc_shape = (2, kv_heads, span, size)
    tokens = rows // parts
    tile_shape = (2, span - rows + tokens, tokens * (heads // kv_heads))
    work = heads * rows // parts * span * len(masks)
    outs = [pltpu.VMEM(cots[0].shape, jnp.bfloat16)] * len(masks)
    if is_last:
        outs += [pltpu.VMEM(kv_shape, jnp.float32)] + [pltpu.VMEM(kv_shape, jnp.bfloat16)] * 4
    else:
        outs += [pltpu.VMEM(acc_shape, jnp.float32)]
    own, far, even, odd = blocks
    operands = [ranges, queries, own, even, far, odd, *cots]
    operands += [] if carried is None else [carried]
    outs = pl.pallas_call(
        functools.partial(grad_kernel, masks, parts, carried is None, is_last),
        out_shape=tuple(outs),
        in_specs=[_VMEM] * len(operands),
        out_specs=(_VMEM,) * len(outs),
        scratch_shapes=[
            pltpu.VMEM(acc_shape, jnp.bfloat16),
            pltpu.VMEM(acc_shape, jnp.float32),
            pltpu.VMEM(tile_shape, jnp.float32),
            pltpu.VMEM(tile_shape, jnp.float32),
            pltpu.VMEM(tile_shape, jnp.bfloat16),
            pltpu.VMEM(tile_shape, jnp.bfloat16),
        ],
        compiler_params=pltpu.CompilerParams(vmem_limit_bytes=VMEM_BYTES),
        cost_estimate=pl.CostEstimate(
            flops=10 * work * size, bytes_accessed=4 * queries.size * 2, transcendentals=work
        ),
        name="gradients",
    )(*operands)
    return outs[: len(masks)], outs[len(masks) :]


def add_kernel(left, right, out):
    out[...] = (left[...].astype(jnp.float32) + right[...].astype(jnp.float32)).astype(out.dtype)


def add(left, right):
    return pl.pallas_call(
        add_kernel,
        out_shape=pltpu.VMEM(left.shape, left.dtype),
        in_specs=[_VMEM] * 2,
        out_specs=_VMEM,
        compiler_params=pltpu.CompilerParams(vmem_limit_bytes=VMEM_BYTES),
        name="add",
    )(left, right)


def finish_order(parts):
    return [1, "odd", "far", *range(2, parts - 1), "even", parts - 1, 0, "own"]


def finish_kernel(parts, *refs):
    *refs, dq_out, dk_out, dv_out = refs
    refs = dict(zip(finish_order(parts), refs))
    dqs = [refs[mask] for mask in range(parts)]
    own, far, even, odd = [refs[name] for name in ("own", "far", "even", "odd")]
    heads = dqs[0].shape[1]
    me = lax.axis_index("kvh")
    for mask in range(parts):
        first = pl.multiple_of((me ^ mask) * heads, heads)
        dq_out[:, pl.ds(first, heads), :] = dqs[mask][...]
    for number, ref in enumerate((dk_out, dv_out)):
        sums = []
        for group in range(ref.shape[1]):
            total = own[number, group]
            for other in (far, even, odd):
                total = total + other[number, group].astype(jnp.float32)
            sums.append(total)
        ref[...] = jnp.stack(sums, axis=1).astype(jnp.bfloat16)


def finish(dqs, partials):
    parts = len(dqs)
    rows, heads, size = dqs[0].shape
    _, kv_heads, kv_rows, _ = partials[0].shape
    kv_out = jax.ShapeDtypeStruct((kv_rows, kv_heads, size), jnp.bfloat16)
    operands = dict(enumerate(dqs)) | dict(zip(("own", "far", "even", "odd"), partials))
    return pl.pallas_call(
        functools.partial(finish_kernel, parts),
        out_shape=(
            jax.ShapeDtypeStruct((rows, heads * parts, size), jnp.bfloat16),
            kv_out,
            kv_out,
        ),
        in_specs=[_VMEM] * (parts + 4),
        out_specs=(_VMEM,) * 3,
        compiler_params=pltpu.CompilerParams(vmem_limit_bytes=VMEM_BYTES),
        name="finish",
    )(*[operands[name] for name in finish_order(parts)])


def shifted(block, distance):
    count = lax.axis_size("seq")
    return lax.ppermute(block, "seq", [(i, (i + distance) % count) for i in range(count)])


def paired(block):
    return lax.ppermute(block, "seq", [(i, i ^ 1) for i in range(lax.axis_size("seq"))])


def ringed(block, direction=1):
    count = lax.axis_size("seq")
    route = []
    for i in range(count):
        target = i + 2 if i % 2 == 0 else i - 2
        route.append((i, min(max(target, 0), count - 1))[::direction])
    return lax.ppermute(block, "seq", route)


def swapped(block, mask):
    return lax.ppermute(block, "kvh", [(i, i ^ mask) for i in range(lax.axis_size("kvh"))])


def local(queries, keys, values, output_gradient, doc_lengths, prefix_lengths):
    parts = lax.axis_size("kvh")
    kv, cots, ranges = prepare(
        doc_lengths, prefix_lengths, output_gradient, keys, values, parts
    )
    even = pack(paired(keys), paired(values))
    blocks = [kv[0], shifted(kv[1], BACK), even, ringed(even)]
    cots = [cots[0]] + [swapped(cots[mask], mask) for mask in range(1, parts)]
    dqs, carried = {}, [None]
    for masks in stages(parts):
        found, carried = gradients(
            masks, parts, ranges, queries, [cots[mask] for mask in masks], blocks, carried[0]
        )
        for mask, dq in zip(masks, found):
            dqs[mask] = swapped(dq, mask) if mask else dq
    own, far_even, far_odd, even, odd = carried
    relayed = add(paired(odd), far_odd)
    partials = [own, ringed(far_even, -1), paired(even), ringed(relayed)]
    return finish([dqs[mask] for mask in range(parts)], partials)


def solution(mesh):
    in_specs = (
        P("seq", "kvh", None),
        P("seq", "kvh", None),
        P("seq", "kvh", None),
        P(("seq", "kvh"), None, None),
        P(),
        P(),
    )
    out_specs = (P(("seq", "kvh"), None, None), P("seq", "kvh", None), P("seq", "kvh", None))
    return jax.shard_map(local, mesh=mesh, in_specs=in_specs, out_specs=out_specs, check_vma=False)
```

```python
import functools

import jax
import jax.numpy as jnp
from jax import lax
from jax.experimental import pallas as pl
from jax.experimental.pallas import tpu as pltpu
from jax.sharding import PartitionSpec as P

BACK = 2
AHEAD = 1
LOG2E = 1.4426950408889634
VMEM_BYTES = 40 * 1024 * 1024
NEG = -1e30
TILE = 8
ALIGN = 16
WIDTHS = (176, 304)

_VMEM = pl.BlockSpec(memory_space=pltpu.VMEM)
_SMEM = pl.BlockSpec(memory_space=pltpu.SMEM)
_HBM = pl.BlockSpec(memory_space=pltpu.HBM)


def stages(parts):
    rest = list(range(parts - 1, 1, -1))
    return [[0, 1, *rest[:-1]], rest[-1:]]


def regroup(buf):
    wide = buf[...].astype(jnp.float32)
    return [wide[:, group, :].astype(jnp.bfloat16) for group in range(buf.shape[1])]


def prep_kernel(parts, lengths_ref, prefixes_ref, cot_ref, key_ref, value_ref, *rest):
    kv_outs, cot_outs, rest = rest[:3], rest[3 : parts + 3], rest[parts + 3 :]
    range_out, key_buf, value_buf, lengths, prefixes, sems, scalar_sems = rest
    heads = cot_ref.shape[1] // parts
    me = lax.axis_index("kvh")
    scalars = [
        pltpu.make_async_copy(lengths_ref, lengths, scalar_sems.at[0]),
        pltpu.make_async_copy(prefixes_ref, prefixes, scalar_sems.at[1]),
    ]
    for copy in scalars:
        copy.start()
    loads = []
    for number, (ref, buf) in enumerate(((key_ref, key_buf), (value_ref, value_buf))):
        loads.append(pltpu.make_async_copy(ref, buf, sems.at[number]))
        loads[-1].start()
    copies = []
    for mask in range(parts):
        first = pl.multiple_of((me ^ mask) * heads, heads)
        copies.append(
            pltpu.make_async_copy(
                cot_ref.at[:, pl.ds(first, heads), :], cot_outs[mask], sems.at[mask + 2]
            )
        )
        copies[-1].start()
    for number, buf in enumerate((key_buf, value_buf)):
        loads[number].wait()
        for group, block in enumerate(regroup(buf)):
            for kv_out in kv_outs:
                kv_out[number, group] = block
    for copy in scalars:
        copy.wait()
    rows = key_buf.shape[0]
    tokens = rows // parts
    lanes = range_out.shape[2]
    lane_token = lax.broadcasted_iota(jnp.int32, (1, lanes), 1) // (lanes // tokens)
    shard = lax.axis_index("seq")
    for mask in range(parts):
        first = (me ^ mask) * tokens
        low, high = bounds(shard * rows + first + lane_token, lengths, prefixes)
        origin = (shard - BACK) * rows + first
        range_out[mask, 0:1, :] = low - origin
        range_out[mask, 1:2, :] = high - origin
    for copy in copies:
        copy.wait()


def prepare(lengths, prefixes, cotangent, keys, values, parts):
    rows, heads, size = cotangent.shape
    kv_rows, kv_heads, _ = keys.shape
    lanes = kv_rows // parts * (heads // parts // kv_heads)
    piece = pltpu.VMEM((rows, heads // parts, size), jnp.bfloat16)
    block = pltpu.VMEM((2, kv_heads, kv_rows, size), jnp.bfloat16)
    operands = [
        pltpu.with_memory_space_constraint(array, pltpu.HBM)
        for array in (lengths, prefixes, cotangent, keys, values)
    ]
    outs = pl.pallas_call(
        functools.partial(prep_kernel, parts),
        out_shape=(block,) * 3 + (piece,) * parts + (pltpu.VMEM((parts, 2, lanes), jnp.int32),),
        in_specs=[_HBM] * 5,
        out_specs=(_VMEM,) * (parts + 4),
        scratch_shapes=[
            pltpu.VMEM(keys.shape, jnp.bfloat16),
            pltpu.VMEM(values.shape, jnp.bfloat16),
            pltpu.SMEM(lengths.shape, jnp.int32),
            pltpu.SMEM(prefixes.shape, jnp.int32),
            pltpu.SemaphoreType.DMA((parts + 2,)),
            pltpu.SemaphoreType.DMA((2,)),
        ],
        compiler_params=pltpu.CompilerParams(vmem_limit_bytes=VMEM_BYTES),
        name="prepare",
    )(*operands)
    return outs[:3], outs[3:-1], outs[-1]


def bounds(position, lengths, prefixes):
    docs = lengths.shape[0]

    def step(doc, carry):
        start, low, high = carry
        end = start + lengths[doc]
        inside = (position >= start) & (position < end)
        reach = jnp.minimum(end, jnp.maximum(position + 1, start + prefixes[doc]))
        return end, jnp.where(inside, start, low), jnp.where(inside, reach, high)

    zero = jnp.zeros_like(position)
    carry = (jnp.int32(0), zero, zero)
    if docs <= 16:
        for doc in range(docs):
            carry = step(doc, carry)
    else:
        carry = lax.fori_loop(0, docs, step, carry)
    return carry[1], carry[2]


def neighbour_slots(shard):
    odd = shard % 2
    ahead, behind = BACK + 1, BACK - 1
    return jnp.where(odd == 1, behind, ahead), jnp.where(odd == 1, ahead, behind)


def grad_kernel(masks, parts, is_first, is_last, range_ref, q_ref, *refs):
    refs = list(refs)
    kv_own, kv_even, kv_far, kv_odd = [refs.pop(0) for _ in range(4)]
    cots = [refs.pop(0) for _ in masks]
    carried = None if is_first else refs.pop(0)
    dqs = [refs.pop(0) for _ in masks]
    outs, (window, acc, score_buf, dprob_buf, prob_buf, dscore_buf) = refs[:-6], refs[-6:]
    rows, heads, size = q_ref.shape
    tokens = rows // parts
    kv_heads = kv_own.shape[1]
    group_size = heads // kv_heads
    span = (BACK + 1 + AHEAD) * rows
    reach = span - rows + tokens
    lanes = tokens * group_size
    scale = size ** (-0.5)
    shard = lax.axis_index("seq")
    me = lax.axis_index("kvh")

    even_slot, odd_slot = neighbour_slots(shard)
    for slot, ref in ((BACK, kv_own), (0, kv_far), (even_slot, kv_even), (odd_slot, kv_odd)):
        part = pl.ds(pl.multiple_of(slot * rows, rows), rows)
        for number in range(2):
            for group in range(kv_heads):
                window[number, group, part] = ref[number, group]
    acc[...] = jnp.zeros_like(acc) if is_first else carried[...]

    contract_last = (((1,), (1,)), ((), ()))
    contract_first = (((0,), (0,)), ((), ()))
    sublane = lax.broadcasted_iota(jnp.int32, (TILE, lanes), 0)
    items = [(place, group) for place in range(len(masks)) for group in range(kv_heads)]

    def operands(item, starts, width):
        place, group = items[item]
        first = pl.multiple_of((me ^ masks[place]) * tokens, tokens)
        of_group = pl.ds(group * group_size, group_size)
        q = q_ref[pl.ds(first, tokens), of_group].astype(jnp.float32)
        cot = cots[place][:, of_group].astype(jnp.float32)
        return (
            pl.ds(pl.multiple_of(first + starts[place], ALIGN), width),
            q.reshape(lanes, size).astype(jnp.bfloat16),
            cot.reshape(lanes, size).astype(jnp.bfloat16),
        )

    def scores_of(item, starts, width):
        place, group = items[item]
        slot = item % 2
        here, q, cot = operands(item, starts, width)
        scores = lax.dot_general(
            window[0, group, here], q, contract_last, preferred_element_type=jnp.float32
        )
        low = range_ref[masks[place], 0:1, :] - starts[place] - sublane
        high = range_ref[masks[place], 1:2, :] - starts[place] - sublane
        top = jnp.full((TILE, lanes), NEG, jnp.float32)
        for row in range(0, width, TILE):
            visible = (low <= row) & (high > row)
            tile = jnp.where(visible, scores[row : row + TILE] * (scale * LOG2E), NEG)
            top = jnp.maximum(top, tile)
            score_buf[slot, row : row + TILE] = tile
        dprob_buf[slot, :width] = lax.dot_general(
            window[1, group, here], cot, contract_last, preferred_element_type=jnp.float32
        )
        return jnp.max(top, axis=0, keepdims=True)

    def softmax_of(item, top, width):
        slot = item % 2
        total = jnp.zeros((TILE, lanes), jnp.float32)
        delta = jnp.zeros((TILE, lanes), jnp.float32)
        for row in range(0, width, TILE):
            tile = slice(row, row + TILE)
            expo = jnp.exp2(score_buf[slot, tile] - top)
            total = total + expo
            delta = delta + expo * dprob_buf[slot, tile]
            score_buf[slot, tile] = expo
        inverse = 1.0 / jnp.sum(total, axis=0, keepdims=True)
        delta = jnp.sum(delta, axis=0, keepdims=True) * inverse
        for row in range(0, width, 2 * TILE):
            tile = slice(row, row + 2 * TILE)
            probs = score_buf[slot, tile] * inverse
            dscores = probs * (dprob_buf[slot, tile] - delta)
            prob_buf[slot, tile] = probs.astype(jnp.bfloat16)
            dscore_buf[slot, tile] = dscores.astype(jnp.bfloat16)

    def gradients_of(item, starts, width):
        place, group = items[item]
        slot = item % 2
        here, q, cot = operands(item, starts, width)
        probs, dscores = prob_buf[slot, :width], dscore_buf[slot, :width]
        acc[1, group, here] += jnp.dot(probs, cot, preferred_element_type=jnp.float32)
        acc[0, group, here] += jnp.dot(dscores, q, preferred_element_type=jnp.float32)
        dq = lax.dot_general(
            window[0, group, here], dscores, contract_first, preferred_element_type=jnp.float32
        )
        dq = jnp.transpose(dq * scale).reshape(tokens, group_size, size)
        dqs[place][:, pl.ds(group * group_size, group_size)] = dq.astype(jnp.bfloat16)

    def chunk(place, width):
        starts = {place: jnp.clip(lowest[place], 0, reach - width)}
        here = [item for item, (of_place, _) in enumerate(items) if of_place == place]
        top = scores_of(here[0], starts, width)
        for item in here:
            later = scores_of(item + 1, starts, width) if item + 1 in here else None
            softmax_of(item, top, width)
            gradients_of(item, starts, width)
            top = later

    lowest = [jnp.min(range_ref[mask, 0:1, :]) & -ALIGN for mask in masks]
    needed = [jnp.max(range_ref[mask, 1:2, :]) - low for mask, low in zip(masks, lowest)]
    widths = [width for width in WIDTHS if width < reach] + [reach]
    for place in range(len(masks)):
        for floor, width in zip([-1] + widths, widths):
            fits = needed[place] > floor
            if width < reach:
                fits = fits & (needed[place] <= width)
            pl.when(fits)(functools.partial(chunk, place, width))

    if not is_last:
        outs[0][...] = acc[...]
        return
    is_odd = (shard % 2).astype(jnp.float32)
    weights = (1.0, 1.0 - is_odd, is_odd, 1.0, 1.0)
    for slot, weight, ref in zip((BACK, 0, 0, even_slot, odd_slot), weights, outs):
        part = pl.ds(pl.multiple_of(slot * rows, rows), rows)
        for group in range(kv_heads):
            ref[0, group] = (acc[0, group, part] * (scale * weight)).astype(ref.dtype)
            ref[1, group] = (acc[1, group, part] * weight).astype(ref.dtype)


def gradients(masks, parts, ranges, queries, cots, blocks, carried):
    rows, heads, size = queries.shape
    is_last = masks == stages(parts)[-1]
    kv_shape = blocks[0].shape
    kv_heads = kv_shape[1]
    span = (BACK + 1 + AHEAD) * rows
    acc_shape = (2, kv_heads, span, size)
    tokens = rows // parts
    tile_shape = (2, span - rows + tokens, tokens * (heads // kv_heads))
    work = heads * rows // parts * span * len(masks)
    outs = [pltpu.VMEM(cots[0].shape, jnp.bfloat16)] * len(masks)
    if is_last:
        outs += [pltpu.VMEM(kv_shape, jnp.float32)] + [pltpu.VMEM(kv_shape, jnp.bfloat16)] * 4
    else:
        outs += [pltpu.VMEM(acc_shape, jnp.float32)]
    own, far, even, odd = blocks
    operands = [ranges, queries, own, even, far, odd, *cots]
    operands += [] if carried is None else [carried]
    outs = pl.pallas_call(
        functools.partial(grad_kernel, masks, parts, carried is None, is_last),
        out_shape=tuple(outs),
        in_specs=[_VMEM] * len(operands),
        out_specs=(_VMEM,) * len(outs),
        scratch_shapes=[
            pltpu.VMEM(acc_shape, jnp.bfloat16),
            pltpu.VMEM(acc_shape, jnp.float32),
            pltpu.VMEM(tile_shape, jnp.float32),
            pltpu.VMEM(tile_shape, jnp.float32),
            pltpu.VMEM(tile_shape, jnp.bfloat16),
            pltpu.VMEM(tile_shape, jnp.bfloat16),
        ],
        compiler_params=pltpu.CompilerParams(vmem_limit_bytes=VMEM_BYTES),
        cost_estimate=pl.CostEstimate(
            flops=10 * work * size, bytes_accessed=4 * queries.size * 2, transcendentals=work
        ),
        name="gradients",
    )(*operands)
    return outs[: len(masks)], outs[len(masks) :]


def add_kernel(left, right, out):
    out[...] = (left[...].astype(jnp.float32) + right[...].astype(jnp.float32)).astype(out.dtype)


def add(left, right):
    return pl.pallas_call(
        add_kernel,
        out_shape=pltpu.VMEM(left.shape, left.dtype),
        in_specs=[_VMEM] * 2,
        out_specs=_VMEM,
        compiler_params=pltpu.CompilerParams(vmem_limit_bytes=VMEM_BYTES),
        name="add",
    )(left, right)


def finish_order(parts):
    return [1, "odd", "far", *range(2, parts - 1), "even", parts - 1, 0, "own"]


def finish_kernel(parts, *refs):
    *refs, dq_out, dk_out, dv_out = refs
    refs = dict(zip(finish_order(parts), refs))
    dqs = [refs[mask] for mask in range(parts)]
    own, far, even, odd = [refs[name] for name in ("own", "far", "even", "odd")]
    heads = dqs[0].shape[1]
    me = lax.axis_index("kvh")
    for mask in range(parts):
        first = pl.multiple_of((me ^ mask) * heads, heads)
        dq_out[:, pl.ds(first, heads), :] = dqs[mask][...]
    for number, ref in enumerate((dk_out, dv_out)):
        sums = []
        for group in range(ref.shape[1]):
            total = own[number, group]
            for other in (far, even, odd):
                total = total + other[number, group].astype(jnp.float32)
            sums.append(total)
        ref[...] = jnp.stack(sums, axis=1).astype(jnp.bfloat16)


def finish(dqs, partials):
    parts = len(dqs)
    rows, heads, size = dqs[0].shape
    _, kv_heads, kv_rows, _ = partials[0].shape
    kv_out = jax.ShapeDtypeStruct((kv_rows, kv_heads, size), jnp.bfloat16)
    operands = dict(enumerate(dqs)) | dict(zip(("own", "far", "even", "odd"), partials))
    return pl.pallas_call(
        functools.partial(finish_kernel, parts),
        out_shape=(
            jax.ShapeDtypeStruct((rows, heads * parts, size), jnp.bfloat16),
            kv_out,
            kv_out,
        ),
        in_specs=[_VMEM] * (parts + 4),
        out_specs=(_VMEM,) * 3,
        compiler_params=pltpu.CompilerParams(vmem_limit_bytes=VMEM_BYTES),
        name="finish",
    )(*[operands[name] for name in finish_order(parts)])


def shifted(block, distance):
    count = lax.axis_size("seq")
    return lax.ppermute(block, "seq", [(i, (i + distance) % count) for i in range(count)])


def paired(block):
    return lax.ppermute(block, "seq", [(i, i ^ 1) for i in range(lax.axis_size("seq"))])


def ringed(block, direction=1):
    count = lax.axis_size("seq")
    route = []
    for i in range(count):
        target = i + 2 if i % 2 == 0 else i - 2
        route.append((i, min(max(target, 0), count - 1))[::direction])
    return lax.ppermute(block, "seq", route)


def swapped(block, mask):
    return lax.ppermute(block, "kvh", [(i, i ^ mask) for i in range(lax.axis_size("kvh"))])


def local(queries, keys, values, output_gradient, doc_lengths, prefix_lengths):
    parts = lax.axis_size("kvh")
    kv, cots, ranges = prepare(
        doc_lengths, prefix_lengths, output_gradient, keys, values, parts
    )
    even = paired(kv[2])
    blocks = [kv[0], shifted(kv[1], BACK), even, ringed(even)]
    cots = [cots[0]] + [swapped(cots[mask], mask) for mask in range(1, parts)]
    dqs, carried = {}, [None]
    for masks in stages(parts):
        found, carried = gradients(
            masks, parts, ranges, queries, [cots[mask] for mask in masks], blocks, carried[0]
        )
        for mask, dq in zip(masks, found):
            dqs[mask] = swapped(dq, mask) if mask else dq
    own, far_even, far_odd, even, odd = carried
    relayed = add(paired(odd), far_odd)
    partials = [own, ringed(far_even, -1), paired(even), ringed(relayed)]
    return finish([dqs[mask] for mask in range(parts)], partials)


def solution(mesh):
    in_specs = (
        P("seq", "kvh", None),
        P("seq", "kvh", None),
        P("seq", "kvh", None),
        P(("seq", "kvh"), None, None),
        P(),
        P(),
    )
    out_specs = (P(("seq", "kvh"), None, None), P("seq", "kvh", None), P("seq", "kvh", None))
    return jax.shard_map(local, mesh=mesh, in_specs=in_specs, out_specs=out_specs, check_vma=False)
```

```python
import functools

import jax
import jax.numpy as jnp
from jax import lax
from jax.experimental import pallas as pl
from jax.experimental.pallas import tpu as pltpu
from jax.sharding import PartitionSpec as P

BACK = 2
AHEAD = 1
LOG2E = 1.4426950408889634
VMEM_BYTES = 40 * 1024 * 1024
NEG = -1e30
TILE = 8
ALIGN = 16
WIDTHS = (176, 304)

_VMEM = pl.BlockSpec(memory_space=pltpu.VMEM)
_SMEM = pl.BlockSpec(memory_space=pltpu.SMEM)
_HBM = pl.BlockSpec(memory_space=pltpu.HBM)


def stages(parts):
    rest = list(range(parts - 1, 1, -1))
    return [[0, 1, *rest[:-1]], rest[-1:]]


def regroup(buf):
    wide = buf[...].astype(jnp.float32)
    return [wide[:, group, :].astype(jnp.bfloat16) for group in range(buf.shape[1])]


def prep_kernel(parts, lengths_ref, prefixes_ref, cot_ref, key_ref, value_ref, *rest):
    kv_outs, cot_outs, rest = rest[:3], rest[3 : parts + 3], rest[parts + 3 :]
    range_out, key_buf, value_buf, lengths, prefixes, sems, scalar_sems = rest
    heads = cot_ref.shape[1] // parts
    me = lax.axis_index("kvh")
    scalars = [
        pltpu.make_async_copy(lengths_ref, lengths, scalar_sems.at[0]),
        pltpu.make_async_copy(prefixes_ref, prefixes, scalar_sems.at[1]),
    ]
    for copy in scalars:
        copy.start()
    loads = []
    for number, (ref, buf) in enumerate(((key_ref, key_buf), (value_ref, value_buf))):
        loads.append(pltpu.make_async_copy(ref, buf, sems.at[number]))
        loads[-1].start()
    copies = []
    for mask in range(parts):
        first = pl.multiple_of((me ^ mask) * heads, heads)
        copies.append(
            pltpu.make_async_copy(
                cot_ref.at[:, pl.ds(first, heads), :], cot_outs[mask], sems.at[mask + 2]
            )
        )
        copies[-1].start()
    for number, buf in enumerate((key_buf, value_buf)):
        loads[number].wait()
        for group, block in enumerate(regroup(buf)):
            for kv_out in kv_outs:
                kv_out[number, group] = block
    for copy in scalars:
        copy.wait()
    rows = key_buf.shape[0]
    tokens = rows // parts
    lanes = range_out.shape[2]
    lane_token = lax.broadcasted_iota(jnp.int32, (1, lanes), 1) // (lanes // tokens)
    shard = lax.axis_index("seq")
    for mask in range(parts):
        first = (me ^ mask) * tokens
        low, high = bounds(shard * rows + first + lane_token, lengths, prefixes)
        origin = (shard - BACK) * rows + first
        range_out[mask, 0:1, :] = low - origin
        range_out[mask, 1:2, :] = high - origin
    for copy in copies:
        copy.wait()


def prepare(lengths, prefixes, cotangent, keys, values, parts):
    rows, heads, size = cotangent.shape
    kv_rows, kv_heads, _ = keys.shape
    lanes = kv_rows // parts * (heads // parts // kv_heads)
    piece = pltpu.VMEM((rows, heads // parts, size), jnp.bfloat16)
    block = pltpu.VMEM((2, kv_heads, kv_rows, size), jnp.bfloat16)
    operands = [
        pltpu.with_memory_space_constraint(array, pltpu.HBM)
        for array in (lengths, prefixes, cotangent, keys, values)
    ]
    outs = pl.pallas_call(
        functools.partial(prep_kernel, parts),
        out_shape=(block,) * 3 + (piece,) * parts + (pltpu.VMEM((parts, 2, lanes), jnp.int32),),
        in_specs=[_HBM] * 5,
        out_specs=(_VMEM,) * (parts + 4),
        scratch_shapes=[
            pltpu.VMEM(keys.shape, jnp.bfloat16),
            pltpu.VMEM(values.shape, jnp.bfloat16),
            pltpu.SMEM(lengths.shape, jnp.int32),
            pltpu.SMEM(prefixes.shape, jnp.int32),
            pltpu.SemaphoreType.DMA((parts + 2,)),
            pltpu.SemaphoreType.DMA((2,)),
        ],
        compiler_params=pltpu.CompilerParams(vmem_limit_bytes=VMEM_BYTES),
        name="prepare",
    )(*operands)
    return outs[:3], outs[3:-1], outs[-1]


def bounds(position, lengths, prefixes):
    docs = lengths.shape[0]

    def step(doc, carry):
        start, low, high = carry
        end = start + lengths[doc]
        inside = (position >= start) & (position < end)
        reach = jnp.minimum(end, jnp.maximum(position + 1, start + prefixes[doc]))
        return end, jnp.where(inside, start, low), jnp.where(inside, reach, high)

    zero = jnp.zeros_like(position)
    carry = (jnp.int32(0), zero, zero)
    if docs <= 16:
        for doc in range(docs):
            carry = step(doc, carry)
    else:
        carry = lax.fori_loop(0, docs, step, carry)
    return carry[1], carry[2]


def neighbour_slots(shard):
    odd = shard % 2
    ahead, behind = BACK + 1, BACK - 1
    return jnp.where(odd == 1, behind, ahead), jnp.where(odd == 1, ahead, behind)


def grad_kernel(masks, parts, is_first, is_last, range_ref, q_ref, *refs):
    refs = list(refs)
    received = [refs.pop(0) for _ in range(4)] if is_first else []
    cots = [refs.pop(0) for _ in masks]
    window, carried = (None, None) if is_first else (refs.pop(0), refs.pop(0))
    dqs = [refs.pop(0) for _ in masks]
    score_buf, dprob_buf, prob_buf, dscore_buf, q_rows, cot_rows = refs[-6:]
    outs = refs[:-6]
    if is_first:
        window, acc = outs
    else:
        acc = outs.pop()
    rows, heads, size = q_ref.shape
    tokens = rows // parts
    kv_heads = window.shape[1]
    group_size = heads // kv_heads
    span = (BACK + 1 + AHEAD) * rows
    reach = span - rows + tokens
    lanes = tokens * group_size
    scale = size ** (-0.5)
    shard = lax.axis_index("seq")
    me = lax.axis_index("kvh")

    even_slot, odd_slot = neighbour_slots(shard)
    if is_first:
        for slot, ref in zip((BACK, even_slot, 0, odd_slot), received):
            part = pl.ds(pl.multiple_of(slot * rows, rows), rows)
            for number in range(2):
                for group in range(kv_heads):
                    window[number, group, part] = ref[number, group]
        acc[...] = jnp.zeros_like(acc)
    else:
        acc[...] = carried[...]

    contract_last = (((1,), (1,)), ((), ()))
    contract_first = (((0,), (0,)), ((), ()))
    sublane = lax.broadcasted_iota(jnp.int32, (TILE, lanes), 0)
    items = [(place, group) for place in range(len(masks)) for group in range(kv_heads)]

    def key_rows(place, starts, width):
        first = pl.multiple_of((me ^ masks[place]) * tokens, tokens)
        return pl.ds(pl.multiple_of(first + starts[place], ALIGN), width)

    def operands(item, starts, width):
        place, group = items[item]
        first = pl.multiple_of((me ^ masks[place]) * tokens, tokens)
        of_group = pl.ds(group * group_size, group_size)
        q = q_ref[pl.ds(first, tokens), of_group].astype(jnp.float32)
        cot = cots[place][:, of_group].astype(jnp.float32)
        return (
            key_rows(place, starts, width),
            q.reshape(lanes, size).astype(jnp.bfloat16),
            cot.reshape(lanes, size).astype(jnp.bfloat16),
        )

    def scores_of(item, starts, width):
        place, group = items[item]
        slot = item % 2
        here, q, cot = operands(item, starts, width)
        q_rows[slot], cot_rows[slot] = q, cot
        scores = lax.dot_general(
            window[0, group, here], q, contract_last, preferred_element_type=jnp.float32
        )
        low = range_ref[masks[place], 0:1, :] - starts[place] - sublane
        high = range_ref[masks[place], 1:2, :] - starts[place] - sublane
        top = jnp.full((TILE, lanes), NEG, jnp.float32)
        for row in range(0, width, TILE):
            visible = (low <= row) & (high > row)
            tile = jnp.where(visible, scores[row : row + TILE] * (scale * LOG2E), NEG)
            top = jnp.maximum(top, tile)
            score_buf[slot, row : row + TILE] = tile
        dprob_buf[slot, :width] = lax.dot_general(
            window[1, group, here], cot, contract_last, preferred_element_type=jnp.float32
        )
        return jnp.max(top, axis=0, keepdims=True)

    def softmax_of(item, top, width):
        slot = item % 2
        total = jnp.zeros((TILE, lanes), jnp.float32)
        delta = jnp.zeros((TILE, lanes), jnp.float32)
        for row in range(0, width, TILE):
            tile = slice(row, row + TILE)
            expo = jnp.exp2(score_buf[slot, tile] - top)
            total = total + expo
            delta = delta + expo * dprob_buf[slot, tile]
            score_buf[slot, tile] = expo
        inverse = 1.0 / jnp.sum(total, axis=0, keepdims=True)
        delta = jnp.sum(delta, axis=0, keepdims=True) * inverse
        for row in range(0, width, 2 * TILE):
            tile = slice(row, row + 2 * TILE)
            probs = score_buf[slot, tile] * inverse
            dscores = probs * (dprob_buf[slot, tile] - delta)
            prob_buf[slot, tile] = probs.astype(jnp.bfloat16)
            dscore_buf[slot, tile] = dscores.astype(jnp.bfloat16)

    def gradients_of(item, starts, width):
        place, group = items[item]
        slot = item % 2
        here, q, cot = key_rows(place, starts, width), q_rows[slot], cot_rows[slot]
        probs, dscores = prob_buf[slot, :width], dscore_buf[slot, :width]
        acc[1, group, here] += jnp.dot(probs, cot, preferred_element_type=jnp.float32)
        acc[0, group, here] += jnp.dot(dscores, q, preferred_element_type=jnp.float32)
        dq = lax.dot_general(
            window[0, group, here], dscores, contract_first, preferred_element_type=jnp.float32
        )
        dq = jnp.transpose(dq * scale).reshape(tokens, group_size, size)
        dqs[place][:, pl.ds(group * group_size, group_size)] = dq.astype(jnp.bfloat16)

    def chunk(place, width):
        starts = {place: jnp.clip(lowest[place], 0, reach - width)}
        here = [item for item, (of_place, _) in enumerate(items) if of_place == place]
        top = scores_of(here[0], starts, width)
        for item in here:
            later = scores_of(item + 1, starts, width) if item + 1 in here else None
            softmax_of(item, top, width)
            gradients_of(item, starts, width)
            top = later

    lowest = [jnp.min(range_ref[mask, 0:1, :]) & -ALIGN for mask in masks]
    needed = [jnp.max(range_ref[mask, 1:2, :]) - low for mask, low in zip(masks, lowest)]
    widths = [width for width in WIDTHS if width < reach] + [reach]
    for place in range(len(masks)):
        for floor, width in zip([-1] + widths, widths):
            fits = needed[place] > floor
            if width < reach:
                fits = fits & (needed[place] <= width)
            pl.when(fits)(functools.partial(chunk, place, width))

    if not is_last:
        return
    is_odd = (shard % 2).astype(jnp.float32)
    weights = (1.0, 1.0 - is_odd, is_odd, 1.0, 1.0)
    for slot, weight, ref in zip((BACK, 0, 0, even_slot, odd_slot), weights, outs):
        part = pl.ds(pl.multiple_of(slot * rows, rows), rows)
        for group in range(kv_heads):
            ref[0, group] = (acc[0, group, part] * (scale * weight)).astype(ref.dtype)
            ref[1, group] = (acc[1, group, part] * weight).astype(ref.dtype)


def gradients(masks, parts, ranges, queries, cots, blocks, carried):
    rows, heads, size = queries.shape
    is_last = masks == stages(parts)[-1]
    kv_shape = blocks[0].shape
    kv_heads = kv_shape[1]
    span = (BACK + 1 + AHEAD) * rows
    acc_shape = (2, kv_heads, span, size)
    tokens = rows // parts
    tile_shape = (2, span - rows + tokens, tokens * (heads // kv_heads))
    work = heads * rows // parts * span * len(masks)
    outs = [pltpu.VMEM(cots[0].shape, jnp.bfloat16)] * len(masks)
    if is_last:
        outs += [pltpu.VMEM(kv_shape, jnp.float32)] + [pltpu.VMEM(kv_shape, jnp.bfloat16)] * 4
    else:
        outs += [pltpu.VMEM(acc_shape, jnp.bfloat16), pltpu.VMEM(acc_shape, jnp.float32)]
    own, far, even, odd = blocks
    operands = [ranges, queries] + ([own, even, far, odd] if carried is None else [])
    operands += [*cots] + ([] if carried is None else list(carried))
    outs = pl.pallas_call(
        functools.partial(grad_kernel, masks, parts, carried is None, is_last),
        out_shape=tuple(outs),
        in_specs=[_VMEM] * len(operands),
        out_specs=(_VMEM,) * len(outs),
        scratch_shapes=([pltpu.VMEM(acc_shape, jnp.float32)] if is_last else [])
        + [
            pltpu.VMEM(tile_shape, jnp.float32),
            pltpu.VMEM(tile_shape, jnp.float32),
            pltpu.VMEM(tile_shape, jnp.bfloat16),
            pltpu.VMEM(tile_shape, jnp.bfloat16),
            pltpu.VMEM((2, tile_shape[2], size), jnp.bfloat16),
            pltpu.VMEM((2, tile_shape[2], size), jnp.bfloat16),
        ],
        compiler_params=pltpu.CompilerParams(vmem_limit_bytes=VMEM_BYTES),
        cost_estimate=pl.CostEstimate(
            flops=10 * work * size, bytes_accessed=4 * queries.size * 2, transcendentals=work
        ),
        name="gradients",
    )(*operands)
    return outs[: len(masks)], outs[len(masks) :]


def add_kernel(left, right, out):
    out[...] = (left[...].astype(jnp.float32) + right[...].astype(jnp.float32)).astype(out.dtype)


def add(left, right):
    return pl.pallas_call(
        add_kernel,
        out_shape=pltpu.VMEM(left.shape, left.dtype),
        in_specs=[_VMEM] * 2,
        out_specs=_VMEM,
        compiler_params=pltpu.CompilerParams(vmem_limit_bytes=VMEM_BYTES),
        name="add",
    )(left, right)


def finish_order(parts):
    return [1, "odd", "far", *range(2, parts - 1), "even", parts - 1, 0, "own"]


def finish_kernel(parts, *refs):
    *refs, dq_out, dk_out, dv_out, dk_buf, dv_buf, sems = refs
    refs = dict(zip(finish_order(parts), refs))
    heads = refs[0].shape[1]
    me = lax.axis_index("kvh")
    copies = []
    for mask in range(parts):
        first = pl.multiple_of((me ^ mask) * heads, heads)
        copies.append(
            pltpu.make_async_copy(refs[mask], dq_out.at[:, pl.ds(first, heads), :], sems.at[mask])
        )
        copies[-1].start()
    for number, (buf, ref) in enumerate(((dk_buf, dk_out), (dv_buf, dv_out))):
        sums = []
        for group in range(buf.shape[1]):
            total = refs["own"][number, group]
            for name in ("far", "even", "odd"):
                total = total + refs[name][number, group].astype(jnp.float32)
            sums.append(total)
        buf[...] = jnp.stack(sums, axis=1).astype(jnp.bfloat16)
        copies.append(pltpu.make_async_copy(buf, ref, sems.at[parts + number]))
        copies[-1].start()
    for copy in copies:
        copy.wait()


def finish(dqs, partials):
    parts = len(dqs)
    rows, heads, size = dqs[0].shape
    _, kv_heads, kv_rows, _ = partials[0].shape
    kv_shape = (kv_rows, kv_heads, size)
    kv_out = jax.ShapeDtypeStruct(kv_shape, jnp.bfloat16)
    operands = dict(enumerate(dqs)) | dict(zip(("own", "far", "even", "odd"), partials))
    return pl.pallas_call(
        functools.partial(finish_kernel, parts),
        out_shape=(
            jax.ShapeDtypeStruct((rows, heads * parts, size), jnp.bfloat16),
            kv_out,
            kv_out,
        ),
        in_specs=[_VMEM] * (parts + 4),
        out_specs=(_HBM,) * 3,
        scratch_shapes=[
            pltpu.VMEM(kv_shape, jnp.bfloat16),
            pltpu.VMEM(kv_shape, jnp.bfloat16),
            pltpu.SemaphoreType.DMA((parts + 2,)),
        ],
        compiler_params=pltpu.CompilerParams(vmem_limit_bytes=VMEM_BYTES),
        name="finish",
    )(*[operands[name] for name in finish_order(parts)])


def shifted(block, distance):
    count = lax.axis_size("seq")
    return lax.ppermute(block, "seq", [(i, (i + distance) % count) for i in range(count)])


def paired(block):
    return lax.ppermute(block, "seq", [(i, i ^ 1) for i in range(lax.axis_size("seq"))])


def ringed(block, direction=1):
    count = lax.axis_size("seq")
    route = []
    for i in range(count):
        target = i + 2 if i % 2 == 0 else i - 2
        route.append((i, min(max(target, 0), count - 1))[::direction])
    return lax.ppermute(block, "seq", route)


def swapped(block, mask):
    return lax.ppermute(block, "kvh", [(i, i ^ mask) for i in range(lax.axis_size("kvh"))])


def local(queries, keys, values, output_gradient, doc_lengths, prefix_lengths):
    parts = lax.axis_size("kvh")
    kv, cots, ranges = prepare(
        doc_lengths, prefix_lengths, output_gradient, keys, values, parts
    )
    even = paired(kv[2])
    blocks = [kv[0], shifted(kv[1], BACK), even, ringed(even)]
    cots = [cots[0]] + [swapped(cots[mask], mask) for mask in range(1, parts)]
    dqs, carried = {}, None
    for masks in stages(parts):
        found, carried = gradients(
            masks, parts, ranges, queries, [cots[mask] for mask in masks], blocks, carried
        )
        for mask, dq in zip(masks, found):
            dqs[mask] = swapped(dq, mask) if mask else dq
    own, far_even, far_odd, even, odd = carried
    relayed = add(paired(odd), far_odd)
    partials = [own, ringed(far_even, -1), paired(even), ringed(relayed)]
    return finish([dqs[mask] for mask in range(parts)], partials)


def solution(mesh):
    in_specs = (
        P("seq", "kvh", None),
        P("seq", "kvh", None),
        P("seq", "kvh", None),
        P(("seq", "kvh"), None, None),
        P(),
        P(),
    )
    out_specs = (P(("seq", "kvh"), None, None), P("seq", "kvh", None), P("seq", "kvh", None))
    return jax.shard_map(local, mesh=mesh, in_specs=in_specs, out_specs=out_specs, check_vma=False)
```

```python
import functools

import jax
import jax.numpy as jnp
from jax import lax
from jax.experimental import pallas as pl
from jax.experimental.pallas import tpu as pltpu
from jax.sharding import PartitionSpec as P

BACK = 2
AHEAD = 1
LOG2E = 1.4426950408889634
VMEM_BYTES = 40 * 1024 * 1024
NEG = -1e30
TILE = 8
ALIGN = 16
WIDTHS = (176, 304)

_VMEM = pl.BlockSpec(memory_space=pltpu.VMEM)
_SMEM = pl.BlockSpec(memory_space=pltpu.SMEM)
_HBM = pl.BlockSpec(memory_space=pltpu.HBM)


def stages(parts):
    rest = list(range(parts - 1, 1, -1))
    return [[0, 1, *rest[:-1]], rest[-1:]]


def regroup(buf):
    wide = buf[...].astype(jnp.float32)
    return [wide[:, group, :].astype(jnp.bfloat16) for group in range(buf.shape[1])]


def prep_kernel(parts, lengths_ref, prefixes_ref, cot_ref, key_ref, value_ref, *rest):
    kv_outs, cot_outs, rest = rest[:3], rest[3 : parts + 3], rest[parts + 3 :]
    range_out, key_buf, value_buf, lengths, prefixes, sems, scalar_sems = rest
    heads = cot_ref.shape[1] // parts
    me = lax.axis_index("kvh")
    scalars = [
        pltpu.make_async_copy(lengths_ref, lengths, scalar_sems.at[0]),
        pltpu.make_async_copy(prefixes_ref, prefixes, scalar_sems.at[1]),
    ]
    for copy in scalars:
        copy.start()
    loads = []
    for number, (ref, buf) in enumerate(((key_ref, key_buf), (value_ref, value_buf))):
        loads.append(pltpu.make_async_copy(ref, buf, sems.at[number]))
        loads[-1].start()
    copies = []
    for mask in range(parts):
        first = pl.multiple_of((me ^ mask) * heads, heads)
        copies.append(
            pltpu.make_async_copy(
                cot_ref.at[:, pl.ds(first, heads), :], cot_outs[mask], sems.at[mask + 2]
            )
        )
        copies[-1].start()
    for number, buf in enumerate((key_buf, value_buf)):
        loads[number].wait()
        for group, block in enumerate(regroup(buf)):
            for kv_out in kv_outs:
                kv_out[number, group] = block
    for copy in scalars:
        copy.wait()
    rows = key_buf.shape[0]
    tokens = rows // parts
    lanes = range_out.shape[2]
    lane_token = lax.broadcasted_iota(jnp.int32, (1, lanes), 1) // (lanes // tokens)
    shard = lax.axis_index("seq")
    for mask in range(parts):
        first = (me ^ mask) * tokens
        low, high = bounds(shard * rows + first + lane_token, lengths, prefixes)
        origin = (shard - BACK) * rows + first
        range_out[mask, 0:1, :] = low - origin
        range_out[mask, 1:2, :] = high - origin
    for copy in copies:
        copy.wait()


def prepare(lengths, prefixes, cotangent, keys, values, parts):
    rows, heads, size = cotangent.shape
    kv_rows, kv_heads, _ = keys.shape
    lanes = kv_rows // parts * (heads // parts // kv_heads)
    piece = pltpu.VMEM((rows, heads // parts, size), jnp.bfloat16)
    block = pltpu.VMEM((2, kv_heads, kv_rows, size), jnp.bfloat16)
    operands = [
        pltpu.with_memory_space_constraint(array, pltpu.HBM)
        for array in (lengths, prefixes, cotangent, keys, values)
    ]
    outs = pl.pallas_call(
        functools.partial(prep_kernel, parts),
        out_shape=(block,) * 3 + (piece,) * parts + (pltpu.VMEM((parts, 2, lanes), jnp.int32),),
        in_specs=[_HBM] * 5,
        out_specs=(_VMEM,) * (parts + 4),
        scratch_shapes=[
            pltpu.VMEM(keys.shape, jnp.bfloat16),
            pltpu.VMEM(values.shape, jnp.bfloat16),
            pltpu.SMEM(lengths.shape, jnp.int32),
            pltpu.SMEM(prefixes.shape, jnp.int32),
            pltpu.SemaphoreType.DMA((parts + 2,)),
            pltpu.SemaphoreType.DMA((2,)),
        ],
        compiler_params=pltpu.CompilerParams(vmem_limit_bytes=VMEM_BYTES),
        name="prepare",
    )(*operands)
    return outs[:3], outs[3:-1], outs[-1]


def bounds(position, lengths, prefixes):
    docs = lengths.shape[0]

    def step(doc, carry):
        start, low, high = carry
        end = start + lengths[doc]
        inside = (position >= start) & (position < end)
        reach = jnp.minimum(end, jnp.maximum(position + 1, start + prefixes[doc]))
        return end, jnp.where(inside, start, low), jnp.where(inside, reach, high)

    zero = jnp.zeros_like(position)
    carry = (jnp.int32(0), zero, zero)
    if docs <= 16:
        for doc in range(docs):
            carry = step(doc, carry)
    else:
        carry = lax.fori_loop(0, docs, step, carry)
    return carry[1], carry[2]


def neighbour_slots(shard):
    odd = shard % 2
    ahead, behind = BACK + 1, BACK - 1
    return jnp.where(odd == 1, behind, ahead), jnp.where(odd == 1, ahead, behind)


def grad_kernel(masks, parts, is_first, is_last, range_ref, q_ref, *refs):
    refs = list(refs)
    received = [refs.pop(0) for _ in range(4)] if is_first else []
    cots = [refs.pop(0) for _ in masks]
    window, carried = (None, None) if is_first else (refs.pop(0), refs.pop(0))
    dqs = [refs.pop(0) for _ in masks]
    score_buf, dprob_buf, prob_buf, dscore_buf, q_rows, cot_rows = refs[-6:]
    outs = refs[:-6]
    if is_first:
        window, acc = outs
    else:
        acc = outs.pop()
    rows, heads, size = q_ref.shape
    tokens = rows // parts
    kv_heads = window.shape[1]
    group_size = heads // kv_heads
    span = (BACK + 1 + AHEAD) * rows
    reach = span - rows + tokens
    lanes = tokens * group_size
    scale = size ** (-0.5)
    shard = lax.axis_index("seq")
    me = lax.axis_index("kvh")

    even_slot, odd_slot = neighbour_slots(shard)
    if is_first:
        for slot, ref in zip((BACK, even_slot, 0, odd_slot), received):
            part = pl.ds(pl.multiple_of(slot * rows, rows), rows)
            for number in range(2):
                for group in range(kv_heads):
                    window[number, group, part] = ref[number, group]
        acc[...] = jnp.zeros_like(acc)
    else:
        acc[...] = carried[...]

    contract_last = (((1,), (1,)), ((), ()))
    contract_first = (((0,), (0,)), ((), ()))
    sublane = lax.broadcasted_iota(jnp.int32, (TILE, lanes), 0)
    items = [(place, group) for place in range(len(masks)) for group in range(kv_heads)]

    def key_rows(place, starts, width):
        first = pl.multiple_of((me ^ masks[place]) * tokens, tokens)
        return pl.ds(pl.multiple_of(first + starts[place], ALIGN), width)

    def operands(item, starts, width):
        place, group = items[item]
        first = pl.multiple_of((me ^ masks[place]) * tokens, tokens)
        of_group = pl.ds(group * group_size, group_size)
        q = q_ref[pl.ds(first, tokens), of_group].astype(jnp.float32)
        cot = cots[place][:, of_group].astype(jnp.float32)
        return (
            key_rows(place, starts, width),
            q.reshape(lanes, size).astype(jnp.bfloat16),
            cot.reshape(lanes, size).astype(jnp.bfloat16),
        )

    def scores_of(item, starts, width):
        place, group = items[item]
        slot = item % 2
        here, q, cot = operands(item, starts, width)
        q_rows[slot], cot_rows[slot] = q, cot
        scores = lax.dot_general(
            window[0, group, here], q, contract_last, preferred_element_type=jnp.float32
        )
        low = range_ref[masks[place], 0:1, :] - starts[place] - sublane
        high = range_ref[masks[place], 1:2, :] - starts[place] - sublane
        top = jnp.full((TILE, lanes), NEG, jnp.float32)
        for row in range(0, width, TILE):
            visible = (low <= row) & (high > row)
            tile = jnp.where(visible, scores[row : row + TILE] * (scale * LOG2E), NEG)
            top = jnp.maximum(top, tile)
            score_buf[slot, row : row + TILE] = tile
        dprob_buf[slot, :width] = lax.dot_general(
            window[1, group, here], cot, contract_last, preferred_element_type=jnp.float32
        )
        return jnp.max(top, axis=0, keepdims=True)

    def softmax_of(item, top, width):
        slot = item % 2
        total = jnp.zeros((TILE, lanes), jnp.float32)
        delta = jnp.zeros((TILE, lanes), jnp.float32)
        for row in range(0, width, TILE):
            tile = slice(row, row + TILE)
            expo = jnp.exp2(score_buf[slot, tile] - top)
            total = total + expo
            delta = delta + expo * dprob_buf[slot, tile]
            score_buf[slot, tile] = expo
        inverse = 1.0 / jnp.sum(total, axis=0, keepdims=True)
        delta = jnp.sum(delta, axis=0, keepdims=True) * inverse
        for row in range(0, width, 2 * TILE):
            tile = slice(row, row + 2 * TILE)
            probs = score_buf[slot, tile] * inverse
            dscores = probs * (dprob_buf[slot, tile] - delta)
            prob_buf[slot, tile] = probs.astype(jnp.bfloat16)
            dscore_buf[slot, tile] = dscores.astype(jnp.bfloat16)

    def gradients_of(item, starts, width):
        place, group = items[item]
        slot = item % 2
        here, q, cot = key_rows(place, starts, width), q_rows[slot], cot_rows[slot]
        probs, dscores = prob_buf[slot, :width], dscore_buf[slot, :width]
        acc[1, group, here] += jnp.dot(probs, cot, preferred_element_type=jnp.float32)
        acc[0, group, here] += jnp.dot(dscores, q, preferred_element_type=jnp.float32)
        dq = lax.dot_general(
            window[0, group, here], dscores, contract_first, preferred_element_type=jnp.float32
        )
        dq = jnp.transpose(dq * scale).reshape(tokens, group_size, size)
        dqs[place][:, pl.ds(group * group_size, group_size)] = dq.astype(jnp.bfloat16)

    def chunk(place, width):
        starts = {place: jnp.clip(lowest[place], 0, reach - width)}
        here = [item for item, (of_place, _) in enumerate(items) if of_place == place]
        top = scores_of(here[0], starts, width)
        for item in here:
            later = scores_of(item + 1, starts, width) if item + 1 in here else None
            softmax_of(item, top, width)
            gradients_of(item, starts, width)
            top = later

    lowest = [jnp.min(range_ref[mask, 0:1, :]) & -ALIGN for mask in masks]
    needed = [jnp.max(range_ref[mask, 1:2, :]) - low for mask, low in zip(masks, lowest)]
    widths = [width for width in WIDTHS if width < reach] + [reach]
    for place in range(len(masks)):
        for floor, width in zip([-1] + widths, widths):
            fits = needed[place] > floor
            if width < reach:
                fits = fits & (needed[place] <= width)
            pl.when(fits)(functools.partial(chunk, place, width))

    if not is_last:
        return
    is_odd = (shard % 2).astype(jnp.float32)
    weights = (1.0, 1.0 - is_odd, is_odd, 1.0, 1.0)
    for slot, weight, ref in zip((BACK, 0, 0, even_slot, odd_slot), weights, outs):
        part = pl.ds(pl.multiple_of(slot * rows, rows), rows)
        for group in range(kv_heads):
            ref[0, group] = (acc[0, group, part] * (scale * weight)).astype(ref.dtype)
            ref[1, group] = (acc[1, group, part] * weight).astype(ref.dtype)


def gradients(masks, parts, ranges, queries, cots, blocks, carried):
    rows, heads, size = queries.shape
    is_last = masks == stages(parts)[-1]
    kv_shape = blocks[0].shape
    kv_heads = kv_shape[1]
    span = (BACK + 1 + AHEAD) * rows
    acc_shape = (2, kv_heads, span, size)
    tokens = rows // parts
    tile_shape = (2, span - rows + tokens, tokens * (heads // kv_heads))
    work = heads * rows // parts * span * len(masks)
    outs = [pltpu.VMEM(cots[0].shape, jnp.bfloat16)] * len(masks)
    if is_last:
        outs += [pltpu.VMEM(kv_shape, jnp.float32)] + [pltpu.VMEM(kv_shape, jnp.bfloat16)] * 4
    else:
        outs += [pltpu.VMEM(acc_shape, jnp.bfloat16), pltpu.VMEM(acc_shape, jnp.float32)]
    own, far, even, odd = blocks
    operands = [ranges, queries] + ([own, even, far, odd] if carried is None else [])
    operands += [*cots] + ([] if carried is None else list(carried))
    outs = pl.pallas_call(
        functools.partial(grad_kernel, masks, parts, carried is None, is_last),
        out_shape=tuple(outs),
        in_specs=[_VMEM] * len(operands),
        out_specs=(_VMEM,) * len(outs),
        scratch_shapes=([pltpu.VMEM(acc_shape, jnp.float32)] if is_last else [])
        + [
            pltpu.VMEM(tile_shape, jnp.float32),
            pltpu.VMEM(tile_shape, jnp.float32),
            pltpu.VMEM(tile_shape, jnp.bfloat16),
            pltpu.VMEM(tile_shape, jnp.bfloat16),
            pltpu.VMEM((2, tile_shape[2], size), jnp.bfloat16),
            pltpu.VMEM((2, tile_shape[2], size), jnp.bfloat16),
        ],
        compiler_params=pltpu.CompilerParams(vmem_limit_bytes=VMEM_BYTES),
        cost_estimate=pl.CostEstimate(
            flops=10 * work * size, bytes_accessed=4 * queries.size * 2, transcendentals=work
        ),
        name="gradients",
    )(*operands)
    return outs[: len(masks)], outs[len(masks) :]


def add_kernel(left, right, out):
    out[...] = (left[...].astype(jnp.float32) + right[...].astype(jnp.float32)).astype(out.dtype)


def add(left, right):
    return pl.pallas_call(
        add_kernel,
        out_shape=pltpu.VMEM(left.shape, left.dtype),
        in_specs=[_VMEM] * 2,
        out_specs=_VMEM,
        compiler_params=pltpu.CompilerParams(vmem_limit_bytes=VMEM_BYTES),
        name="add",
    )(left, right)


def finish_order(parts):
    return [1, *range(3, parts), "far", "odd", "even", 2, 0, "own"]


def finish_kernel(parts, *refs):
    *refs, dq_out, dk_out, dv_out, dk_buf, dv_buf, sems = refs
    refs = dict(zip(finish_order(parts), refs))
    heads = refs[0].shape[1]
    me = lax.axis_index("kvh")
    copies = []
    for mask in range(parts):
        first = pl.multiple_of((me ^ mask) * heads, heads)
        copies.append(
            pltpu.make_async_copy(refs[mask], dq_out.at[:, pl.ds(first, heads), :], sems.at[mask])
        )
        copies[-1].start()
    for number, (buf, ref) in enumerate(((dk_buf, dk_out), (dv_buf, dv_out))):
        sums = []
        for group in range(buf.shape[1]):
            total = refs["own"][number, group]
            for name in ("far", "even", "odd"):
                total = total + refs[name][number, group].astype(jnp.float32)
            sums.append(total)
        buf[...] = jnp.stack(sums, axis=1).astype(jnp.bfloat16)
        copies.append(pltpu.make_async_copy(buf, ref, sems.at[parts + number]))
        copies[-1].start()
    for copy in copies:
        copy.wait()


def finish(dqs, partials):
    parts = len(dqs)
    rows, heads, size = dqs[0].shape
    _, kv_heads, kv_rows, _ = partials[0].shape
    kv_shape = (kv_rows, kv_heads, size)
    kv_out = jax.ShapeDtypeStruct(kv_shape, jnp.bfloat16)
    operands = dict(enumerate(dqs)) | dict(zip(("own", "far", "even", "odd"), partials))
    return pl.pallas_call(
        functools.partial(finish_kernel, parts),
        out_shape=(
            jax.ShapeDtypeStruct((rows, heads * parts, size), jnp.bfloat16),
            kv_out,
            kv_out,
        ),
        in_specs=[_VMEM] * (parts + 4),
        out_specs=(_HBM,) * 3,
        scratch_shapes=[
            pltpu.VMEM(kv_shape, jnp.bfloat16),
            pltpu.VMEM(kv_shape, jnp.bfloat16),
            pltpu.SemaphoreType.DMA((parts + 2,)),
        ],
        compiler_params=pltpu.CompilerParams(vmem_limit_bytes=VMEM_BYTES),
        name="finish",
    )(*[operands[name] for name in finish_order(parts)])


def shifted(block, distance):
    count = lax.axis_size("seq")
    return lax.ppermute(block, "seq", [(i, (i + distance) % count) for i in range(count)])


def paired(block):
    return lax.ppermute(block, "seq", [(i, i ^ 1) for i in range(lax.axis_size("seq"))])


def ringed(block, direction=1):
    count = lax.axis_size("seq")
    route = []
    for i in range(count):
        target = i + 2 if i % 2 == 0 else i - 2
        route.append((i, min(max(target, 0), count - 1))[::direction])
    return lax.ppermute(block, "seq", route)


def swapped(block, mask):
    return lax.ppermute(block, "kvh", [(i, i ^ mask) for i in range(lax.axis_size("kvh"))])


def local(queries, keys, values, output_gradient, doc_lengths, prefix_lengths):
    parts = lax.axis_size("kvh")
    kv, cots, ranges = prepare(
        doc_lengths, prefix_lengths, output_gradient, keys, values, parts
    )
    even = paired(kv[2])
    blocks = [kv[0], shifted(kv[1], BACK), even, ringed(even)]
    cots = [cots[0]] + [swapped(cots[mask], mask) for mask in range(1, parts)]
    dqs, carried = {}, None
    for masks in stages(parts):
        found, carried = gradients(
            masks, parts, ranges, queries, [cots[mask] for mask in masks], blocks, carried
        )
        for mask, dq in zip(masks, found):
            dqs[mask] = swapped(dq, mask) if mask else dq
    own, far_even, far_odd, even, odd = carried
    relayed = add(paired(odd), far_odd)
    partials = [own, ringed(far_even, -1), paired(even), ringed(relayed)]
    return finish([dqs[mask] for mask in range(parts)], partials)


def solution(mesh):
    in_specs = (
        P("seq", "kvh", None),
        P("seq", "kvh", None),
        P("seq", "kvh", None),
        P(("seq", "kvh"), None, None),
        P(),
        P(),
    )
    out_specs = (P(("seq", "kvh"), None, None), P("seq", "kvh", None), P("seq", "kvh", None))
    return jax.shard_map(local, mesh=mesh, in_specs=in_specs, out_specs=out_specs, check_vma=False)
```

```python
import functools

import jax
import jax.numpy as jnp
from jax import lax
from jax.experimental import pallas as pl
from jax.experimental.pallas import tpu as pltpu
from jax.sharding import PartitionSpec as P

BACK = 2
AHEAD = 1
LOG2E = 1.4426950408889634
VMEM_BYTES = 40 * 1024 * 1024
NEG = -1e30
TILE = 8
ALIGN = 16
WIDTHS = (176, 304)

_VMEM = pl.BlockSpec(memory_space=pltpu.VMEM)
_SMEM = pl.BlockSpec(memory_space=pltpu.SMEM)
_HBM = pl.BlockSpec(memory_space=pltpu.HBM)


def stages(parts):
    rest = list(range(parts - 1, 1, -1))
    return [[0, 1, *rest[:-1]], rest[-1:]]


def regroup(buf):
    wide = buf[...].astype(jnp.float32)
    return [wide[:, group, :].astype(jnp.bfloat16) for group in range(buf.shape[1])]


def prep_kernel(parts, lengths_ref, prefixes_ref, cot_ref, key_ref, value_ref, *rest):
    kv_outs, cot_outs, rest = rest[:3], rest[3 : parts + 3], rest[parts + 3 :]
    range_out, key_buf, value_buf, lengths, prefixes, sems, scalar_sems = rest
    heads = cot_ref.shape[1] // parts
    me = lax.axis_index("kvh")
    scalars = [
        pltpu.make_async_copy(lengths_ref, lengths, scalar_sems.at[0]),
        pltpu.make_async_copy(prefixes_ref, prefixes, scalar_sems.at[1]),
    ]
    for copy in scalars:
        copy.start()
    loads = []
    for number, (ref, buf) in enumerate(((key_ref, key_buf), (value_ref, value_buf))):
        loads.append(pltpu.make_async_copy(ref, buf, sems.at[number]))
        loads[-1].start()
    copies = []
    for mask in range(parts):
        first = pl.multiple_of((me ^ mask) * heads, heads)
        copies.append(
            pltpu.make_async_copy(
                cot_ref.at[:, pl.ds(first, heads), :], cot_outs[mask], sems.at[mask + 2]
            )
        )
        copies[-1].start()
    for number, buf in enumerate((key_buf, value_buf)):
        loads[number].wait()
        for group, block in enumerate(regroup(buf)):
            for kv_out in kv_outs:
                kv_out[number, group] = block
    for copy in scalars:
        copy.wait()
    rows = key_buf.shape[0]
    tokens = rows // parts
    lanes = range_out.shape[2]
    lane_token = lax.broadcasted_iota(jnp.int32, (1, lanes), 1) // (lanes // tokens)
    shard = lax.axis_index("seq")
    for mask in range(parts):
        first = (me ^ mask) * tokens
        low, high = bounds(shard * rows + first + lane_token, lengths, prefixes)
        origin = (shard - BACK) * rows + first
        range_out[mask, 0:1, :] = low - origin
        range_out[mask, 1:2, :] = high - origin
    for copy in copies:
        copy.wait()


def prepare(lengths, prefixes, cotangent, keys, values, parts):
    rows, heads, size = cotangent.shape
    kv_rows, kv_heads, _ = keys.shape
    lanes = kv_rows // parts * (heads // parts // kv_heads)
    piece = pltpu.VMEM((rows, heads // parts, size), jnp.bfloat16)
    block = pltpu.VMEM((2, kv_heads, kv_rows, size), jnp.bfloat16)
    operands = [
        pltpu.with_memory_space_constraint(array, pltpu.HBM)
        for array in (lengths, prefixes, cotangent, keys, values)
    ]
    outs = pl.pallas_call(
        functools.partial(prep_kernel, parts),
        out_shape=(block,) * 3 + (piece,) * parts + (pltpu.VMEM((parts, 2, lanes), jnp.int32),),
        in_specs=[_HBM] * 5,
        out_specs=(_VMEM,) * (parts + 4),
        scratch_shapes=[
            pltpu.VMEM(keys.shape, jnp.bfloat16),
            pltpu.VMEM(values.shape, jnp.bfloat16),
            pltpu.SMEM(lengths.shape, jnp.int32),
            pltpu.SMEM(prefixes.shape, jnp.int32),
            pltpu.SemaphoreType.DMA((parts + 2,)),
            pltpu.SemaphoreType.DMA((2,)),
        ],
        compiler_params=pltpu.CompilerParams(vmem_limit_bytes=VMEM_BYTES),
        name="prepare",
    )(*operands)
    return outs[:3], outs[3:-1], outs[-1]


def bounds(position, lengths, prefixes):
    docs = lengths.shape[0]

    def step(doc, carry):
        start, low, high = carry
        end = start + lengths[doc]
        inside = (position >= start) & (position < end)
        reach = jnp.minimum(end, jnp.maximum(position + 1, start + prefixes[doc]))
        return end, jnp.where(inside, start, low), jnp.where(inside, reach, high)

    zero = jnp.zeros_like(position)
    carry = (jnp.int32(0), zero, zero)
    if docs <= 16:
        for doc in range(docs):
            carry = step(doc, carry)
    else:
        carry = lax.fori_loop(0, docs, step, carry)
    return carry[1], carry[2]


def neighbour_slots(shard):
    odd = shard % 2
    ahead, behind = BACK + 1, BACK - 1
    return jnp.where(odd == 1, behind, ahead), jnp.where(odd == 1, ahead, behind)


def grad_kernel(masks, parts, is_first, is_last, range_ref, q_ref, *refs):
    refs = list(refs)
    received = [refs.pop(0) for _ in range(4)] if is_first else []
    cots = [refs.pop(0) for _ in masks]
    window, carried = (None, None) if is_first else (refs.pop(0), refs.pop(0))
    dqs = [refs.pop(0) for _ in masks]
    score_buf, dprob_buf, prob_buf, dscore_buf, q_rows, cot_rows = refs[-6:]
    outs = refs[:-6]
    if is_first:
        window, acc = outs
    else:
        acc = outs.pop()
    rows, heads, size = q_ref.shape
    tokens = rows // parts
    kv_heads = window.shape[1]
    group_size = heads // kv_heads
    span = (BACK + 1 + AHEAD) * rows
    reach = span - rows + tokens
    lanes = tokens * group_size
    scale = size ** (-0.5)
    shard = lax.axis_index("seq")
    me = lax.axis_index("kvh")

    even_slot, odd_slot = neighbour_slots(shard)
    if is_first:
        for slot, ref in zip((BACK, even_slot, 0, odd_slot), received):
            part = pl.ds(pl.multiple_of(slot * rows, rows), rows)
            for number in range(2):
                for group in range(kv_heads):
                    window[number, group, part] = ref[number, group]
        acc[...] = jnp.zeros_like(acc)
    else:
        acc[...] = carried[...]

    contract_last = (((1,), (1,)), ((), ()))
    contract_first = (((0,), (0,)), ((), ()))
    sublane = lax.broadcasted_iota(jnp.int32, (TILE, lanes), 0)
    items = [(place, group) for place in range(len(masks)) for group in range(kv_heads)]

    def key_rows(place, starts, width):
        first = pl.multiple_of((me ^ masks[place]) * tokens, tokens)
        return pl.ds(pl.multiple_of(first + starts[place], ALIGN), width)

    def operands(item, starts, width):
        place, group = items[item]
        first = pl.multiple_of((me ^ masks[place]) * tokens, tokens)
        of_group = pl.ds(group * group_size, group_size)
        q = q_ref[pl.ds(first, tokens), of_group].astype(jnp.float32)
        cot = cots[place][:, of_group].astype(jnp.float32)
        return (
            key_rows(place, starts, width),
            q.reshape(lanes, size).astype(jnp.bfloat16),
            cot.reshape(lanes, size).astype(jnp.bfloat16),
        )

    def scores_of(item, starts, width):
        place, group = items[item]
        slot = item % 2
        here, q, cot = operands(item, starts, width)
        q_rows[slot], cot_rows[slot] = q, cot
        scores = lax.dot_general(
            window[0, group, here], q, contract_last, preferred_element_type=jnp.float32
        )
        low = range_ref[masks[place], 0:1, :] - starts[place] - sublane
        high = range_ref[masks[place], 1:2, :] - starts[place] - sublane
        top = jnp.full((TILE, lanes), NEG, jnp.float32)
        for row in range(0, width, TILE):
            visible = (low <= row) & (high > row)
            tile = jnp.where(visible, scores[row : row + TILE] * (scale * LOG2E), NEG)
            top = jnp.maximum(top, tile)
            score_buf[slot, row : row + TILE] = tile
        dprob_buf[slot, :width] = lax.dot_general(
            window[1, group, here], cot, contract_last, preferred_element_type=jnp.float32
        )
        return jnp.max(top, axis=0, keepdims=True)

    def softmax_of(item, top, width):
        slot = item % 2
        total = jnp.zeros((TILE, lanes), jnp.float32)
        delta = jnp.zeros((TILE, lanes), jnp.float32)
        for row in range(0, width, TILE):
            tile = slice(row, row + TILE)
            expo = jnp.exp2(score_buf[slot, tile] - top)
            total = total + expo
            delta = delta + expo * dprob_buf[slot, tile]
            score_buf[slot, tile] = expo
        inverse = 1.0 / jnp.sum(total, axis=0, keepdims=True)
        delta = jnp.sum(delta, axis=0, keepdims=True) * inverse
        for row in range(0, width, 2 * TILE):
            tile = slice(row, row + 2 * TILE)
            probs = score_buf[slot, tile] * inverse
            dscores = probs * (dprob_buf[slot, tile] - delta)
            prob_buf[slot, tile] = probs.astype(jnp.bfloat16)
            dscore_buf[slot, tile] = dscores.astype(jnp.bfloat16)

    def gradients_of(item, starts, width):
        place, group = items[item]
        slot = item % 2
        here, q, cot = key_rows(place, starts, width), q_rows[slot], cot_rows[slot]
        probs, dscores = prob_buf[slot, :width], dscore_buf[slot, :width]
        acc[1, group, here] += jnp.dot(probs, cot, preferred_element_type=jnp.float32)
        acc[0, group, here] += jnp.dot(dscores, q, preferred_element_type=jnp.float32)
        dq = lax.dot_general(
            window[0, group, here], dscores, contract_first, preferred_element_type=jnp.float32
        )
        dq = jnp.transpose(dq * scale).reshape(tokens, group_size, size)
        dqs[place][:, pl.ds(group * group_size, group_size)] = dq.astype(jnp.bfloat16)

    def run(places, width):
        starts = {place: jnp.clip(lowest[place], 0, reach - width) for place in places}
        here = [item for item, (place, _) in enumerate(items) if place in places]
        top = scores_of(here[0], starts, width)
        for item in here:
            later = scores_of(item + 1, starts, width) if item + 1 in here else None
            softmax_of(item, top, width)
            gradients_of(item, starts, width)
            top = later

    lowest = [jnp.min(range_ref[mask, 0:1, :]) & -ALIGN for mask in masks]
    needed = [jnp.max(range_ref[mask, 1:2, :]) - low for mask, low in zip(masks, lowest)]
    widths = [width for width in WIDTHS if width < reach] + [reach]
    every = range(len(masks))
    together = functools.reduce(jnp.maximum, needed) <= widths[0]
    pl.when(together)(functools.partial(run, every, widths[0]))

    def apart():
        for place in every:
            for floor, width in zip([-1] + widths, widths):
                fits = needed[place] > floor
                if width < reach:
                    fits = fits & (needed[place] <= width)
                pl.when(fits)(functools.partial(run, [place], width))

    pl.when(jnp.logical_not(together))(apart)

    if not is_last:
        return
    is_odd = (shard % 2).astype(jnp.float32)
    weights = (1.0, 1.0 - is_odd, is_odd, 1.0, 1.0)
    for slot, weight, ref in zip((BACK, 0, 0, even_slot, odd_slot), weights, outs):
        part = pl.ds(pl.multiple_of(slot * rows, rows), rows)
        for group in range(kv_heads):
            ref[0, group] = (acc[0, group, part] * (scale * weight)).astype(ref.dtype)
            ref[1, group] = (acc[1, group, part] * weight).astype(ref.dtype)


def gradients(masks, parts, ranges, queries, cots, blocks, carried):
    rows, heads, size = queries.shape
    is_last = masks == stages(parts)[-1]
    kv_shape = blocks[0].shape
    kv_heads = kv_shape[1]
    span = (BACK + 1 + AHEAD) * rows
    acc_shape = (2, kv_heads, span, size)
    tokens = rows // parts
    tile_shape = (2, span - rows + tokens, tokens * (heads // kv_heads))
    work = heads * rows // parts * span * len(masks)
    outs = [pltpu.VMEM(cots[0].shape, jnp.bfloat16)] * len(masks)
    if is_last:
        outs += [pltpu.VMEM(kv_shape, jnp.float32)] + [pltpu.VMEM(kv_shape, jnp.bfloat16)] * 4
    else:
        outs += [pltpu.VMEM(acc_shape, jnp.bfloat16), pltpu.VMEM(acc_shape, jnp.float32)]
    own, far, even, odd = blocks
    operands = [ranges, queries] + ([own, even, far, odd] if carried is None else [])
    operands += [*cots] + ([] if carried is None else list(carried))
    outs = pl.pallas_call(
        functools.partial(grad_kernel, masks, parts, carried is None, is_last),
        out_shape=tuple(outs),
        in_specs=[_VMEM] * len(operands),
        out_specs=(_VMEM,) * len(outs),
        scratch_shapes=([pltpu.VMEM(acc_shape, jnp.float32)] if is_last else [])
        + [
            pltpu.VMEM(tile_shape, jnp.float32),
            pltpu.VMEM(tile_shape, jnp.float32),
            pltpu.VMEM(tile_shape, jnp.bfloat16),
            pltpu.VMEM(tile_shape, jnp.bfloat16),
            pltpu.VMEM((2, tile_shape[2], size), jnp.bfloat16),
            pltpu.VMEM((2, tile_shape[2], size), jnp.bfloat16),
        ],
        compiler_params=pltpu.CompilerParams(vmem_limit_bytes=VMEM_BYTES),
        cost_estimate=pl.CostEstimate(
            flops=10 * work * size, bytes_accessed=4 * queries.size * 2, transcendentals=work
        ),
        name="gradients",
    )(*operands)
    return outs[: len(masks)], outs[len(masks) :]


def add_kernel(left, right, out):
    out[...] = (left[...].astype(jnp.float32) + right[...].astype(jnp.float32)).astype(out.dtype)


def add(left, right):
    return pl.pallas_call(
        add_kernel,
        out_shape=pltpu.VMEM(left.shape, left.dtype),
        in_specs=[_VMEM] * 2,
        out_specs=_VMEM,
        compiler_params=pltpu.CompilerParams(vmem_limit_bytes=VMEM_BYTES),
        name="add",
    )(left, right)


def finish_order(parts):
    return [1, *range(3, parts), "far", "odd", "even", 2, 0, "own"]


def finish_kernel(parts, *refs):
    *refs, dq_out, dk_out, dv_out, dk_buf, dv_buf, sems = refs
    refs = dict(zip(finish_order(parts), refs))
    heads = refs[0].shape[1]
    me = lax.axis_index("kvh")
    copies = []
    for mask in range(parts):
        first = pl.multiple_of((me ^ mask) * heads, heads)
        copies.append(
            pltpu.make_async_copy(refs[mask], dq_out.at[:, pl.ds(first, heads), :], sems.at[mask])
        )
        copies[-1].start()
    for number, (buf, ref) in enumerate(((dk_buf, dk_out), (dv_buf, dv_out))):
        sums = []
        for group in range(buf.shape[1]):
            total = refs["own"][number, group]
            for name in ("far", "even", "odd"):
                total = total + refs[name][number, group].astype(jnp.float32)
            sums.append(total)
        buf[...] = jnp.stack(sums, axis=1).astype(jnp.bfloat16)
        copies.append(pltpu.make_async_copy(buf, ref, sems.at[parts + number]))
        copies[-1].start()
    for copy in copies:
        copy.wait()


def finish(dqs, partials):
    parts = len(dqs)
    rows, heads, size = dqs[0].shape
    _, kv_heads, kv_rows, _ = partials[0].shape
    kv_shape = (kv_rows, kv_heads, size)
    kv_out = jax.ShapeDtypeStruct(kv_shape, jnp.bfloat16)
    operands = dict(enumerate(dqs)) | dict(zip(("own", "far", "even", "odd"), partials))
    return pl.pallas_call(
        functools.partial(finish_kernel, parts),
        out_shape=(
            jax.ShapeDtypeStruct((rows, heads * parts, size), jnp.bfloat16),
            kv_out,
            kv_out,
        ),
        in_specs=[_VMEM] * (parts + 4),
        out_specs=(_HBM,) * 3,
        scratch_shapes=[
            pltpu.VMEM(kv_shape, jnp.bfloat16),
            pltpu.VMEM(kv_shape, jnp.bfloat16),
            pltpu.SemaphoreType.DMA((parts + 2,)),
        ],
        compiler_params=pltpu.CompilerParams(vmem_limit_bytes=VMEM_BYTES),
        name="finish",
    )(*[operands[name] for name in finish_order(parts)])


def shifted(block, distance):
    count = lax.axis_size("seq")
    return lax.ppermute(block, "seq", [(i, (i + distance) % count) for i in range(count)])


def paired(block):
    return lax.ppermute(block, "seq", [(i, i ^ 1) for i in range(lax.axis_size("seq"))])


def ringed(block, direction=1):
    count = lax.axis_size("seq")
    route = []
    for i in range(count):
        target = i + 2 if i % 2 == 0 else i - 2
        route.append((i, min(max(target, 0), count - 1))[::direction])
    return lax.ppermute(block, "seq", route)


def swapped(block, mask):
    return lax.ppermute(block, "kvh", [(i, i ^ mask) for i in range(lax.axis_size("kvh"))])


def local(queries, keys, values, output_gradient, doc_lengths, prefix_lengths):
    parts = lax.axis_size("kvh")
    kv, cots, ranges = prepare(
        doc_lengths, prefix_lengths, output_gradient, keys, values, parts
    )
    even = paired(kv[2])
    blocks = [kv[0], shifted(kv[1], BACK), even, ringed(even)]
    cots = [cots[0]] + [swapped(cots[mask], mask) for mask in range(1, parts)]
    dqs, carried = {}, None
    for masks in stages(parts):
        found, carried = gradients(
            masks, parts, ranges, queries, [cots[mask] for mask in masks], blocks, carried
        )
        for mask, dq in zip(masks, found):
            dqs[mask] = swapped(dq, mask) if mask else dq
    own, far_even, far_odd, even, odd = carried
    relayed = add(paired(odd), far_odd)
    partials = [own, ringed(far_even, -1), paired(even), ringed(relayed)]
    return finish([dqs[mask] for mask in range(parts)], partials)


def solution(mesh):
    in_specs = (
        P("seq", "kvh", None),
        P("seq", "kvh", None),
        P("seq", "kvh", None),
        P(("seq", "kvh"), None, None),
        P(),
        P(),
    )
    out_specs = (P(("seq", "kvh"), None, None), P("seq", "kvh", None), P("seq", "kvh", None))
    return jax.shard_map(local, mesh=mesh, in_specs=in_specs, out_specs=out_specs, check_vma=False)
```

```python
import functools

import jax
import jax.numpy as jnp
from jax import lax
from jax.experimental import pallas as pl
from jax.experimental.pallas import tpu as pltpu
from jax.sharding import PartitionSpec as P

BACK = 2
AHEAD = 1
LOG2E = 1.4426950408889634
VMEM_BYTES = 40 * 1024 * 1024
NEG = -1e30
TILE = 8
ALIGN = 16
WIDTHS = (176, 304)

_VMEM = pl.BlockSpec(memory_space=pltpu.VMEM)
_SMEM = pl.BlockSpec(memory_space=pltpu.SMEM)
_HBM = pl.BlockSpec(memory_space=pltpu.HBM)


def stages(parts):
    rest = list(range(parts - 1, 1, -1))
    return [[0, 1, *rest[:-1]], rest[-1:]]


def regroup(buf):
    wide = buf[...].astype(jnp.float32)
    return [wide[:, group, :].astype(jnp.bfloat16) for group in range(buf.shape[1])]


def prep_kernel(parts, lengths_ref, prefixes_ref, cot_ref, key_ref, value_ref, *rest):
    kv_outs, cot_outs, rest = rest[:3], rest[3 : parts + 3], rest[parts + 3 :]
    range_out, key_buf, value_buf, lengths, prefixes, sems, scalar_sems = rest
    heads = cot_ref.shape[1] // parts
    me = lax.axis_index("kvh")
    scalars = [
        pltpu.make_async_copy(lengths_ref, lengths, scalar_sems.at[0]),
        pltpu.make_async_copy(prefixes_ref, prefixes, scalar_sems.at[1]),
    ]
    for copy in scalars:
        copy.start()
    loads = []
    for number, (ref, buf) in enumerate(((key_ref, key_buf), (value_ref, value_buf))):
        loads.append(pltpu.make_async_copy(ref, buf, sems.at[number]))
        loads[-1].start()
    copies = []
    for mask in range(parts):
        first = pl.multiple_of((me ^ mask) * heads, heads)
        copies.append(
            pltpu.make_async_copy(
                cot_ref.at[:, pl.ds(first, heads), :], cot_outs[mask], sems.at[mask + 2]
            )
        )
        copies[-1].start()
    for number, buf in enumerate((key_buf, value_buf)):
        loads[number].wait()
        for group, block in enumerate(regroup(buf)):
            for kv_out in kv_outs:
                kv_out[number, group] = block
    for copy in scalars:
        copy.wait()
    rows = key_buf.shape[0]
    tokens = rows // parts
    lanes = range_out.shape[2]
    lane_token = lax.broadcasted_iota(jnp.int32, (1, lanes), 1) // (lanes // tokens)
    shard = lax.axis_index("seq")
    for mask in range(parts):
        first = (me ^ mask) * tokens
        low, high = bounds(shard * rows + first + lane_token, lengths, prefixes)
        origin = (shard - BACK) * rows + first
        range_out[mask, 0:1, :] = low - origin
        range_out[mask, 1:2, :] = high - origin
    for copy in copies:
        copy.wait()


def prepare(lengths, prefixes, cotangent, keys, values, parts):
    rows, heads, size = cotangent.shape
    kv_rows, kv_heads, _ = keys.shape
    lanes = kv_rows // parts * (heads // parts // kv_heads)
    piece = pltpu.VMEM((rows, heads // parts, size), jnp.bfloat16)
    block = pltpu.VMEM((2, kv_heads, kv_rows, size), jnp.bfloat16)
    operands = [
        pltpu.with_memory_space_constraint(array, pltpu.HBM)
        for array in (lengths, prefixes, cotangent, keys, values)
    ]
    outs = pl.pallas_call(
        functools.partial(prep_kernel, parts),
        out_shape=(block,) * 3 + (piece,) * parts + (pltpu.VMEM((parts, 2, lanes), jnp.int32),),
        in_specs=[_HBM] * 5,
        out_specs=(_VMEM,) * (parts + 4),
        scratch_shapes=[
            pltpu.VMEM(keys.shape, jnp.bfloat16),
            pltpu.VMEM(values.shape, jnp.bfloat16),
            pltpu.SMEM(lengths.shape, jnp.int32),
            pltpu.SMEM(prefixes.shape, jnp.int32),
            pltpu.SemaphoreType.DMA((parts + 2,)),
            pltpu.SemaphoreType.DMA((2,)),
        ],
        compiler_params=pltpu.CompilerParams(vmem_limit_bytes=VMEM_BYTES),
        name="prepare",
    )(*operands)
    return outs[:3], outs[3:-1], outs[-1]


def bounds(position, lengths, prefixes):
    docs = lengths.shape[0]

    def step(doc, carry):
        start, low, high = carry
        end = start + lengths[doc]
        inside = (position >= start) & (position < end)
        reach = jnp.minimum(end, jnp.maximum(position + 1, start + prefixes[doc]))
        return end, jnp.where(inside, start, low), jnp.where(inside, reach, high)

    zero = jnp.zeros_like(position)
    carry = (jnp.int32(0), zero, zero)
    if docs <= 16:
        for doc in range(docs):
            carry = step(doc, carry)
    else:
        carry = lax.fori_loop(0, docs, step, carry)
    return carry[1], carry[2]


def neighbour_slots(shard):
    odd = shard % 2
    ahead, behind = BACK + 1, BACK - 1
    return jnp.where(odd == 1, behind, ahead), jnp.where(odd == 1, ahead, behind)


def grad_kernel(masks, parts, is_first, is_last, range_ref, q_ref, *refs):
    refs = list(refs)
    received = [refs.pop(0) for _ in range(4)] if is_first else []
    cots = [refs.pop(0) for _ in masks]
    window, carried = (None, None) if is_first else (refs.pop(0), refs.pop(0))
    dqs = [refs.pop(0) for _ in masks]
    score_buf, dprob_buf, prob_buf, dscore_buf, q_rows, cot_rows = refs[-6:]
    outs = refs[:-6]
    if is_first:
        window, acc = outs
    else:
        acc = outs.pop()
    rows, heads, size = q_ref.shape
    tokens = rows // parts
    kv_heads = window.shape[1]
    group_size = heads // kv_heads
    span = (BACK + 1 + AHEAD) * rows
    reach = span - rows + tokens
    lanes = tokens * group_size
    scale = size ** (-0.5)
    shard = lax.axis_index("seq")
    me = lax.axis_index("kvh")

    even_slot, odd_slot = neighbour_slots(shard)
    if is_first:
        for slot, ref in zip((BACK, even_slot, 0, odd_slot), received):
            part = pl.ds(pl.multiple_of(slot * rows, rows), rows)
            for number in range(2):
                for group in range(kv_heads):
                    window[number, group, part] = ref[number, group]
        acc[...] = jnp.zeros_like(acc)
    else:
        acc[...] = carried[...]

    contract_last = (((1,), (1,)), ((), ()))
    contract_first = (((0,), (0,)), ((), ()))
    sublane = lax.broadcasted_iota(jnp.int32, (TILE, lanes), 0)
    items = [(place, group) for place in range(len(masks)) for group in range(kv_heads)]

    def key_rows(place, starts, width):
        first = pl.multiple_of((me ^ masks[place]) * tokens, tokens)
        return pl.ds(pl.multiple_of(first + starts[place], ALIGN), width)

    def operands(item, starts, width):
        place, group = items[item]
        first = pl.multiple_of((me ^ masks[place]) * tokens, tokens)
        of_group = pl.ds(group * group_size, group_size)
        q = q_ref[pl.ds(first, tokens), of_group].astype(jnp.float32)
        cot = cots[place][:, of_group].astype(jnp.float32)
        return (
            key_rows(place, starts, width),
            q.reshape(lanes, size).astype(jnp.bfloat16),
            cot.reshape(lanes, size).astype(jnp.bfloat16),
        )

    def scores_of(item, starts, width):
        place, group = items[item]
        slot = item % 2
        here, q, cot = operands(item, starts, width)
        q_rows[slot], cot_rows[slot] = q, cot
        scores = lax.dot_general(
            window[0, group, here], q, contract_last, preferred_element_type=jnp.float32
        )
        low = range_ref[masks[place], 0:1, :] - starts[place] - sublane
        high = range_ref[masks[place], 1:2, :] - starts[place] - sublane
        top = jnp.full((TILE, lanes), NEG, jnp.float32)
        for row in range(0, width, TILE):
            visible = (low <= row) & (high > row)
            tile = jnp.where(visible, scores[row : row + TILE] * (scale * LOG2E), NEG)
            top = jnp.maximum(top, tile)
            score_buf[slot, row : row + TILE] = tile
        dprob_buf[slot, :width] = lax.dot_general(
            window[1, group, here], cot, contract_last, preferred_element_type=jnp.float32
        )
        return jnp.max(top, axis=0, keepdims=True)

    def softmax_of(item, top, width):
        slot = item % 2
        total = jnp.zeros((TILE, lanes), jnp.float32)
        delta = jnp.zeros((TILE, lanes), jnp.float32)
        for row in range(0, width, TILE):
            tile = slice(row, row + TILE)
            expo = jnp.exp2(score_buf[slot, tile] - top)
            total = total + expo
            delta = delta + expo * dprob_buf[slot, tile]
            score_buf[slot, tile] = expo
        inverse = 1.0 / jnp.sum(total, axis=0, keepdims=True)
        delta = jnp.sum(delta, axis=0, keepdims=True) * inverse
        for row in range(0, width, 2 * TILE):
            tile = slice(row, row + 2 * TILE)
            probs = score_buf[slot, tile] * inverse
            dscores = probs * (dprob_buf[slot, tile] - delta)
            prob_buf[slot, tile] = probs.astype(jnp.bfloat16)
            dscore_buf[slot, tile] = dscores.astype(jnp.bfloat16)

    def gradients_of(item, starts, width):
        place, group = items[item]
        slot = item % 2
        here, q, cot = key_rows(place, starts, width), q_rows[slot], cot_rows[slot]
        probs, dscores = prob_buf[slot, :width], dscore_buf[slot, :width]
        acc[1, group, here] += jnp.dot(probs, cot, preferred_element_type=jnp.float32)
        acc[0, group, here] += jnp.dot(dscores, q, preferred_element_type=jnp.float32)
        dq = lax.dot_general(
            window[0, group, here], dscores, contract_first, preferred_element_type=jnp.float32
        )
        dq = jnp.transpose(dq * scale).reshape(tokens, group_size, size)
        dqs[place][:, pl.ds(group * group_size, group_size)] = dq.astype(jnp.bfloat16)

    def run(places, width):
        starts = {place: jnp.clip(lowest[place], 0, reach - width) for place in places}
        here = [item for item, (place, _) in enumerate(items) if place in places]
        top = scores_of(here[0], starts, width)
        for item in here:
            later = scores_of(item + 1, starts, width) if item + 1 in here else None
            softmax_of(item, top, width)
            gradients_of(item, starts, width)
            top = later

    lowest = [jnp.min(range_ref[mask, 0:1, :]) & -ALIGN for mask in masks]
    needed = [jnp.max(range_ref[mask, 1:2, :]) - low for mask, low in zip(masks, lowest)]
    widths = [width for width in WIDTHS if width < reach] + [reach]
    every = range(len(masks))
    most = functools.reduce(jnp.maximum, needed)
    together = most <= widths[-2]
    for floor, width in zip([-1] + widths, widths[:-1]):
        pl.when((most > floor) & (most <= width))(functools.partial(run, every, width))

    def apart():
        for place in every:
            for floor, width in zip([-1] + widths, widths):
                fits = needed[place] > floor
                if width < reach:
                    fits = fits & (needed[place] <= width)
                pl.when(fits)(functools.partial(run, [place], width))

    pl.when(jnp.logical_not(together))(apart)

    if not is_last:
        return
    is_odd = (shard % 2).astype(jnp.float32)
    weights = (1.0, 1.0 - is_odd, is_odd, 1.0, 1.0)
    for slot, weight, ref in zip((BACK, 0, 0, even_slot, odd_slot), weights, outs):
        part = pl.ds(pl.multiple_of(slot * rows, rows), rows)
        for group in range(kv_heads):
            ref[0, group] = (acc[0, group, part] * (scale * weight)).astype(ref.dtype)
            ref[1, group] = (acc[1, group, part] * weight).astype(ref.dtype)


def gradients(masks, parts, ranges, queries, cots, blocks, carried):
    rows, heads, size = queries.shape
    is_last = masks == stages(parts)[-1]
    kv_shape = blocks[0].shape
    kv_heads = kv_shape[1]
    span = (BACK + 1 + AHEAD) * rows
    acc_shape = (2, kv_heads, span, size)
    tokens = rows // parts
    tile_shape = (2, span - rows + tokens, tokens * (heads // kv_heads))
    work = heads * rows // parts * span * len(masks)
    outs = [pltpu.VMEM(cots[0].shape, jnp.bfloat16)] * len(masks)
    if is_last:
        outs += [pltpu.VMEM(kv_shape, jnp.float32)] + [pltpu.VMEM(kv_shape, jnp.bfloat16)] * 4
    else:
        outs += [pltpu.VMEM(acc_shape, jnp.bfloat16), pltpu.VMEM(acc_shape, jnp.float32)]
    own, far, even, odd = blocks
    operands = [ranges, queries] + ([own, even, far, odd] if carried is None else [])
    operands += [*cots] + ([] if carried is None else list(carried))
    outs = pl.pallas_call(
        functools.partial(grad_kernel, masks, parts, carried is None, is_last),
        out_shape=tuple(outs),
        in_specs=[_VMEM] * len(operands),
        out_specs=(_VMEM,) * len(outs),
        scratch_shapes=([pltpu.VMEM(acc_shape, jnp.float32)] if is_last else [])
        + [
            pltpu.VMEM(tile_shape, jnp.float32),
            pltpu.VMEM(tile_shape, jnp.float32),
            pltpu.VMEM(tile_shape, jnp.bfloat16),
            pltpu.VMEM(tile_shape, jnp.bfloat16),
            pltpu.VMEM((2, tile_shape[2], size), jnp.bfloat16),
            pltpu.VMEM((2, tile_shape[2], size), jnp.bfloat16),
        ],
        compiler_params=pltpu.CompilerParams(vmem_limit_bytes=VMEM_BYTES),
        cost_estimate=pl.CostEstimate(
            flops=10 * work * size, bytes_accessed=4 * queries.size * 2, transcendentals=work
        ),
        name="gradients",
    )(*operands)
    return outs[: len(masks)], outs[len(masks) :]


def add_kernel(left, right, out):
    out[...] = (left[...].astype(jnp.float32) + right[...].astype(jnp.float32)).astype(out.dtype)


def add(left, right):
    return pl.pallas_call(
        add_kernel,
        out_shape=pltpu.VMEM(left.shape, left.dtype),
        in_specs=[_VMEM] * 2,
        out_specs=_VMEM,
        compiler_params=pltpu.CompilerParams(vmem_limit_bytes=VMEM_BYTES),
        name="add",
    )(left, right)


def finish_order(parts):
    return [1, *range(3, parts), "far", "odd", "even", 2, 0, "own"]


def finish_kernel(parts, *refs):
    *refs, dq_out, dk_out, dv_out, dk_buf, dv_buf, sems = refs
    refs = dict(zip(finish_order(parts), refs))
    heads = refs[0].shape[1]
    me = lax.axis_index("kvh")
    copies = []
    for mask in range(parts):
        first = pl.multiple_of((me ^ mask) * heads, heads)
        copies.append(
            pltpu.make_async_copy(refs[mask], dq_out.at[:, pl.ds(first, heads), :], sems.at[mask])
        )
        copies[-1].start()
    for number, (buf, ref) in enumerate(((dk_buf, dk_out), (dv_buf, dv_out))):
        sums = []
        for group in range(buf.shape[1]):
            total = refs["own"][number, group]
            for name in ("far", "even", "odd"):
                total = total + refs[name][number, group].astype(jnp.float32)
            sums.append(total)
        buf[...] = jnp.stack(sums, axis=1).astype(jnp.bfloat16)
        copies.append(pltpu.make_async_copy(buf, ref, sems.at[parts + number]))
        copies[-1].start()
    for copy in copies:
        copy.wait()


def finish(dqs, partials):
    parts = len(dqs)
    rows, heads, size = dqs[0].shape
    _, kv_heads, kv_rows, _ = partials[0].shape
    kv_shape = (kv_rows, kv_heads, size)
    kv_out = jax.ShapeDtypeStruct(kv_shape, jnp.bfloat16)
    operands = dict(enumerate(dqs)) | dict(zip(("own", "far", "even", "odd"), partials))
    return pl.pallas_call(
        functools.partial(finish_kernel, parts),
        out_shape=(
            jax.ShapeDtypeStruct((rows, heads * parts, size), jnp.bfloat16),
            kv_out,
            kv_out,
        ),
        in_specs=[_VMEM] * (parts + 4),
        out_specs=(_HBM,) * 3,
        scratch_shapes=[
            pltpu.VMEM(kv_shape, jnp.bfloat16),
            pltpu.VMEM(kv_shape, jnp.bfloat16),
            pltpu.SemaphoreType.DMA((parts + 2,)),
        ],
        compiler_params=pltpu.CompilerParams(vmem_limit_bytes=VMEM_BYTES),
        name="finish",
    )(*[operands[name] for name in finish_order(parts)])


def shifted(block, distance):
    count = lax.axis_size("seq")
    return lax.ppermute(block, "seq", [(i, (i + distance) % count) for i in range(count)])


def paired(block):
    return lax.ppermute(block, "seq", [(i, i ^ 1) for i in range(lax.axis_size("seq"))])


def ringed(block, direction=1):
    count = lax.axis_size("seq")
    route = []
    for i in range(count):
        target = i + 2 if i % 2 == 0 else i - 2
        route.append((i, min(max(target, 0), count - 1))[::direction])
    return lax.ppermute(block, "seq", route)


def swapped(block, mask):
    return lax.ppermute(block, "kvh", [(i, i ^ mask) for i in range(lax.axis_size("kvh"))])


def local(queries, keys, values, output_gradient, doc_lengths, prefix_lengths):
    parts = lax.axis_size("kvh")
    kv, cots, ranges = prepare(
        doc_lengths, prefix_lengths, output_gradient, keys, values, parts
    )
    even = paired(kv[2])
    blocks = [kv[0], shifted(kv[1], BACK), even, ringed(even)]
    cots = [cots[0]] + [swapped(cots[mask], mask) for mask in range(1, parts)]
    dqs, carried = {}, None
    for masks in stages(parts):
        found, carried = gradients(
            masks, parts, ranges, queries, [cots[mask] for mask in masks], blocks, carried
        )
        for mask, dq in zip(masks, found):
            dqs[mask] = swapped(dq, mask) if mask else dq
    own, far_even, far_odd, even, odd = carried
    relayed = add(paired(odd), far_odd)
    partials = [own, ringed(far_even, -1), paired(even), ringed(relayed)]
    return finish([dqs[mask] for mask in range(parts)], partials)


def solution(mesh):
    in_specs = (
        P("seq", "kvh", None),
        P("seq", "kvh", None),
        P("seq", "kvh", None),
        P(("seq", "kvh"), None, None),
        P(),
        P(),
    )
    out_specs = (P(("seq", "kvh"), None, None), P("seq", "kvh", None), P("seq", "kvh", None))
    return jax.shard_map(local, mesh=mesh, in_specs=in_specs, out_specs=out_specs, check_vma=False)
```
